128 devices in a mesh: gy: 16 (over y, x), gz: 8 (over z, core).
Axes of the slice: x: 4, y: 4, z: 4, core: 2. Of those that a mesh axis runs over, the one named last changes fastest.
Arguments:
- phase: bfloat16 [16, 512, 1024], P(None, 'gy', 'gz'), may hold values from 0 to 1
- undercool: bfloat16 [16, 512, 1024], P(None, 'gy', 'gz'), may hold values from -4 to 4
- perm_base: bfloat16 [16, 512, 1024], P(None, 'gy', 'gz'), may hold values from 0.5 to 10
- source: float32 [16, 512, 1024], P(None, 'gy', 'gz'), may hold values from -6 to 6
- pressure: float32 [16, 512, 1024], P(None, 'gy', 'gz'), may hold values from -6 to 6
Outputs:
- phase_next: bfloat16 [16, 512, 1024], P(None, 'gy', 'gz')
- pressure_next: float32 [16, 512, 1024], P(None, 'gy', 'gz')
- residual: float32 [16, 512, 1024], P(None, 'gy', 'gz')
The draws below stay inside these ranges and needn't reach their ends.
All inputs are finite; a program needn't handle non-finite values.
Results may differ from the reference program's by a relative error of at most 0.0004.
Values may be sent and summed in bfloat16 or wider, within the bound.
A program may use at most 128 MiB of HBM per device.

```python
import math
import jax
import jax.numpy as jnp
from jax import lax

LEVELS = 5
PRE = 2
POST = 2
COARSE_SWEEPS = 20
NX = 16
NY = 512
NZ = 1024


def draw_source(key, part):
    extent = (NX, NY, NZ)
    return jnp.clip(jax.random.normal(key, extent, jnp.float32), -6.0, 6.0)


def block_scale(own_key, shape, pieces, low, high):
    def one(position, shards_of):
        steps = jax.random.uniform(jax.random.fold_in(jax.random.fold_in(own_key, 6), position), (shards_of,), jnp.float32, low / len(pieces), high / len(pieces))
        return jnp.repeat(jnp.exp(steps), shape[position] // shards_of).reshape((-1,) + (1,) * (len(shape) - position - 1))

    gain = one(*pieces[0])
    for cut in pieces[1:]:
        gain = gain * one(*cut)
    return gain


def noise(stream_key, shape, deviation, limit, shards=(), kind=jnp.bfloat16):
    result = jax.random.normal(stream_key, shape, jnp.float32) * deviation
    if len(shards) > 0:
        result = block_scale(stream_key, shape, shards, -0.22, 0.18) * result
    return jnp.clip(result, min=-limit, max=limit).astype(kind)


def setup_inputs(seed: int = 0) -> dict:
    key_list = jax.random.split(jax.random.key(seed), 6)
    phase = jnp.clip(1.0 * jax.random.uniform(key_list[0], (NX, NY, NZ), jnp.float32) ** block_scale(key_list[0], (NX, NY, NZ), ((1, 16), (2, 8)), -0.2, 0.2), 0.0, 1.0).astype(jnp.bfloat16)
    undercool = noise(key_list[1], (NX, NY, NZ), 1.0, 4.0, ((1, 16), (2, 8)))
    perm_base = jnp.clip(jnp.exp(math.log(10.0) - 2.9957323 * jax.random.uniform(key_list[2], (NX, NY, NZ), jnp.float32) ** block_scale(key_list[2], (NX, NY, NZ), ((1, 16), (2, 8)), -0.2, 0.2)), 0.5, 10.0).astype(jnp.bfloat16)
    source = draw_source(jax.random.fold_in(key_list[5], 71), 0)
    pressure = noise(key_list[4], (NX, NY, NZ), 1.0, 6.0, ((1, 16), (2, 8)), jnp.float32)
    return {"phase": phase, "undercool": undercool, "perm_base": perm_base, "source": source, "pressure": pressure}


def shifted(padded):
    return (padded[2:, 1:-1, 1:-1], padded[:-2, 1:-1, 1:-1], padded[1:-1, 2:, 1:-1],
            padded[1:-1, :-2, 1:-1], padded[1:-1, 1:-1, 2:], padded[1:-1, 1:-1, :-2])


def restrict(array):
    n_one, n_two, n_three = array.shape
    blocks = array.reshape(n_one // 2, 2, n_two // 2, 2, n_three // 2, 2)
    return jnp.sum(blocks, axis=(1, 3, 5)) * 0.125


def prolong(array):
    return jnp.repeat(jnp.repeat(jnp.repeat(array, 2, 0), 2, 1), 2, 2)


def parity(extent):
    parity_sum = lax.broadcasted_iota(jnp.int32, extent, 0) + lax.broadcasted_iota(jnp.int32, extent, 1) + lax.broadcasted_iota(jnp.int32, extent, 2)
    return parity_sum % 2 == 0


def face_sums(padded_iterate, conduct, padded_conduct):
    flux_sum = jnp.zeros(conduct.shape, jnp.float32)
    diag_sum = jnp.zeros(conduct.shape, jnp.float32)
    for near_value, near_coef in zip(shifted(padded_iterate), shifted(padded_conduct)):
        face_coef = 0.5 * (conduct + near_coef)
        flux_sum = flux_sum + face_coef * near_value
        diag_sum = diag_sum + face_coef
    return flux_sum, diag_sum


def half_sweep(iterate, right, level_data, red_cells):
    conduct, padded_conduct, factor = level_data
    flux_sum, diag_sum = face_sums(jnp.pad(iterate, 1), conduct, padded_conduct)
    update = (right + factor * flux_sum) / (factor * diag_sum)
    return jnp.where(red_cells, update, iterate)


def red_black(iterate, right, level_data):
    red_cells = parity(iterate.shape)
    iterate = half_sweep(iterate, right, level_data, red_cells)
    return half_sweep(iterate, right, level_data, jnp.logical_not(red_cells))


def defect_of(iterate, right, level_data):
    conduct, padded_conduct, factor = level_data
    flux_sum, diag_sum = face_sums(jnp.pad(iterate, 1), conduct, padded_conduct)
    return right - factor * (diag_sum * iterate - flux_sum)


def cycle(depth, right, iterate, levels):
    level_data = levels[depth]
    if depth == LEVELS - 1:
        return lax.fori_loop(0, COARSE_SWEEPS, lambda number, guess: red_black(guess, right, level_data), iterate)
    for sweep in range(PRE):
        iterate = red_black(iterate, right, level_data)
    defect = restrict(defect_of(iterate, right, level_data))
    correction = cycle(depth + 1, defect, jnp.zeros_like(defect), levels)
    iterate = iterate + prolong(correction)
    for sweep in range(POST):
        iterate = red_black(iterate, right, level_data)
    return iterate


def reference(phase, undercool, perm_base, source, pressure):
    ice_now = phase.astype(jnp.float32)
    laplace = jnp.zeros_like(ice_now)
    for near_value in shifted(jnp.pad(ice_now, 1)):
        laplace = laplace + near_value
    laplace = laplace - 6.0 * ice_now
    well_term = 2.0 * ice_now * (1.0 - ice_now) * (1.0 - 2.0 * ice_now)
    drive_term = 30.0 * ice_now * ice_now * (1.0 - ice_now) * (1.0 - ice_now) * undercool.astype(jnp.float32)
    ice_new = jnp.clip(ice_now + 0.12 * laplace - 0.5 * well_term + 0.25 * drive_term, 0.0, 1.0)
    phase_next = ice_new.astype(jnp.bfloat16)
    conduct = perm_base.astype(jnp.float32) * jnp.exp(-1.5 * ice_new)
    levels = []
    for depth in range(LEVELS):
        if depth > 0:
            conduct = restrict(conduct)
        levels.append((conduct, jnp.pad(conduct, 1), 0.25 ** depth))
    pressure_next = cycle(0, source, pressure, levels)
    residual = defect_of(pressure_next, source, levels[0])
    return phase_next, pressure_next, residual
```

```python
import functools
import jax
import jax.numpy as jnp
from jax import lax
from jax.experimental import pallas as pl
from jax.experimental.pallas import tpu as pltpu
from jax.sharding import PartitionSpec as P

MESH = pl.DeviceIdType.MESH
F32 = jnp.float32
BF16 = jnp.bfloat16
COARSE_SWEEPS = 20
NX, NY, NZ = 16, 32, 128
HY = 8
R0 = NY + 2 * HY
R1 = 24
R2 = 14
NEAR = [(dy, dz) for dy in (-1, 0, 1) for dz in (-1, 0, 1) if (dy, dz) != (0, 0)]
X_IN, X_F, X_K, X_B1, X_V0, X_B2 = range(6)
N_X = 6


def roll(x, shift, axis):
    size = x.shape[axis]
    shift = shift % size
    return x if shift == 0 else pltpu.roll(x, shift, axis)


def loop(lo, hi, body, step=2):
    def trip(i, carry):
        for j in range(step):
            body(lo + i * step + j, j)
        return carry

    lax.fori_loop(0, (hi - lo) // step, trip, 0)


def kernel(
    GY, GZ, phase_h, under_h, perm_h, src_h, pres_h, phase_o, pres_o, res_o,
    inb, inf, tmp, pb, outb,
    ha, hf, zp, zpf, zb, zbf,
    ice, und, prm, S0, V0, K0, G0, BD0, D0, zv,
    KX, BX, CX, K1, V1, G1, I1, BD1, D1, K2, V2, G2, I2, BD2, D2,
    msg_k, msg_b, GK, GB, K3, G3, I3, D3, buf4, e3x, pair2,
    ssem, rsem, gs, gr, lsem, osem,
):
    gy, gz = lax.axis_index("gy"), lax.axis_index("gz")
    me = gy * GZ + gz

    def peer(dy, dz):
        return (lax.rem(gy + dy + GY, GY), lax.rem(gz + dz + GZ, GZ))

    barrier = pltpu.get_barrier_semaphore()

    def other(i):
        q = lax.rem(me + i, GY * GZ)
        return (q // GZ, lax.rem(q, GZ))

    def greet(i, carry):
        pl.semaphore_signal(barrier, inc=1, device_id=other(i), device_id_type=MESH)
        return carry

    lax.fori_loop(1, GY * GZ, greet, 0)

    loads = []
    for n, (src, dst) in enumerate(
        ((phase_h, inb.at[0]), (under_h, inb.at[1]), (perm_h, inb.at[2]), (src_h, inf.at[0]), (pres_h, inf.at[1]))
    ):
        copy = pltpu.make_async_copy(src, dst, lsem.at[n])
        copy.start()
        loads.append(copy)

    lane = lax.broadcasted_iota(jnp.int32, (8, 128), 1)
    sub = lax.broadcasted_iota(jnp.int32, (8, 128), 0)
    lane2 = lax.broadcasted_iota(jnp.int32, (8, 256), 1)
    sub2 = lax.broadcasted_iota(jnp.int32, (8, 256), 0)
    odd = lane % 2 == 1
    odd2 = lane2 % 2 == 1
    right_in, left_in = gz < GZ - 1, gz > 0
    up_in, down_in = gy > 0, gy < GY - 1
    ring_in = (lane2 < 128) | ((lane2 < 192) & right_in) | ((lane2 >= 192) & left_in)

    def cat(a, b):
        return jnp.concatenate([a, b], axis=-1)

    def ring(o, d):
        a, b = o[:, :128], o[:, 128:]
        fa, fb = roll(a, -d, 1), roll(b, -d, 1)
        ba, bb = roll(a, d, 1), roll(b, d, 1)
        end, start = lane >= 128 - d, lane < d
        ahead = cat(jnp.where(end, fb, fa), jnp.where(end, fa, fb))
        behind = cat(jnp.where(start, bb, ba), jnp.where(start, ba, bb))
        return ahead, behind

    for copy in loads:
        copy.wait()
    for n in range(3):
        for x in range(NX):
            tmp[n, pl.ds(x * NY, NY), :] = inb[n, x].astype(F32)
    for n in range(2):
        for x in range(NX):
            tmp[3 + n, pl.ds(x * NY, NY), :] = inf[n, x]

    def red_black_of(n, y, j):
        even = tmp[n, pl.ds(y, 8, stride=2 * NY), :]
        odds = tmp[n, pl.ds(NY + y, 8, stride=2 * NY), :]
        par = odd if j % 2 == 0 else jnp.logical_not(odd)
        return jnp.where(par, odds, even), jnp.where(par, even, odds)

    zp[...] = jnp.zeros_like(zp)
    zpf[...] = jnp.zeros_like(zpf)

    def prepare(k, carry):
        packed = jnp.zeros((48, 128), F32)
        packed_f = jnp.zeros((24, 128), F32)
        group = lax.broadcasted_iota(jnp.int32, (48, 128), 1) // 16
        for q in range(8):
            y = 8 * k + q
            parts = []
            for n in range(3):
                parts.extend(red_black_of(n, y, q))
            row = jnp.concatenate(parts, axis=0)
            ha[HY + y] = row.astype(BF16)
            s_r, s_b = red_black_of(3, y, q)
            _, v_b = red_black_of(4, y, q)
            row_f = jnp.concatenate([s_r, s_b, v_b], axis=0)
            hf[HY + y] = row_f
            packed = jnp.where(group == q, roll(row, 16 * q + 8, 1), packed)
            packed_f = jnp.where(group[:24] == q, roll(row_f, 16 * q + 8, 1), packed_f)
        zp[k] = packed.astype(BF16)
        zpf[k] = packed_f
        return carry

    lax.fori_loop(0, 4, prepare, 0)

    pl.semaphore_wait(barrier, GY * GZ - 1)

    def exchange(ex, pieces):
        copies = []
        for n, (dy, dz) in enumerate(NEAR):
            src, dst = pieces(dy, dz)
            copy = pltpu.make_async_remote_copy(
                src, dst, ssem.at[ex, n], rsem.at[ex, n], device_id=peer(dy, dz), device_id_type=MESH
            )
            copy.start()
            copies.append(copy)
        return copies

    def received(copies):
        for copy in copies:
            copy.wait_recv()

    def input_pieces(rows, packed, landing, width):
        def pieces(dy, dz):
            if dz == 0 and dy < 0:
                return rows.at[pl.ds(HY, width)], rows.at[pl.ds(HY + NY, width)]
            if dz == 0:
                return rows.at[pl.ds(HY + NY - width, width)], rows.at[pl.ds(HY - width, width)]
            side = 0 if dz > 0 else 1
            if dy == 0:
                return packed, landing.at[side, pl.ds(1, 4)]
            if dy > 0:
                return packed.at[pl.ds(3, 1)], landing.at[side, pl.ds(0, 1)]
            return packed.at[pl.ds(0, 1)], landing.at[side, pl.ds(5, 1)]

        return pieces

    x_in = exchange(X_IN, input_pieces(ha, zp, zb, 6))
    x_f = exchange(X_F, input_pieces(hf, zpf, zbf, 5))

    zero_row = jnp.zeros((8, 256), F32)
    e3x[...] = jnp.zeros_like(e3x)
    for c in range(2):
        for r in (0, R2 - 1):
            K2[c, r] = zero_row
            V2[c, r] = zero_row
        for r in (0, 1, R1 - 2, R1 - 1):
            V1[c, r] = zero_row
        for r in (3, R0 - 4):
            V0[c, r] = zero_row

    received(x_in)
    received(x_f)

    def row_mask(r, width):
        ok = ((r >= HY) | up_in) & ((r < HY + NY) | down_in)
        lanes = (lane2 < 128) | ((lane2 < 128 + width) & right_in) | ((lane2 >= 256 - width) & left_in)
        return lanes & ok

    def unpack(k, carry):
        group = lax.broadcasted_iota(jnp.int32, (48, 128), 1) % 16 < 8
        merged = jnp.where(group, zb[0, k].astype(F32), zb[1, k].astype(F32))
        merged_f = jnp.where(group[:24], zbf[0, k], zbf[1, k])
        for q in range(8):
            r = 8 * k + q
            ok = row_mask(r, 6) & (r >= 2) & (r < R0 - 2)
            ok5 = row_mask(r, 5) & (r >= 3) & (r < R0 - 3)
            side = roll(merged, 120 - 16 * q, 1)
            side_f = roll(merged_f, 120 - 16 * q, 1)
            a = ha[r].astype(F32)
            f = hf[r]
            for c in range(2):
                s = slice(8 * c, 8 * c + 8)
                ice[c, r] = jnp.where(ok, cat(a[s], side[s]), 0.0)
                s = slice(16 + 8 * c, 24 + 8 * c)
                und[c, r] = cat(a[s], side[s])
                s = slice(32 + 8 * c, 40 + 8 * c)
                prm[c, r] = jnp.where(ok5, cat(a[s], side[s]), 0.0)
                s = slice(8 * c, 8 * c + 8)
                S0[c, r] = cat(f[s], side_f[s])
            V0[1, r] = jnp.where(ok5, cat(f[16:24], side_f[16:24]), 0.0)
        return carry

    lax.fori_loop(0, 6, unpack, 0)

    def pick(c, j):
        return odd2 if (c + j) % 2 == 0 else jnp.logical_not(odd2)

    def x_outer(o, take):
        return jnp.where(take, roll(o, -1, 0), roll(o, 1, 0))

    def x_edge(take):
        return jnp.where(take, sub2, 7 - sub2) == 7

    def near0(ref, c, r, j):
        o = ref[1 - c, r]
        take = pick(c, j)
        ahead, behind = ring(o, 1)
        return (ref[1 - c, r - 1], ref[1 - c, r + 1], o, x_outer(o, take), ahead, behind)

    def permeability(r, j):
        for c in range(2):
            now = ice[c, r]
            near = list(near0(ice, c, r, j))
            near[3] = jnp.where(x_edge(pick(c, j)), 0.0, near[3])
            lap = near[0]
            for value in near[1:]:
                lap = lap + value
            lap = lap - 6.0 * now
            well = 2.0 * now * (1.0 - now) * (1.0 - 2.0 * now)
            drive = 30.0 * now * now * (1.0 - now) * (1.0 - now) * und[c, r]
            new = jnp.clip(now + 0.12 * lap - 0.5 * well + 0.25 * drive, 0.0, 1.0)
            K0[c, r] = jnp.where(prm[c, r] > 0.0, prm[c, r] * jnp.exp(-1.5 * new), 0.0)
            und[c, r] = new

    loop(2, R0 - 2, permeability)

    def swap_lanes(x, d):
        return jnp.where((lax.broadcasted_iota(jnp.int32, x.shape, 1) // d) % 2 == 0, roll(x, -d, 1), roll(x, d, 1))

    def swap_subs(x, d):
        return jnp.where((lax.broadcasted_iota(jnp.int32, x.shape, 0) // d) % 2 == 0, roll(x, -d, 0), roll(x, d, 0))

    def parity_y(level, ln, sb):
        return (sb // (1 if level == 1 else 2) + ln // (2 if level == 1 else 4)) % 2 == 1

    def own0(c, r):
        return K0[c, r, :, :128]

    def coarse0(y):
        r = HY + 2 * y
        t = (own0(0, r) + own0(1, r)) + (own0(0, r + 1) + own0(1, r + 1))
        return 0.125 * (t + swap_lanes(t, 1))

    p1, p2 = parity_y(1, lane, sub), parity_y(2, lane, sub)

    def split(p, low, high):
        return jnp.where(p, high, low), jnp.where(p, low, high)

    k2_rows = []
    for yp in range(8):
        red, black = split(p1, coarse0(2 * yp), coarse0(2 * yp + 1))
        KX[1, 1, yp] = jnp.where(odd, black, red)
        t = red + black
        t = t + swap_subs(t, 1)
        k2_rows.append(0.125 * (t + swap_lanes(t, 2)))
    k3_rows = []
    for yp in range(4):
        red, black = split(p2, k2_rows[2 * yp], k2_rows[2 * yp + 1])
        KX[1, 1, 8 + yp] = jnp.where(odd, black, red)
        t = red + black
        t = t + swap_subs(t, 2)
        k3_rows.append(0.125 * (t + swap_lanes(t, 4)))

    def block_pieces(ref):
        return lambda dy, dz: (ref.at[1, 1], ref.at[1 - dy, 1 - dz])

    x_k = exchange(X_K, block_pieces(KX))

    squeeze = (
        lax.broadcasted_iota(jnp.int32, (128, 128), 0) == 8 * (lax.broadcasted_iota(jnp.int32, (128, 128), 1) % 16)
    ).astype(F32)

    def dot(a, b):
        return lax.dot_general(
            a, b, (((1,), (0,)), ((), ())), precision=lax.Precision.HIGHEST, preferred_element_type=F32
        )

    def message(rows):
        piece = jnp.zeros((8, 128), F32)
        for y in range(4):
            u = rows[y]
            t = jnp.where((y + lane // 8) % 2 == 0, u, roll(u, 4, 0))
            piece = jnp.where(sub % 4 == y, t, piece)
        wide = dot(piece, squeeze)
        return jnp.sum(jnp.where(lane // 16 == sub, wide, 0.0), axis=0, keepdims=True)

    def gather(msg, landing, n, row):
        msg[0] = row
        landing[pl.ds(me, 1)] = row.reshape(1, 1, 128)

        def send(i, carry):
            pltpu.make_async_remote_copy(
                msg, landing.at[pl.ds(me, 1)], gs.at[n], gr.at[n], device_id=other(i), device_id_type=MESH
            ).start()
            return carry

        lax.fori_loop(1, GY * GZ, send, 0)

    def all_bytes(landing, sem):
        part = landing.at[pl.ds(0, GY * GZ - 1)]
        pltpu.make_async_copy(part, part, sem).wait()

    def global_level3(landing):
        x = landing[...].reshape(GY, GZ, 128)
        ln = lax.broadcasted_iota(jnp.int32, x.shape, 2)
        sb = lax.broadcasted_iota(jnp.int32, x.shape, 1)
        for bit in (1, 2, 4):
            s_set, t_set = (sb // bit) % 2 == 1, (ln // (16 * bit)) % 2 == 1
            down = roll(roll(x, bit, 1), -16 * bit, 2)
            up = roll(roll(x, -bit, 1), 16 * bit, 2)
            x = jnp.where(s_set == t_set, x, jnp.where(s_set, down, up))
        pairs = x.reshape(GY // 2, 2, 8, 128)
        even, odds = pairs[:, 0], pairs[:, 1]
        low = lax.broadcasted_iota(jnp.int32, even.shape, 1) < 4
        red = jnp.where(low, even, roll(odds, 4, 1))
        black = jnp.where(low, roll(even, 4, 1), odds)
        return red.reshape(64, 128), black.reshape(64, 128)

    gather(msg_k, GK, 0, message(k3_rows))

    def faces0(r, j):
        ok = row_mask(r, 5)
        for c in range(2):
            k = K0[c, r]
            take = pick(c, j)
            edge = x_edge(take)
            near = list(near0(K0, c, r, j))
            near[3] = jnp.where(edge, 0.0, near[3])
            f = [0.5 * (k + value) for value in near]
            d = ((f[0] + f[1]) + (f[2] + f[3])) + (f[4] + f[5])
            inv = jnp.where(ok, 1.0 / d, 0.0)
            for n in range(6):
                g = f[n] * inv
                G0[c, r, n] = jnp.where(edge, 0.0, g) if n == 3 else g
            BD0[c, r] = jnp.where(ok, S0[c, r], 0.0) * inv
            D0[c, r] = d

    loop(4, R0 - 4, faces0)

    def update0(c, r, j):
        near = near0(V0, c, r, j)
        t = [G0[c, r, n] * near[n] for n in range(6)]
        return BD0[c, r] + (((t[0] + t[1]) + (t[2] + t[3])) + (t[4] + t[5]))

    def sweep0(c, lo, hi):
        def body(r, j):
            V0[c, r] = update0(c, r, j)

        loop(lo, hi, body)

    sweep0(0, 4, R0 - 4)
    sweep0(1, 4, R0 - 4)
    sweep0(0, 6, R0 - 6)
    sweep0(1, 6, R0 - 6)

    def defect0(r, j):
        return (D0[0, r] * (update0(0, r, j) - V0[0, r]))[:, :128]

    def right1(yp, carry):
        rows = []
        for j in range(2):
            r = HY + 4 * yp + 2 * j
            t = defect0(r, 0) + defect0(r + 1, 1)
            rows.append(0.125 * (t + swap_lanes(t, 1)))
        red, black = split(p1, rows[0], rows[1])
        BX[1, 1, yp] = jnp.where(odd, black, red)
        return carry

    lax.fori_loop(0, 8, right1, 0)
    x_b1 = exchange(X_B1, block_pieces(BX))

    received(x_k)

    def joined(ref, yb, r):
        a = ref[yb, 1, r]
        b = jnp.where(lane < 64, ref[yb, 2, r], ref[yb, 0, r])
        return cat(a, b)

    def apart(x):
        a, b = x[:, :128], x[:, 128:]
        red = cat(jnp.where(odd, roll(a, 1, 1), a), jnp.where(odd, roll(b, 1, 1), b))
        black = cat(jnp.where(odd, a, roll(a, -1, 1)), jnp.where(odd, b, roll(b, -1, 1)))
        return red, black

    for yb in range(3):
        row_ok = (up_in, True, down_in)[yb]
        ok = ring_in & row_ok

        def spread1(r, carry, yb=yb, ok=ok):
            red, black = apart(joined(KX, yb, r))
            K1[0, 8 * yb + r] = jnp.where(ok, red, 0.0)
            K1[1, 8 * yb + r] = jnp.where(ok, black, 0.0)
            return carry

        lax.fori_loop(0, 8, spread1, 0)
        for r in range(4):
            red, black = apart(joined(KX, yb, 8 + r))
            K2[0, 1 + 4 * yb + r] = jnp.where(ok, red, 0.0)
            K2[1, 1 + 4 * yb + r] = jnp.where(ok, black, 0.0)

    def near_y(level, ref, c, r):
        dx, dz = (1, 2) if level == 1 else (2, 4)
        p = parity_y(level, lane2, sub2)
        o, low, high = ref[1 - c, r], ref[1 - c, r - 1], ref[1 - c, r + 1]
        outer = jnp.where(p, high, low) if c == 0 else jnp.where(p, low, high)
        ahead, behind = ring(o, dz)
        return (o, outer, roll(o, -dx, 0), roll(o, dx, 0), ahead, behind)

    def faces_y(level, K, G, I, D, r):
        dx = 1 if level == 1 else 2
        s = 0.25**level
        for c in range(2):
            k = K[c, r]
            near = list(near_y(level, K, c, r))
            last, first = sub2 >= 8 - dx, sub2 < dx
            near[2] = jnp.where(last, 0.0, near[2])
            near[3] = jnp.where(first, 0.0, near[3])
            f = [0.5 * (k + value) for value in near]
            d = ((f[0] + f[1]) + (f[2] + f[3])) + (f[4] + f[5])
            inv = jnp.where(k > 0.0, 1.0 / d, 0.0)
            for n in range(6):
                g = f[n] * inv
                if n == 2:
                    g = jnp.where(last, 0.0, g)
                if n == 3:
                    g = jnp.where(first, 0.0, g)
                G[c, r, n] = g
            I[c, r] = inv * (1.0 / s)
            if c == 0:
                D[r] = s * d

    loop(2, R1 - 2, lambda r, j: faces_y(1, K1, G1, I1, D1, r))
    loop(1, R2 - 1, lambda r, j: faces_y(2, K2, G2, I2, D2, r))

    all_bytes(GK, gr.at[0])
    k3r, k3b = global_level3(GK)
    row3 = lax.broadcasted_iota(jnp.int32, (64, 128), 0)
    lane3 = lax.broadcasted_iota(jnp.int32, (64, 128), 1)
    odd3 = (row3 + lane3) % 2 == 1
    edges3 = (row3 == 0, row3 == 63, lane3 == 0, lane3 == 127)

    def near3(o):
        return (roll(o, 1, 0), roll(o, -1, 0), roll(o, 1, 1), roll(o, -1, 1), o)

    def faces3(c, k, o):
        s = 0.25**3
        near = [jnp.where(e, 0.0, v) for e, v in zip(edges3, near3(o))] + [o]
        f = [0.5 * (k + value) for value in near] + [0.5 * k]
        d = ((f[0] + f[1]) + (f[2] + f[3])) + (f[4] + f[5])
        inv = 1.0 / d
        for n in range(5):
            g = f[n] * inv
            G3[c, n] = jnp.where(edges3[n], 0.0, g) if n < 4 else g
        I3[c] = inv * (1.0 / s)
        if c == 0:
            D3[...] = s * d

    faces3(0, k3r, k3b)
    faces3(1, k3b, k3r)

    lane4 = lax.broadcasted_iota(jnp.int32, (16, 128), 1)
    row4 = lax.broadcasted_iota(jnp.int32, (16, 128), 0)
    p4 = (lane4 // 2) % 2 == 1

    def level4_of(total):
        t = total + swap_subs(total, 1)
        buf4[...] = 0.125 * (t + swap_lanes(t, 1))
        low, high = buf4[pl.ds(0, 16, stride=4), :], buf4[pl.ds(2, 16, stride=4), :]
        return split(p4, low, high)

    k4 = level4_of(k3r + k3b)

    def near4(c, o):
        low, high = roll(o, 1, 0), roll(o, -1, 0)
        outer = jnp.where(p4, high, low) if c == 0 else jnp.where(p4, low, high)
        return (o, outer, roll(o, -2, 1), roll(o, 2, 1))

    def faces4(c):
        s = 0.25**4
        k = k4[c]
        take = p4 if c == 0 else jnp.logical_not(p4)
        edges = (None, jnp.where(take, row4, 15 - row4) == 15, lane4 >= 126, lane4 < 2)
        near = near4(c, k4[1 - c])
        near = [v if e is None else jnp.where(e, 0.0, v) for e, v in zip(edges, near)]
        f = [0.5 * (k + value) for value in near]
        d = ((f[0] + f[1]) + (f[2] + f[3])) + k
        inv = 1.0 / d
        g = [v * inv if e is None else jnp.where(e, 0.0, v * inv) for e, v in zip(edges, f)]
        return g, inv * (1.0 / s)

    g4r, i4r = faces4(0)
    g4b, i4b = faces4(1)

    received(x_b1)

    def v0_pieces(dy, dz):
        def at(r, n):
            return V0.at[1, pl.ds(r, n), :, pl.ds(0, 128)]

        lo, n, to = {-1: (HY, 5, HY + NY), 0: (HY, NY, HY), 1: (HY + NY - 5, 5, HY - 5)}[dy]
        if dz == 0:
            return at(lo, n), at(to, n)
        return at(lo, n), zv.at[0 if dz > 0 else 1, pl.ds(to, n)]

    x_v0 = exchange(X_V0, v0_pieces)

    for yb in range(3):

        def spread_b(r, carry, yb=yb):
            red, black = apart(joined(BX, yb, r))
            row = 8 * yb + r
            BD1[0, row] = red * I1[0, row]
            BD1[1, row] = black * I1[1, row]
            V1[0, row] = red * I1[0, row]
            return carry

        lo, hi = ((2, 8), (0, 8), (0, 6))[yb]
        lax.fori_loop(lo, hi, spread_b, 0)

    def update_y(level, V, G, BD, c, r):
        near = near_y(level, V, c, r)
        t = [G[c, r, n] * near[n] for n in range(6)]
        return BD[c, r] + (((t[0] + t[1]) + (t[2] + t[3])) + (t[4] + t[5]))

    def sweep_y(level, V, G, BD, c, lo, hi):
        def body(r, j):
            V[c, r] = update_y(level, V, G, BD, c, r)

        loop(lo, hi, body)

    sweep_y(1, V1, G1, BD1, 1, 2, 22)
    sweep_y(1, V1, G1, BD1, 0, 2, 22)
    sweep_y(1, V1, G1, BD1, 1, 2, 22)

    p2w = parity_y(2, lane2, sub2)

    def right2(i, carry):
        rows = []
        for j in range(2):
            r = 4 + 2 * i + j
            t = D1[r] * (update_y(1, V1, G1, BD1, 0, r) - V1[0, r])
            t = t + swap_subs(t, 1)
            a, b = t[:, :128], t[:, 128:]
            rows.append(0.125 * cat(a + swap_lanes(a, 2), b + swap_lanes(b, 2)))
        red, black = split(p2w, rows[0], rows[1])
        row = 3 + i
        BD2[0, row] = red * I2[0, row]
        BD2[1, row] = black * I2[1, row]
        V2[0, row] = red * I2[0, row]
        pair2[i] = jnp.where(odd, black[:, :128], red[:, :128])
        return carry

    V2[0, 2] = zero_row
    V2[0, 11] = zero_row
    V2[1, 2] = zero_row
    V2[1, 11] = zero_row
    lax.fori_loop(0, 8, right2, 0)

    sweep_y(2, V2, G2, BD2, 1, 3, 11)
    sweep_y(2, V2, G2, BD2, 0, 3, 11)
    sweep_y(2, V2, G2, BD2, 1, 3, 11)
    rows = []
    for y in range(4):
        r = 5 + y
        t = (D2[r] * (update_y(2, V2, G2, BD2, 0, r) - V2[0, r]))[:, :128]
        t = t + swap_subs(t, 2)
        rows.append(0.125 * (t + swap_lanes(t, 4)))
    gather(msg_b, GB, 1, message(rows))

    for y in range(4):
        CX[1, 1, y] = jnp.where(lane % 4 < 2, pair2[2 + y], V2[1, 5 + y, :, :128])
    x_b2 = exchange(X_B2, block_pieces(CX))
    received(x_v0)
    for copy in x_v0:
        copy.wait_send()

    def v0_sides(r, j):
        ok = ((r >= HY) | up_in) & ((r < HY + NY) | down_in)
        V0[1, r, :, 128:] = jnp.where(
            ok & (((lane < 5) & right_in) | ((lane >= 123) & left_in)), jnp.where(lane < 64, zv[1, r], zv[0, r]), 0.0
        )
        V0[1, r, :, :128] = jnp.where(ok, V0[1, r, :, :128], 0.0)

    loop(HY - 5, HY + NY + 5, v0_sides)
    received(x_b2)
    for yb in range(3):
        row_ok = (up_in, True, down_in)[yb]
        for r in range(4):
            x = joined(CX, yb, r)
            row = 1 + 4 * yb + r

            def fill(x):
                a, b = x[:, :128], x[:, 128:]
                first = cat(jnp.where(odd, roll(a, 1, 1), a), jnp.where(odd, roll(b, 1, 1), b))
                second = cat(jnp.where(odd, a, roll(a, -1, 1)), jnp.where(odd, b, roll(b, -1, 1)))
                return first, second

            first, second = fill(x)
            head = lane2 % 4 < 2

            def pair_up(y):
                return cat(roll(y[:, :128], 2, 1), roll(y[:, 128:], 2, 1))

            def pair_down(y):
                return cat(roll(y[:, :128], -2, 1), roll(y[:, 128:], -2, 1))

            BD2[0, row] = jnp.where(head, first, pair_up(first)) * I2[0, row]
            BD2[1, row] = jnp.where(head, second, pair_up(second)) * I2[1, row]
            V2[1, row] = jnp.where(ring_in & row_ok, jnp.where(head, pair_down(x), x), 0.0)

    zrow = lax.broadcasted_iota(jnp.int32, (128, 256), 0)
    zcol = lax.broadcasted_iota(jnp.int32, (128, 256), 1)
    expand = (zrow == gz * 16 + zcol // 8 - jnp.where(zcol >= 192, 32, 0)).astype(F32)

    all_bytes(GB, gr.at[1])
    b3r, b3b = global_level3(GB)
    bd3 = (b3r * I3[0], b3b * I3[1])

    def update3(c, o):
        near = near3(o)
        t = [G3[c, n] * near[n] for n in range(5)]
        return bd3[c] + (((t[0] + t[1]) + (t[2] + t[3])) + t[4])

    v_r = bd3[0]
    v_b = update3(1, v_r)
    v_r = update3(0, v_b)
    v_b = update3(1, v_r)
    r3 = D3[...] * (update3(0, v_b) - v_r)
    b4 = level4_of(r3)
    bd4r, bd4b = b4[0] * i4r, b4[1] * i4b

    def update4(c, g, bd, o):
        near = near4(c, o)
        return bd + ((g[0] * near[0] + g[1] * near[1]) + (g[2] * near[2] + g[3] * near[3]))

    def sweep4(i, carry):
        red, black = carry
        red = update4(0, g4r, bd4r, black)
        black = update4(1, g4b, bd4b, red)
        return red, black

    zero4 = jnp.zeros((16, 128), F32)
    e_r, e_b = lax.fori_loop(0, COARSE_SWEEPS, sweep4, (zero4, zero4))
    low, high = split(p4, e_r, e_b)
    buf4[pl.ds(0, 16, stride=4), :] = low
    buf4[pl.ds(1, 16, stride=4), :] = low
    buf4[pl.ds(2, 16, stride=4), :] = high
    buf4[pl.ds(3, 16, stride=4), :] = high
    v_b = v_b + buf4[...]
    v_r = update3(0, v_b)
    v_b = update3(1, v_r)
    v_r = update3(0, v_b)
    v_b = update3(1, v_r)

    x_low, x_high = split(odd3, v_r, v_b)
    e3x[0, pl.ds(8, 64), :] = x_low
    e3x[1, pl.ds(8, 64), :] = x_high
    parts = []
    for n in range(2):
        for i in range(12):
            parts.append(e3x[n, pl.ds(gy * 4 + (4 + i), 1), :])
    wide = dot(jnp.concatenate(parts, axis=0), expand)
    for i in range(12):
        e = jnp.where(sub2 < 4, wide[i : i + 1], wide[12 + i : 13 + i])
        row_ok = up_in if i < 4 else (down_in if i >= 8 else True)
        V2[1, 1 + i] = V2[1, 1 + i] + jnp.where(ring_in & row_ok, e, 0.0)
    sweep_y(2, V2, G2, BD2, 0, 1, 13)
    sweep_y(2, V2, G2, BD2, 1, 1, 13)
    sweep_y(2, V2, G2, BD2, 0, 1, 13)
    sweep_y(2, V2, G2, BD2, 1, 3, 11)

    p1w = parity_y(1, lane2, sub2)

    def correct1(i, carry):
        low, high = split(p2w, V2[0, 3 + i], V2[1, 3 + i])
        V1[1, 4 + 2 * i] = V1[1, 4 + 2 * i] + low
        V1[1, 5 + 2 * i] = V1[1, 5 + 2 * i] + high
        return carry

    lax.fori_loop(0, 8, correct1, 0)
    sweep_y(1, V1, G1, BD1, 0, 4, 20)
    sweep_y(1, V1, G1, BD1, 1, 4, 20)
    sweep_y(1, V1, G1, BD1, 0, 4, 20)
    sweep_y(1, V1, G1, BD1, 1, 6, 18)

    def correct0(i, carry):
        low, high = split(p1w, V1[0, 6 + i], V1[1, 6 + i])
        for j in range(2):
            V0[1, 4 * i + j] = V0[1, 4 * i + j] + low
            V0[1, 4 * i + 2 + j] = V0[1, 4 * i + 2 + j] + high
        return carry

    lax.fori_loop(0, 12, correct0, 0)
    sweep0(0, 4, R0 - 4)
    sweep0(1, 4, R0 - 4)
    sweep0(0, 6, R0 - 6)
    sweep0(1, 6, R0 - 6)

    def results(r, j):
        y = r - HY
        par = odd if j % 2 == 0 else jnp.logical_not(odd)

        def put(n, red, black):
            tmp[n, pl.ds(y, 8, stride=2 * NY), :] = jnp.where(par, black, red)
            tmp[n, pl.ds(NY + y, 8, stride=2 * NY), :] = jnp.where(par, red, black)

        v_red, v_black = V0[0, r], V0[1, r]
        put(0, v_red[:, :128], v_black[:, :128])
        res_red = D0[0, r] * (update0(0, r, j) - v_red)
        res_black = D0[1, r] * (update0(1, r, j) - v_black)
        put(1, res_red[:, :128], res_black[:, :128])
        put(2, und[0, r, :, :128], und[1, r, :, :128])

    loop(HY, HY + NY, results)
    for x in range(NX):
        outb[x] = tmp[2, pl.ds(x * NY, NY), :].astype(BF16)
        pb[0, x] = tmp[0, pl.ds(x * NY, NY), :]
        pb[1, x] = tmp[1, pl.ds(x * NY, NY), :]
    stores = []
    for n, (src, dst) in enumerate(((outb, phase_o), (pb.at[0], pres_o), (pb.at[1], res_o))):
        copy = pltpu.make_async_copy(src, dst, osem.at[n])
        copy.start()
        stores.append(copy)

    for copies in (x_in, x_f, x_k, x_b1, x_b2):
        for copy in copies:
            copy.wait_send()
    all_bytes(GK, gs.at[0])
    all_bytes(GB, gs.at[1])
    for copy in stores:
        copy.wait()


def per_device(GY, GZ, phase, undercool, perm_base, source, pressure):
    def vm(*shape):
        return pltpu.VMEM(shape, F32)

    scratch = [
        pltpu.VMEM((3, NX, NY, NZ), BF16),
        vm(2, NX, NY, NZ),
        vm(5, NX * NY, NZ),
        vm(2, NX, NY, NZ),
        pltpu.VMEM((NX, NY, NZ), BF16),
        pltpu.VMEM((R0, 48, 128), BF16),
        vm(R0, 24, 128),
        pltpu.VMEM((4, 48, 128), BF16),
        vm(4, 24, 128),
        pltpu.VMEM((2, 6, 48, 128), BF16),
        vm(2, 6, 24, 128),
        vm(2, R0, 8, 256),
        vm(2, R0, 8, 256),
        vm(2, R0, 8, 256),
        vm(2, R0, 8, 256),
        vm(2, R0, 8, 256),
        vm(2, R0, 8, 256),
        vm(2, R0, 6, 8, 256),
        vm(2, R0, 8, 256),
        vm(2, R0, 8, 256),
        vm(2, R0, 8, 128),
        vm(3, 3, 12, 8, 128),
        vm(3, 3, 8, 8, 128),
        vm(3, 3, 4, 8, 128),
        vm(2, R1, 8, 256),
        vm(2, R1, 8, 256),
        vm(2, R1, 6, 8, 256),
        vm(2, R1, 8, 256),
        vm(2, R1, 8, 256),
        vm(R1, 8, 256),
        vm(2, R2, 8, 256),
        vm(2, R2, 8, 256),
        vm(2, R2, 6, 8, 256),
        vm(2, R2, 8, 256),
        vm(2, R2, 8, 256),
        vm(R2, 8, 256),
        vm(1, 1, 128),
        vm(1, 1, 128),
        vm(GY * GZ, 1, 128),
        vm(GY * GZ, 1, 128),
        vm(2, 64, 128),
        vm(2, 5, 64, 128),
        vm(2, 64, 128),
        vm(64, 128),
        vm(64, 128),
        vm(2, 80, 128),
        vm(8, 8, 128),
        pltpu.SemaphoreType.DMA((N_X, 8)),
        pltpu.SemaphoreType.DMA((N_X, 8)),
        pltpu.SemaphoreType.DMA((2,)),
        pltpu.SemaphoreType.DMA((2,)),
        pltpu.SemaphoreType.DMA((5,)),
        pltpu.SemaphoreType.DMA((3,)),
    ]
    hbm = pl.BlockSpec(memory_space=pl.ANY)
    return pl.pallas_call(
        functools.partial(kernel, GY, GZ),
        out_shape=(
            jax.ShapeDtypeStruct((NX, NY, NZ), BF16),
            jax.ShapeDtypeStruct((NX, NY, NZ), F32),
            jax.ShapeDtypeStruct((NX, NY, NZ), F32),
        ),
        in_specs=[hbm] * 5,
        out_specs=(hbm, hbm, hbm),
        scratch_shapes=scratch,
        compiler_params=pltpu.CompilerParams(
            collective_id=0, has_side_effects=True, vmem_limit_bytes=48 * 2**20
        ),
    )(phase, undercool, perm_base, source, pressure)


def solution(mesh):
    spec = P(None, "gy", "gz")
    return jax.shard_map(
        functools.partial(per_device, mesh.shape["gy"], mesh.shape["gz"]),
        mesh=mesh,
        in_specs=(spec,) * 5,
        out_specs=(spec,) * 3,
        check_vma=False,
    )
```

```python
import functools
import jax
import jax.numpy as jnp
from jax import lax
from jax.experimental import pallas as pl
from jax.experimental.pallas import tpu as pltpu
from jax.sharding import PartitionSpec as P

MESH = pl.DeviceIdType.MESH
F32 = jnp.float32
BF16 = jnp.bfloat16
COARSE_SWEEPS = 20
NX, NY, NZ = 16, 32, 128
HY = 8
R0 = NY + 2 * HY
R1 = 24
R2 = 14
NEAR = [(dy, dz) for dy in (-1, 0, 1) for dz in (-1, 0, 1) if (dy, dz) != (0, 0)]
X_IN, X_F, X_K, X_B1, X_V0, X_B2 = range(6)
N_X = 6


def roll(x, shift, axis):
    size = x.shape[axis]
    shift = shift % size
    return x if shift == 0 else pltpu.roll(x, shift, axis)


def loop(lo, hi, body, step=2):
    def trip(i, carry):
        stores = []
        for j in range(step):
            stores.extend(body(lo + i * step + j, j))
        for ref, index, value in stores:
            ref[index] = value
        return carry

    trips = (hi - lo) // step
    assert trips * step == hi - lo
    if trips == 1:
        trip(0, 0)
    else:
        lax.fori_loop(0, trips, trip, 0)


def kernel(
    GY, GZ, phase_h, under_h, perm_h, src_h, pres_h, phase_o, pres_o, res_o,
    inb, inf, tmp, pb, outb,
    ha, hf, zp, zpf, zb, zbf,
    ice, und, prm, S0, V0, K0, G0, BD0, D0, zv,
    KX, CX, K1, V1, G1, I1, BD1, D1, K2, V2, G2, I2, BD2, D2,
    b1, zp1, zb1, msg_k, msg_b, GK, GB, K3, G3, I3, D3, buf4, e3x, pair2,
    ssem, rsem, gs, gr, lsem, osem,
):
    gy, gz = lax.axis_index("gy"), lax.axis_index("gz")
    me = gy * GZ + gz

    def peer(dy, dz):
        return (lax.rem(gy + dy + GY, GY), lax.rem(gz + dz + GZ, GZ))

    barrier = pltpu.get_barrier_semaphore()

    def other(i):
        q = lax.rem(me + i, GY * GZ)
        return (q // GZ, lax.rem(q, GZ))

    def greet(i, carry):
        pl.semaphore_signal(barrier, inc=1, device_id=other(i), device_id_type=MESH)
        return carry

    lax.fori_loop(1, GY * GZ, greet, 0)

    loads = []
    for n, (src, dst) in enumerate(
        ((phase_h, inb.at[0]), (under_h, inb.at[1]), (perm_h, inb.at[2]), (src_h, inf.at[0]), (pres_h, inf.at[1]))
    ):
        copy = pltpu.make_async_copy(src, dst, lsem.at[n])
        copy.start()
        loads.append(copy)

    lane = lax.broadcasted_iota(jnp.int32, (8, 128), 1)
    sub = lax.broadcasted_iota(jnp.int32, (8, 128), 0)
    lane2 = lax.broadcasted_iota(jnp.int32, (8, 256), 1)
    sub2 = lax.broadcasted_iota(jnp.int32, (8, 256), 0)
    odd = lane % 2 == 1
    odd2 = lane2 % 2 == 1
    right_in, left_in = gz < GZ - 1, gz > 0
    up_in, down_in = gy > 0, gy < GY - 1
    ring_in = (lane2 < 128) | ((lane2 < 192) & right_in) | ((lane2 >= 192) & left_in)

    def cat(a, b):
        return jnp.concatenate([a, b], axis=-1)

    def ring(o, d):
        a, b = o[:, :128], o[:, 128:]
        fa, fb = roll(a, -d, 1), roll(b, -d, 1)
        ba, bb = roll(a, d, 1), roll(b, d, 1)
        end, start = lane >= 128 - d, lane < d
        ahead = cat(jnp.where(end, fb, fa), jnp.where(end, fa, fb))
        behind = cat(jnp.where(start, bb, ba), jnp.where(start, ba, bb))
        return ahead, behind

    for copy in loads:
        copy.wait()
    for n in range(3):
        for x in range(NX):
            tmp[n, pl.ds(x * NY, NY), :] = inb[n, x].astype(F32)
    for n in range(2):
        for x in range(NX):
            tmp[3 + n, pl.ds(x * NY, NY), :] = inf[n, x]

    def red_black_of(n, y, j):
        even = tmp[n, pl.ds(y, 8, stride=2 * NY), :]
        odds = tmp[n, pl.ds(NY + y, 8, stride=2 * NY), :]
        par = odd if j % 2 == 0 else jnp.logical_not(odd)
        return jnp.where(par, odds, even), jnp.where(par, even, odds)

    zp[...] = jnp.zeros_like(zp)
    zpf[...] = jnp.zeros_like(zpf)

    def prepare(k, carry):
        packed = jnp.zeros((48, 128), F32)
        packed_f = jnp.zeros((24, 128), F32)
        group = lax.broadcasted_iota(jnp.int32, (48, 128), 1) // 16
        for q in range(8):
            y = 8 * k + q
            parts = []
            for n in range(3):
                parts.extend(red_black_of(n, y, q))
            row = jnp.concatenate(parts, axis=0)
            ha[HY + y] = row.astype(BF16)
            s_r, s_b = red_black_of(3, y, q)
            _, v_b = red_black_of(4, y, q)
            row_f = jnp.concatenate([s_r, s_b, v_b], axis=0)
            hf[HY + y] = row_f
            packed = jnp.where(group == q, roll(row, 16 * q + 8, 1), packed)
            packed_f = jnp.where(group[:24] == q, roll(row_f, 16 * q + 8, 1), packed_f)
        zp[k] = packed.astype(BF16)
        zpf[k] = packed_f
        return carry

    lax.fori_loop(0, 4, prepare, 0)

    pl.semaphore_wait(barrier, GY * GZ - 1)

    def exchange(ex, pieces):
        copies = []
        for n, (dy, dz) in enumerate(NEAR):
            src, dst = pieces(dy, dz)
            copy = pltpu.make_async_remote_copy(
                src, dst, ssem.at[ex, n], rsem.at[ex, n], device_id=peer(dy, dz), device_id_type=MESH
            )
            copy.start()
            copies.append(copy)
        return copies

    def received(copies):
        for copy in copies:
            copy.wait_recv()

    def input_pieces(rows, packed, landing, width):
        def pieces(dy, dz):
            if dz == 0 and dy < 0:
                return rows.at[pl.ds(HY, width)], rows.at[pl.ds(HY + NY, width)]
            if dz == 0:
                return rows.at[pl.ds(HY + NY - width, width)], rows.at[pl.ds(HY - width, width)]
            side = 0 if dz > 0 else 1
            if dy == 0:
                return packed, landing.at[side, pl.ds(1, 4)]
            if dy > 0:
                return packed.at[pl.ds(3, 1)], landing.at[side, pl.ds(0, 1)]
            return packed.at[pl.ds(0, 1)], landing.at[side, pl.ds(5, 1)]

        return pieces

    x_in = exchange(X_IN, input_pieces(ha, zp, zb, 6))
    x_f = exchange(X_F, input_pieces(hf, zpf, zbf, 5))

    zero_row = jnp.zeros((8, 256), F32)
    e3x[...] = jnp.zeros_like(e3x)
    for c in range(2):
        for r in (0, R2 - 1):
            K2[c, r] = zero_row
            V2[c, r] = zero_row
        for r in (0, 1, R1 - 2, R1 - 1):
            V1[c, r] = zero_row
        for r in (3, R0 - 4):
            V0[c, r] = zero_row

    received(x_in)
    received(x_f)

    def row_mask(r, width):
        ok = ((r >= HY) | up_in) & ((r < HY + NY) | down_in)
        lanes = (lane2 < 128) | ((lane2 < 128 + width) & right_in) | ((lane2 >= 256 - width) & left_in)
        return lanes & ok

    def unpack(k, carry):
        group = lax.broadcasted_iota(jnp.int32, (48, 128), 1) % 16 < 8
        merged = jnp.where(group, zb[0, k].astype(F32), zb[1, k].astype(F32))
        merged_f = jnp.where(group[:24], zbf[0, k], zbf[1, k])
        for q in range(8):
            r = 8 * k + q
            ok = row_mask(r, 6) & (r >= 2) & (r < R0 - 2)
            ok5 = row_mask(r, 5) & (r >= 3) & (r < R0 - 3)
            side = roll(merged, 120 - 16 * q, 1)
            side_f = roll(merged_f, 120 - 16 * q, 1)
            a = ha[r].astype(F32)
            f = hf[r]
            for c in range(2):
                s = slice(8 * c, 8 * c + 8)
                ice[c, r] = jnp.where(ok, cat(a[s], side[s]), 0.0)
                s = slice(16 + 8 * c, 24 + 8 * c)
                und[c, r] = cat(a[s], side[s])
                s = slice(32 + 8 * c, 40 + 8 * c)
                prm[c, r] = jnp.where(ok5, cat(a[s], side[s]), 0.0)
                s = slice(8 * c, 8 * c + 8)
                S0[c, r] = cat(f[s], side_f[s])
            V0[1, r] = jnp.where(ok5, cat(f[16:24], side_f[16:24]), 0.0)
        return carry

    lax.fori_loop(0, 6, unpack, 0)

    def pick(c, j):
        return odd2 if (c + j) % 2 == 0 else jnp.logical_not(odd2)

    def x_outer(o, take):
        return jnp.where(take, roll(o, -1, 0), roll(o, 1, 0))

    def x_edge(take):
        return jnp.where(take, sub2, 7 - sub2) == 7

    def near0(ref, c, r, j):
        o = ref[1 - c, r]
        take = pick(c, j)
        ahead, behind = ring(o, 1)
        return (ref[1 - c, r - 1], ref[1 - c, r + 1], o, x_outer(o, take), ahead, behind)

    def permeability(r, j):
        stores = []
        for c in range(2):
            now = ice[c, r]
            near = list(near0(ice, c, r, j))
            near[3] = jnp.where(x_edge(pick(c, j)), 0.0, near[3])
            lap = near[0]
            for value in near[1:]:
                lap = lap + value
            lap = lap - 6.0 * now
            well = 2.0 * now * (1.0 - now) * (1.0 - 2.0 * now)
            drive = 30.0 * now * now * (1.0 - now) * (1.0 - now) * und[c, r]
            new = jnp.clip(now + 0.12 * lap - 0.5 * well + 0.25 * drive, 0.0, 1.0)
            stores.append((K0, (c, r), jnp.where(prm[c, r] > 0.0, prm[c, r] * jnp.exp(-1.5 * new), 0.0)))
            stores.append((und, (c, r), new))
        return stores

    loop(2, R0 - 2, permeability)

    def swap_lanes(x, d):
        return jnp.where((lax.broadcasted_iota(jnp.int32, x.shape, 1) // d) % 2 == 0, roll(x, -d, 1), roll(x, d, 1))

    def swap_subs(x, d):
        return jnp.where((lax.broadcasted_iota(jnp.int32, x.shape, 0) // d) % 2 == 0, roll(x, -d, 0), roll(x, d, 0))

    def parity_y(level, ln, sb):
        return (sb // (1 if level == 1 else 2) + ln // (2 if level == 1 else 4)) % 2 == 1

    def own0(c, r):
        return K0[c, r, :, :128]

    def coarse0(y):
        r = HY + 2 * y
        t = (own0(0, r) + own0(1, r)) + (own0(0, r + 1) + own0(1, r + 1))
        return 0.125 * (t + swap_lanes(t, 1))

    p1, p2 = parity_y(1, lane, sub), parity_y(2, lane, sub)

    def split(p, low, high):
        return jnp.where(p, high, low), jnp.where(p, low, high)

    k2_rows = []
    for yp in range(8):
        red, black = split(p1, coarse0(2 * yp), coarse0(2 * yp + 1))
        KX[1, 1, yp] = jnp.where(odd, black, red)
        t = red + black
        t = t + swap_subs(t, 1)
        k2_rows.append(0.125 * (t + swap_lanes(t, 2)))
    k3_rows = []
    for yp in range(4):
        red, black = split(p2, k2_rows[2 * yp], k2_rows[2 * yp + 1])
        KX[1, 1, 8 + yp] = jnp.where(odd, black, red)
        t = red + black
        t = t + swap_subs(t, 2)
        k3_rows.append(0.125 * (t + swap_lanes(t, 4)))

    def block_pieces(ref):
        return lambda dy, dz: (ref.at[1, 1], ref.at[1 - dy, 1 - dz])

    x_k = exchange(X_K, block_pieces(KX))

    squeeze = (
        lax.broadcasted_iota(jnp.int32, (128, 128), 0) == 8 * (lax.broadcasted_iota(jnp.int32, (128, 128), 1) % 16)
    ).astype(F32)

    def dot(a, b):
        return lax.dot_general(
            a, b, (((1,), (0,)), ((), ())), precision=lax.Precision.HIGHEST, preferred_element_type=F32
        )

    def message(rows):
        piece = jnp.zeros((8, 128), F32)
        for y in range(4):
            u = rows[y]
            t = jnp.where((y + lane // 8) % 2 == 0, u, roll(u, 4, 0))
            piece = jnp.where(sub % 4 == y, t, piece)
        wide = dot(piece, squeeze)
        return jnp.sum(jnp.where(lane // 16 == sub, wide, 0.0), axis=0, keepdims=True)

    def gather(msg, landing, n, row):
        msg[0] = row
        landing[pl.ds(me, 1)] = row.reshape(1, 1, 128)

        def send(i, carry):
            pltpu.make_async_remote_copy(
                msg, landing.at[pl.ds(me, 1)], gs.at[n], gr.at[n], device_id=other(i), device_id_type=MESH
            ).start()
            return carry

        lax.fori_loop(1, GY * GZ, send, 0)

    def all_bytes(landing, sem):
        part = landing.at[pl.ds(0, GY * GZ - 1)]
        pltpu.make_async_copy(part, part, sem).wait()

    def global_level3(landing):
        x = landing[...].reshape(GY, GZ, 128)
        ln = lax.broadcasted_iota(jnp.int32, x.shape, 2)
        sb = lax.broadcasted_iota(jnp.int32, x.shape, 1)
        for bit in (1, 2, 4):
            s_set, t_set = (sb // bit) % 2 == 1, (ln // (16 * bit)) % 2 == 1
            down = roll(roll(x, bit, 1), -16 * bit, 2)
            up = roll(roll(x, -bit, 1), 16 * bit, 2)
            x = jnp.where(s_set == t_set, x, jnp.where(s_set, down, up))
        pairs = x.reshape(GY // 2, 2, 8, 128)
        even, odds = pairs[:, 0], pairs[:, 1]
        low = lax.broadcasted_iota(jnp.int32, even.shape, 1) < 4
        red = jnp.where(low, even, roll(odds, 4, 1))
        black = jnp.where(low, roll(even, 4, 1), odds)
        return red.reshape(64, 128), black.reshape(64, 128)

    gather(msg_k, GK, 0, message(k3_rows))

    def faces0(r, j):
        stores = []
        ok = row_mask(r, 5)
        for c in range(2):
            k = K0[c, r]
            take = pick(c, j)
            edge = x_edge(take)
            near = list(near0(K0, c, r, j))
            near[3] = jnp.where(edge, 0.0, near[3])
            f = [0.5 * (k + value) for value in near]
            d = ((f[0] + f[1]) + (f[2] + f[3])) + (f[4] + f[5])
            inv = jnp.where(ok, 1.0 / d, 0.0)
            for n in range(6):
                g = f[n] * inv
                stores.append((G0, (c, r, n), jnp.where(edge, 0.0, g) if n == 3 else g))
            stores.append((BD0, (c, r), jnp.where(ok, S0[c, r], 0.0) * inv))
            stores.append((D0, (c, r), d))
        return stores

    loop(4, R0 - 4, faces0)

    def update0(c, r, j):
        near = near0(V0, c, r, j)
        t = [G0[c, r, n] * near[n] for n in range(6)]
        return BD0[c, r] + (((t[0] + t[1]) + (t[2] + t[3])) + (t[4] + t[5]))

    def sweep0(c, lo, hi):
        def body(r, j):
            return [(V0, (c, r), update0(c, r, j % 2))]

        loop(lo, hi, body, 4)

    sweep0(0, 4, R0 - 4)
    sweep0(1, 4, R0 - 4)
    sweep0(0, 6, R0 - 6)
    sweep0(1, 6, R0 - 6)

    def defect0(r, j):
        return (D0[0, r] * (update0(0, r, j) - V0[0, r]))[:, :128]

    def right1(yp, j):
        rows = []
        for j in range(2):
            r = HY + 4 * yp + 2 * j
            t = defect0(r, 0) + defect0(r + 1, 1)
            rows.append(0.125 * (t + swap_lanes(t, 1)))
        red, black = split(p1, rows[0], rows[1])
        return [(b1, (8 + yp,), jnp.where(odd, black, red))]

    loop(0, 8, right1, 2)
    for k in range(4):
        first, second = b1[8 + 2 * k], b1[9 + 2 * k]
        zp1[k] = jnp.where(lane < 64, roll(first, 32, 1), roll(second, 96, 1))

    def b1_pieces(dy, dz):
        if dz == 0 and dy < 0:
            return b1.at[pl.ds(8, 6)], b1.at[pl.ds(16, 6)]
        if dz == 0:
            return b1.at[pl.ds(10, 6)], b1.at[pl.ds(2, 6)]
        side = 0 if dz > 0 else 1
        if dy == 0:
            return zp1, zb1.at[side, pl.ds(4, 4)]
        if dy > 0:
            return zp1.at[pl.ds(1, 3)], zb1.at[side, pl.ds(1, 3)]
        return zp1.at[pl.ds(0, 3)], zb1.at[side, pl.ds(8, 3)]

    x_b1 = exchange(X_B1, b1_pieces)

    received(x_k)

    def joined(ref, yb, r):
        a = ref[yb, 1, r]
        b = jnp.where(lane < 64, ref[yb, 2, r], ref[yb, 0, r])
        return cat(a, b)

    def apart(x):
        a, b = x[:, :128], x[:, 128:]
        red = cat(jnp.where(odd, roll(a, 1, 1), a), jnp.where(odd, roll(b, 1, 1), b))
        black = cat(jnp.where(odd, a, roll(a, -1, 1)), jnp.where(odd, b, roll(b, -1, 1)))
        return red, black

    for yb in range(3):
        row_ok = (up_in, True, down_in)[yb]
        ok = ring_in & row_ok

        def spread1(r, carry, yb=yb, ok=ok):
            red, black = apart(joined(KX, yb, r))
            K1[0, 8 * yb + r] = jnp.where(ok, red, 0.0)
            K1[1, 8 * yb + r] = jnp.where(ok, black, 0.0)
            return carry

        lax.fori_loop(0, 8, spread1, 0)
        for r in range(4):
            red, black = apart(joined(KX, yb, 8 + r))
            K2[0, 1 + 4 * yb + r] = jnp.where(ok, red, 0.0)
            K2[1, 1 + 4 * yb + r] = jnp.where(ok, black, 0.0)

    def near_y(level, ref, c, r):
        dx, dz = (1, 2) if level == 1 else (2, 4)
        p = parity_y(level, lane2, sub2)
        o, low, high = ref[1 - c, r], ref[1 - c, r - 1], ref[1 - c, r + 1]
        outer = jnp.where(p, high, low) if c == 0 else jnp.where(p, low, high)
        ahead, behind = ring(o, dz)
        return (o, outer, roll(o, -dx, 0), roll(o, dx, 0), ahead, behind)

    def faces_y(level, K, G, I, D, r):
        dx = 1 if level == 1 else 2
        s = 0.25**level
        stores = []
        for c in range(2):
            k = K[c, r]
            near = list(near_y(level, K, c, r))
            last, first = sub2 >= 8 - dx, sub2 < dx
            near[2] = jnp.where(last, 0.0, near[2])
            near[3] = jnp.where(first, 0.0, near[3])
            f = [0.5 * (k + value) for value in near]
            d = ((f[0] + f[1]) + (f[2] + f[3])) + (f[4] + f[5])
            inv = jnp.where(k > 0.0, 1.0 / d, 0.0)
            for n in range(6):
                g = f[n] * inv
                if n == 2:
                    g = jnp.where(last, 0.0, g)
                if n == 3:
                    g = jnp.where(first, 0.0, g)
                stores.append((G, (c, r, n), g))
            stores.append((I, (c, r), inv * (1.0 / s)))
            if c == 0:
                stores.append((D, (r,), s * d))
        return stores

    loop(2, R1 - 2, lambda r, j: faces_y(1, K1, G1, I1, D1, r))
    loop(1, R2 - 1, lambda r, j: faces_y(2, K2, G2, I2, D2, r))

    all_bytes(GK, gr.at[0])
    k3r, k3b = global_level3(GK)
    row3 = lax.broadcasted_iota(jnp.int32, (64, 128), 0)
    lane3 = lax.broadcasted_iota(jnp.int32, (64, 128), 1)
    odd3 = (row3 + lane3) % 2 == 1
    edges3 = (row3 == 0, row3 == 63, lane3 == 0, lane3 == 127)

    def near3(o):
        return (roll(o, 1, 0), roll(o, -1, 0), roll(o, 1, 1), roll(o, -1, 1), o)

    def faces3(c, k, o):
        s = 0.25**3
        near = [jnp.where(e, 0.0, v) for e, v in zip(edges3, near3(o))] + [o]
        f = [0.5 * (k + value) for value in near] + [0.5 * k]
        d = ((f[0] + f[1]) + (f[2] + f[3])) + (f[4] + f[5])
        inv = 1.0 / d
        for n in range(5):
            g = f[n] * inv
            G3[c, n] = jnp.where(edges3[n], 0.0, g) if n < 4 else g
        I3[c] = inv * (1.0 / s)
        if c == 0:
            D3[...] = s * d

    faces3(0, k3r, k3b)
    faces3(1, k3b, k3r)

    lane4 = lax.broadcasted_iota(jnp.int32, (16, 128), 1)
    row4 = lax.broadcasted_iota(jnp.int32, (16, 128), 0)
    p4 = (lane4 // 2) % 2 == 1

    def level4_of(total):
        t = total + swap_subs(total, 1)
        buf4[...] = 0.125 * (t + swap_lanes(t, 1))
        low, high = buf4[pl.ds(0, 16, stride=4), :], buf4[pl.ds(2, 16, stride=4), :]
        return split(p4, low, high)

    k4 = level4_of(k3r + k3b)

    def near4(c, o):
        low, high = roll(o, 1, 0), roll(o, -1, 0)
        outer = jnp.where(p4, high, low) if c == 0 else jnp.where(p4, low, high)
        return (o, outer, roll(o, -2, 1), roll(o, 2, 1))

    def faces4(c):
        s = 0.25**4
        k = k4[c]
        take = p4 if c == 0 else jnp.logical_not(p4)
        edges = (None, jnp.where(take, row4, 15 - row4) == 15, lane4 >= 126, lane4 < 2)
        near = near4(c, k4[1 - c])
        near = [v if e is None else jnp.where(e, 0.0, v) for e, v in zip(edges, near)]
        f = [0.5 * (k + value) for value in near]
        d = ((f[0] + f[1]) + (f[2] + f[3])) + k
        inv = 1.0 / d
        g = [v * inv if e is None else jnp.where(e, 0.0, v * inv) for e, v in zip(edges, f)]
        return g, inv * (1.0 / s)

    g4r, i4r = faces4(0)
    g4b, i4b = faces4(1)

    received(x_b1)

    def v0_pieces(dy, dz):
        def at(r, n):
            return V0.at[1, pl.ds(r, n), :, pl.ds(0, 128)]

        lo, n, to = {-1: (HY, 5, HY + NY), 0: (HY, NY, HY), 1: (HY + NY - 5, 5, HY - 5)}[dy]
        if dz == 0:
            return at(lo, n), at(to, n)
        return at(lo, n), zv.at[0 if dz > 0 else 1, pl.ds(to, n)]

    def spread_b(k, j):
        stores = []
        merged = jnp.where(lane % 64 < 32, zb1[0, k], zb1[1, k])
        for q in range(2):
            r = 2 * k + q
            red, black = apart(cat(b1[r], roll(merged, -64 * q - 32, 1)))
            stores.append((BD1, (0, r), jnp.where(I1[0, r] > 0.0, red, 0.0) * I1[0, r]))
            stores.append((BD1, (1, r), jnp.where(I1[1, r] > 0.0, black, 0.0) * I1[1, r]))
            stores.append((V1, (0, r), stores[-2][2]))
        return stores

    loop(1, 11, spread_b, 2)

    def update_y(level, V, G, BD, c, r):
        near = near_y(level, V, c, r)
        t = [G[c, r, n] * near[n] for n in range(6)]
        return BD[c, r] + (((t[0] + t[1]) + (t[2] + t[3])) + (t[4] + t[5]))

    def sweep_y(level, V, G, BD, c, lo, hi):
        def body(r, j):
            return [(V, (c, r), update_y(level, V, G, BD, c, r))]

        loop(lo, hi, body, 4)

    sweep_y(1, V1, G1, BD1, 1, 2, 22)
    sweep_y(1, V1, G1, BD1, 0, 2, 22)
    sweep_y(1, V1, G1, BD1, 1, 2, 22)

    p2w = parity_y(2, lane2, sub2)

    def right2(i, j):
        rows = []
        for j in range(2):
            r = 4 + 2 * i + j
            t = D1[r] * (update_y(1, V1, G1, BD1, 0, r) - V1[0, r])
            t = t + swap_subs(t, 1)
            a, b = t[:, :128], t[:, 128:]
            rows.append(0.125 * cat(a + swap_lanes(a, 2), b + swap_lanes(b, 2)))
        red, black = split(p2w, rows[0], rows[1])
        row = 3 + i
        first = red * I2[0, row]
        return [
            (BD2, (0, row), first),
            (V2, (0, row), first),
            (BD2, (1, row), black * I2[1, row]),
            (pair2, (i,), jnp.where(odd, black[:, :128], red[:, :128])),
        ]

    V2[0, 2] = zero_row
    V2[0, 11] = zero_row
    V2[1, 2] = zero_row
    V2[1, 11] = zero_row
    loop(0, 8, right2, 2)

    sweep_y(2, V2, G2, BD2, 1, 3, 11)
    sweep_y(2, V2, G2, BD2, 0, 3, 11)
    sweep_y(2, V2, G2, BD2, 1, 3, 11)
    rows = []
    for y in range(4):
        r = 5 + y
        t = (D2[r] * (update_y(2, V2, G2, BD2, 0, r) - V2[0, r]))[:, :128]
        t = t + swap_subs(t, 2)
        rows.append(0.125 * (t + swap_lanes(t, 4)))
    gather(msg_b, GB, 1, message(rows))

    for y in range(4):
        CX[1, 1, y] = jnp.where(lane % 4 < 2, pair2[2 + y], V2[1, 5 + y, :, :128])
    x_b2 = exchange(X_B2, block_pieces(CX))
    x_v0 = exchange(X_V0, v0_pieces)
    received(x_b2)
    for yb in range(3):
        row_ok = (up_in, True, down_in)[yb]
        for r in range(4):
            x = joined(CX, yb, r)
            row = 1 + 4 * yb + r

            def fill(x):
                a, b = x[:, :128], x[:, 128:]
                first = cat(jnp.where(odd, roll(a, 1, 1), a), jnp.where(odd, roll(b, 1, 1), b))
                second = cat(jnp.where(odd, a, roll(a, -1, 1)), jnp.where(odd, b, roll(b, -1, 1)))
                return first, second

            first, second = fill(x)
            head = lane2 % 4 < 2

            def pair_up(y):
                return cat(roll(y[:, :128], 2, 1), roll(y[:, 128:], 2, 1))

            def pair_down(y):
                return cat(roll(y[:, :128], -2, 1), roll(y[:, 128:], -2, 1))

            BD2[0, row] = jnp.where(head, first, pair_up(first)) * I2[0, row]
            BD2[1, row] = jnp.where(head, second, pair_up(second)) * I2[1, row]
            V2[1, row] = jnp.where(ring_in & row_ok, jnp.where(head, pair_down(x), x), 0.0)

    received(x_v0)
    for copy in x_v0:
        copy.wait_send()

    def v0_sides(r, j):
        ok = ((r >= HY) | up_in) & ((r < HY + NY) | down_in)
        side = jnp.where(
            ok & (((lane < 5) & right_in) | ((lane >= 123) & left_in)), jnp.where(lane < 64, zv[1, r], zv[0, r]), 0.0
        )
        return [(V0, (1, r), cat(jnp.where(ok, V0[1, r, :, :128], 0.0), side))]

    loop(HY - 5, HY + NY + 5, v0_sides, 3)
    zrow = lax.broadcasted_iota(jnp.int32, (128, 256), 0)
    zcol = lax.broadcasted_iota(jnp.int32, (128, 256), 1)
    expand = (zrow == gz * 16 + zcol // 8 - jnp.where(zcol >= 192, 32, 0)).astype(F32)

    all_bytes(GB, gr.at[1])
    b3r, b3b = global_level3(GB)
    bd3 = (b3r * I3[0], b3b * I3[1])

    def update3(c, o):
        near = near3(o)
        t = [G3[c, n] * near[n] for n in range(5)]
        return bd3[c] + (((t[0] + t[1]) + (t[2] + t[3])) + t[4])

    v_r = bd3[0]
    v_b = update3(1, v_r)
    v_r = update3(0, v_b)
    v_b = update3(1, v_r)
    r3 = D3[...] * (update3(0, v_b) - v_r)
    b4 = level4_of(r3)
    bd4r, bd4b = b4[0] * i4r, b4[1] * i4b

    def update4(c, g, bd, o):
        near = near4(c, o)
        return bd + ((g[0] * near[0] + g[1] * near[1]) + (g[2] * near[2] + g[3] * near[3]))

    def sweep4(i, carry):
        red, black = carry
        red = update4(0, g4r, bd4r, black)
        black = update4(1, g4b, bd4b, red)
        return red, black

    zero4 = jnp.zeros((16, 128), F32)
    e_r, e_b = lax.fori_loop(0, COARSE_SWEEPS, sweep4, (zero4, zero4))
    low, high = split(p4, e_r, e_b)
    buf4[pl.ds(0, 16, stride=4), :] = low
    buf4[pl.ds(1, 16, stride=4), :] = low
    buf4[pl.ds(2, 16, stride=4), :] = high
    buf4[pl.ds(3, 16, stride=4), :] = high
    v_b = v_b + buf4[...]
    v_r = update3(0, v_b)
    v_b = update3(1, v_r)
    v_r = update3(0, v_b)
    v_b = update3(1, v_r)

    x_low, x_high = split(odd3, v_r, v_b)
    e3x[0, pl.ds(8, 64), :] = x_low
    e3x[1, pl.ds(8, 64), :] = x_high
    parts = []
    for n in range(2):
        for i in range(12):
            parts.append(e3x[n, pl.ds(gy * 4 + (4 + i), 1), :])
    wide = dot(jnp.concatenate(parts, axis=0), expand)
    for i in range(12):
        e = jnp.where(sub2 < 4, wide[i : i + 1], wide[12 + i : 13 + i])
        row_ok = up_in if i < 4 else (down_in if i >= 8 else True)
        V2[1, 1 + i] = V2[1, 1 + i] + jnp.where(ring_in & row_ok, e, 0.0)
    sweep_y(2, V2, G2, BD2, 0, 1, 13)
    sweep_y(2, V2, G2, BD2, 1, 1, 13)
    sweep_y(2, V2, G2, BD2, 0, 1, 13)
    sweep_y(2, V2, G2, BD2, 1, 3, 11)

    p1w = parity_y(1, lane2, sub2)

    def correct1(i, j):
        low, high = split(p2w, V2[0, 3 + i], V2[1, 3 + i])
        return [(V1, (1, 4 + 2 * i + n), V1[1, 4 + 2 * i + n] + e) for n, e in ((0, low), (1, high))]

    loop(0, 8, correct1, 4)
    sweep_y(1, V1, G1, BD1, 0, 4, 20)
    sweep_y(1, V1, G1, BD1, 1, 4, 20)
    sweep_y(1, V1, G1, BD1, 0, 4, 20)
    sweep_y(1, V1, G1, BD1, 1, 6, 18)

    def correct0(i, j):
        low, high = split(p1w, V1[0, 6 + i], V1[1, 6 + i])
        return [
            (V0, (1, 4 * i + n), V0[1, 4 * i + n] + e) for n, e in ((0, low), (1, low), (2, high), (3, high))
        ]

    loop(0, 12, correct0, 2)
    sweep0(0, 4, R0 - 4)
    sweep0(1, 4, R0 - 4)
    sweep0(0, 6, R0 - 6)
    sweep0(1, 6, R0 - 6)

    def results(r, j):
        y = r - HY
        par = odd if j % 2 == 0 else jnp.logical_not(odd)
        stores = []

        def put(n, red, black):
            stores.append((tmp, (n, pl.ds(y, 8, stride=2 * NY)), jnp.where(par, black, red)))
            stores.append((tmp, (n, pl.ds(NY + y, 8, stride=2 * NY)), jnp.where(par, red, black)))

        v_red, v_black = V0[0, r], V0[1, r]
        put(0, v_red[:, :128], v_black[:, :128])
        res_red = D0[0, r] * (update0(0, r, j) - v_red)
        res_black = D0[1, r] * (update0(1, r, j) - v_black)
        put(1, res_red[:, :128], res_black[:, :128])
        put(2, und[0, r, :, :128], und[1, r, :, :128])
        return stores

    loop(HY, HY + NY, results)
    for x in range(NX):
        outb[x] = tmp[2, pl.ds(x * NY, NY), :].astype(BF16)
        pb[0, x] = tmp[0, pl.ds(x * NY, NY), :]
        pb[1, x] = tmp[1, pl.ds(x * NY, NY), :]
    stores = []
    for n, (src, dst) in enumerate(((outb, phase_o), (pb.at[0], pres_o), (pb.at[1], res_o))):
        copy = pltpu.make_async_copy(src, dst, osem.at[n])
        copy.start()
        stores.append(copy)

    for copies in (x_in, x_f, x_k, x_b1, x_b2):
        for copy in copies:
            copy.wait_send()
    all_bytes(GK, gs.at[0])
    all_bytes(GB, gs.at[1])
    for copy in stores:
        copy.wait()


def per_device(GY, GZ, phase, undercool, perm_base, source, pressure):
    def vm(*shape):
        return pltpu.VMEM(shape, F32)

    scratch = [
        pltpu.VMEM((3, NX, NY, NZ), BF16),
        vm(2, NX, NY, NZ),
        vm(5, NX * NY, NZ),
        vm(2, NX, NY, NZ),
        pltpu.VMEM((NX, NY, NZ), BF16),
        pltpu.VMEM((R0, 48, 128), BF16),
        vm(R0, 24, 128),
        pltpu.VMEM((4, 48, 128), BF16),
        vm(4, 24, 128),
        pltpu.VMEM((2, 6, 48, 128), BF16),
        vm(2, 6, 24, 128),
        vm(2, R0, 8, 256),
        vm(2, R0, 8, 256),
        vm(2, R0, 8, 256),
        vm(2, R0, 8, 256),
        vm(2, R0, 8, 256),
        vm(2, R0, 8, 256),
        vm(2, R0, 6, 8, 256),
        vm(2, R0, 8, 256),
        vm(2, R0, 8, 256),
        vm(2, R0, 8, 128),
        vm(3, 3, 12, 8, 128),
        vm(3, 3, 4, 8, 128),
        vm(2, R1, 8, 256),
        vm(2, R1, 8, 256),
        vm(2, R1, 6, 8, 256),
        vm(2, R1, 8, 256),
        vm(2, R1, 8, 256),
        vm(R1, 8, 256),
        vm(2, R2, 8, 256),
        vm(2, R2, 8, 256),
        vm(2, R2, 6, 8, 256),
        vm(2, R2, 8, 256),
        vm(2, R2, 8, 256),
        vm(R2, 8, 256),
        vm(R1, 8, 128),
        vm(4, 8, 128),
        vm(2, 12, 8, 128),
        vm(1, 1, 128),
        vm(1, 1, 128),
        vm(GY * GZ, 1, 128),
        vm(GY * GZ, 1, 128),
        vm(2, 64, 128),
        vm(2, 5, 64, 128),
        vm(2, 64, 128),
        vm(64, 128),
        vm(64, 128),
        vm(2, 80, 128),
        vm(8, 8, 128),
        pltpu.SemaphoreType.DMA((N_X, 8)),
        pltpu.SemaphoreType.DMA((N_X, 8)),
        pltpu.SemaphoreType.DMA((2,)),
        pltpu.SemaphoreType.DMA((2,)),
        pltpu.SemaphoreType.DMA((5,)),
        pltpu.SemaphoreType.DMA((3,)),
    ]
    hbm = pl.BlockSpec(memory_space=pltpu.HBM)
    return pl.pallas_call(
        functools.partial(kernel, GY, GZ),
        out_shape=(
            jax.ShapeDtypeStruct((NX, NY, NZ), BF16),
            jax.ShapeDtypeStruct((NX, NY, NZ), F32),
            jax.ShapeDtypeStruct((NX, NY, NZ), F32),
        ),
        in_specs=[hbm] * 5,
        out_specs=(hbm, hbm, hbm),
        scratch_shapes=scratch,
        compiler_params=pltpu.CompilerParams(
            collective_id=0, has_side_effects=True, vmem_limit_bytes=48 * 2**20
        ),
    )(phase, undercool, perm_base, source, pressure)


def solution(mesh):
    spec = P(None, "gy", "gz")
    return jax.shard_map(
        functools.partial(per_device, mesh.shape["gy"], mesh.shape["gz"]),
        mesh=mesh,
        in_specs=(spec,) * 5,
        out_specs=(spec,) * 3,
        check_vma=False,
    )
```

```python
import functools
import jax
import jax.numpy as jnp
from jax import lax
from jax.experimental import pallas as pl
from jax.experimental.pallas import tpu as pltpu
from jax.sharding import PartitionSpec as P

MESH = pl.DeviceIdType.MESH
F32 = jnp.float32
BF16 = jnp.bfloat16
COARSE_SWEEPS = 20
NX, NY, NZ = 16, 32, 128
HY = 8
R0 = NY + 2 * HY
R1 = 24
R2 = 14
NEAR = [(dy, dz) for dy in (-1, 0, 1) for dz in (-1, 0, 1) if (dy, dz) != (0, 0)]
X_IN, X_F, X_K, X_B1, X_V0, X_B2 = range(6)
N_X = 6


def roll(x, shift, axis):
    size = x.shape[axis]
    shift = shift % size
    return x if shift == 0 else pltpu.roll(x, shift, axis)


def loop(lo, hi, body, step=2):
    def trip(i, carry):
        stores = []
        for j in range(step):
            stores.extend(body(lo + i * step + j, j))
        for ref, index, value in stores:
            ref[index] = value
        return carry

    trips = (hi - lo) // step
    assert trips * step == hi - lo
    if trips == 1:
        trip(0, 0)
    else:
        lax.fori_loop(0, trips, trip, 0)


def kernel(
    GY, GZ, phase_h, under_h, perm_h, src_h, pres_h, ice_o, fin_o,
    inb, tmp, outb, outf,
    ha, hf, zp, zpf, zb, zbf,
    ice, und, prm, S0, V0, K0, G0, BD0, D0, zv,
    KX, CX, K1, V1, G1, I1, BD1, D1, K2, V2, G2, I2, BD2, D2,
    b1, zp1, zb1, msg_k, msg_b, GK, GB, K3, G3, I3, D3, buf4, e3x, pair2,
    ssem, rsem, gs, gr, lsem, osem, known,
):
    gy, gz = lax.axis_index("gy"), lax.axis_index("gz")
    me = gy * GZ + gz

    def peer(dy, dz):
        return (lax.rem(gy + dy + GY, GY), lax.rem(gz + dz + GZ, GZ))

    barrier = pltpu.get_barrier_semaphore()

    for dy, dz in NEAR:
        pl.semaphore_signal(barrier, inc=1, device_id=peer(dy, dz), device_id_type=MESH)

    loads = []
    for n, (src, dst) in enumerate(
        ((phase_h, inb.at[0]), (under_h, inb.at[1]), (perm_h, inb.at[2]), (src_h, tmp.at[3]), (pres_h, tmp.at[4]))
    ):
        copy = pltpu.make_async_copy(src, dst, lsem.at[n])
        copy.start()
        loads.append(copy)

    lane = lax.broadcasted_iota(jnp.int32, (8, 128), 1)
    sub = lax.broadcasted_iota(jnp.int32, (8, 128), 0)
    lane2 = lax.broadcasted_iota(jnp.int32, (8, 256), 1)
    sub2 = lax.broadcasted_iota(jnp.int32, (8, 256), 0)
    odd = lane % 2 == 1
    odd2 = lane2 % 2 == 1
    right_in, left_in = gz < GZ - 1, gz > 0
    up_in, down_in = gy > 0, gy < GY - 1
    ring_in = (lane2 < 128) | ((lane2 < 192) & right_in) | ((lane2 >= 192) & left_in)

    def cat(a, b):
        return jnp.concatenate([a, b], axis=-1)

    def ring(o, d):
        a, b = o[:, :128], o[:, 128:]
        fa, fb = roll(a, -d, 1), roll(b, -d, 1)
        ba, bb = roll(a, d, 1), roll(b, d, 1)
        end, start = lane >= 128 - d, lane < d
        ahead = cat(jnp.where(end, fb, fa), jnp.where(end, fa, fb))
        behind = cat(jnp.where(start, bb, ba), jnp.where(start, ba, bb))
        return ahead, behind

    for copy in loads:
        copy.wait()
    for n in range(3):
        tmp[n] = inb[n].astype(F32)

    def red_black_of(n, y, j):
        even = tmp[n, pl.ds(y, 8, stride=2 * NY), :]
        odds = tmp[n, pl.ds(NY + y, 8, stride=2 * NY), :]
        par = odd if j % 2 == 0 else jnp.logical_not(odd)
        return jnp.where(par, odds, even), jnp.where(par, even, odds)

    zp[...] = jnp.zeros_like(zp)
    zpf[...] = jnp.zeros_like(zpf)

    def prepare(k, carry):
        packed = jnp.zeros((48, 128), F32)
        packed_f = jnp.zeros((24, 128), F32)
        group = lax.broadcasted_iota(jnp.int32, (48, 128), 1) // 16
        for q in range(8):
            y = 8 * k + q
            parts = []
            for n in range(3):
                parts.extend(red_black_of(n, y, q))
            row = jnp.concatenate(parts, axis=0)
            ha[HY + y] = row.astype(BF16)
            s_r, s_b = red_black_of(3, y, q)
            _, v_b = red_black_of(4, y, q)
            row_f = jnp.concatenate([s_r, s_b, v_b], axis=0)
            hf[HY + y] = row_f
            packed = jnp.where(group == q, roll(row, 16 * q + 8, 1), packed)
            packed_f = jnp.where(group[:24] == q, roll(row_f, 16 * q + 8, 1), packed_f)
        zp[k] = packed.astype(BF16)
        zpf[k] = packed_f
        return carry

    lax.fori_loop(0, 4, prepare, 0)

    pl.semaphore_wait(barrier, len(NEAR))

    def exchange(ex, pieces):
        copies = []
        for n, (dy, dz) in enumerate(NEAR):
            src, dst = pieces(dy, dz)
            copy = pltpu.make_async_remote_copy(
                src, dst, ssem.at[ex, n], rsem.at[ex, n], device_id=peer(dy, dz), device_id_type=MESH
            )
            copy.start()
            copies.append(copy)
        return copies

    def received(copies):
        for copy in copies:
            copy.wait_recv()

    def input_pieces(rows, packed, landing, width):
        def pieces(dy, dz):
            if dz == 0 and dy < 0:
                return rows.at[pl.ds(HY, width)], rows.at[pl.ds(HY + NY, width)]
            if dz == 0:
                return rows.at[pl.ds(HY + NY - width, width)], rows.at[pl.ds(HY - width, width)]
            side = 0 if dz > 0 else 1
            if dy == 0:
                return packed, landing.at[side, pl.ds(1, 4)]
            if dy > 0:
                return packed.at[pl.ds(3, 1)], landing.at[side, pl.ds(0, 1)]
            return packed.at[pl.ds(0, 1)], landing.at[side, pl.ds(5, 1)]

        return pieces

    x_in = exchange(X_IN, input_pieces(ha, zp, zb, 6))
    x_f = exchange(X_F, input_pieces(hf, zpf, zbf, 5))

    zero_row = jnp.zeros((8, 256), F32)
    e3x[...] = jnp.zeros_like(e3x)
    for c in range(2):
        for r in (0, R2 - 1):
            K2[c, r] = zero_row
            V2[c, r] = zero_row
        for r in (0, 1, R1 - 2, R1 - 1):
            V1[c, r] = zero_row
        for r in (3, R0 - 4):
            V0[c, r] = zero_row

    received(x_in)
    received(x_f)
    for dy, dz in NEAR:
        pl.semaphore_signal(known.at[0], inc=1, device_id=peer(2 * dy, 2 * dz), device_id_type=MESH)

    def row_mask(r, width):
        ok = ((r >= HY) | up_in) & ((r < HY + NY) | down_in)
        lanes = (lane2 < 128) | ((lane2 < 128 + width) & right_in) | ((lane2 >= 256 - width) & left_in)
        return lanes & ok

    def unpack(k, carry):
        group = lax.broadcasted_iota(jnp.int32, (48, 128), 1) % 16 < 8
        merged = jnp.where(group, zb[0, k].astype(F32), zb[1, k].astype(F32))
        merged_f = jnp.where(group[:24], zbf[0, k], zbf[1, k])
        for q in range(8):
            r = 8 * k + q
            ok = row_mask(r, 6) & (r >= 2) & (r < R0 - 2)
            ok5 = row_mask(r, 5) & (r >= 3) & (r < R0 - 3)
            side = roll(merged, 120 - 16 * q, 1)
            side_f = roll(merged_f, 120 - 16 * q, 1)
            a = ha[r].astype(F32)
            f = hf[r]
            for c in range(2):
                s = slice(8 * c, 8 * c + 8)
                ice[c, r] = jnp.where(ok, cat(a[s], side[s]), 0.0)
                s = slice(16 + 8 * c, 24 + 8 * c)
                und[c, r] = cat(a[s], side[s])
                s = slice(32 + 8 * c, 40 + 8 * c)
                prm[c, r] = jnp.where(ok5, cat(a[s], side[s]), 0.0)
                s = slice(8 * c, 8 * c + 8)
                S0[c, r] = cat(f[s], side_f[s])
            V0[1, r] = jnp.where(ok5, cat(f[16:24], side_f[16:24]), 0.0)
        return carry

    lax.fori_loop(0, 6, unpack, 0)

    def pick(c, j):
        return odd2 if (c + j) % 2 == 0 else jnp.logical_not(odd2)

    def x_outer(o, take):
        return jnp.where(take, roll(o, -1, 0), roll(o, 1, 0))

    def x_edge(take):
        return jnp.where(take, sub2, 7 - sub2) == 7

    def near0(ref, c, r, j):
        o = ref[1 - c, r]
        take = pick(c, j)
        ahead, behind = ring(o, 1)
        return (ref[1 - c, r - 1], ref[1 - c, r + 1], o, x_outer(o, take), ahead, behind)

    def permeability(r, j):
        stores = []
        for c in range(2):
            now = ice[c, r]
            near = list(near0(ice, c, r, j))
            near[3] = jnp.where(x_edge(pick(c, j)), 0.0, near[3])
            lap = near[0]
            for value in near[1:]:
                lap = lap + value
            lap = lap - 6.0 * now
            well = 2.0 * now * (1.0 - now) * (1.0 - 2.0 * now)
            drive = 30.0 * now * now * (1.0 - now) * (1.0 - now) * und[c, r]
            new = jnp.clip(now + 0.12 * lap - 0.5 * well + 0.25 * drive, 0.0, 1.0)
            stores.append((K0, (c, r), jnp.where(prm[c, r] > 0.0, prm[c, r] * jnp.exp(-1.5 * new), 0.0)))
            stores.append((und, (c, r), new))
        return stores

    loop(2, R0 - 2, permeability)

    def swap_lanes(x, d):
        return jnp.where((lax.broadcasted_iota(jnp.int32, x.shape, 1) // d) % 2 == 0, roll(x, -d, 1), roll(x, d, 1))

    def swap_subs(x, d):
        return jnp.where((lax.broadcasted_iota(jnp.int32, x.shape, 0) // d) % 2 == 0, roll(x, -d, 0), roll(x, d, 0))

    def parity_y(level, ln, sb):
        return (sb // (1 if level == 1 else 2) + ln // (2 if level == 1 else 4)) % 2 == 1

    def own0(c, r):
        return K0[c, r, :, :128]

    def coarse0(y):
        r = HY + 2 * y
        t = (own0(0, r) + own0(1, r)) + (own0(0, r + 1) + own0(1, r + 1))
        return 0.125 * (t + swap_lanes(t, 1))

    p1, p2 = parity_y(1, lane, sub), parity_y(2, lane, sub)

    def split(p, low, high):
        return jnp.where(p, high, low), jnp.where(p, low, high)

    k2_rows = []
    for yp in range(8):
        red, black = split(p1, coarse0(2 * yp), coarse0(2 * yp + 1))
        KX[1, 1, yp] = jnp.where(odd, black, red)
        t = red + black
        t = t + swap_subs(t, 1)
        k2_rows.append(0.125 * (t + swap_lanes(t, 2)))
    k3_rows = []
    for yp in range(4):
        red, black = split(p2, k2_rows[2 * yp], k2_rows[2 * yp + 1])
        KX[1, 1, 8 + yp] = jnp.where(odd, black, red)
        t = red + black
        t = t + swap_subs(t, 2)
        k3_rows.append(0.125 * (t + swap_lanes(t, 4)))

    def block_pieces(ref):
        return lambda dy, dz: (ref.at[1, 1], ref.at[1 - dy, 1 - dz])

    x_k = exchange(X_K, block_pieces(KX))

    squeeze = (
        lax.broadcasted_iota(jnp.int32, (128, 128), 0) == 8 * (lax.broadcasted_iota(jnp.int32, (128, 128), 1) % 16)
    ).astype(F32)

    def dot(a, b):
        return lax.dot_general(
            a, b, (((1,), (0,)), ((), ())), precision=lax.Precision.HIGHEST, preferred_element_type=F32
        )

    def message(rows):
        piece = jnp.zeros((8, 128), F32)
        for y in range(4):
            u = rows[y]
            t = jnp.where((y + lane // 8) % 2 == 0, u, roll(u, 4, 0))
            piece = jnp.where(sub % 4 == y, t, piece)
        wide = dot(piece, squeeze)
        return jnp.sum(jnp.where(lane // 16 == sub, wide, 0.0), axis=0, keepdims=True)

    def gather(msg, landing, n, row):
        msg[0] = row
        landing[pl.ds(me, 1)] = row.reshape(1, 1, 128)

        def start(y, z):
            pltpu.make_async_remote_copy(
                msg, landing.at[pl.ds(me, 1)], gs.at[n], gr.at[n], device_id=(y, z), device_id_type=MESH
            ).start()

        columns = [lax.rem(gz + i, GZ) for i in (4, 3, 5, 2, 6, 1, 7, 0)]

        def send(i, carry):
            y = lax.rem(gy + i, GY)
            for z in columns:
                start(y, z)
            return carry

        lax.fori_loop(1, GY, send, 0)
        for z in columns[:-1]:
            start(gy, z)

    def all_bytes(landing, sem):
        part = landing.at[pl.ds(0, GY * GZ - 1)]
        pltpu.make_async_copy(part, part, sem).wait()

    def global_level3(landing):
        x = landing[...].reshape(GY, GZ, 128)
        ln = lax.broadcasted_iota(jnp.int32, x.shape, 2)
        sb = lax.broadcasted_iota(jnp.int32, x.shape, 1)
        for bit in (1, 2, 4):
            s_set, t_set = (sb // bit) % 2 == 1, (ln // (16 * bit)) % 2 == 1
            down = roll(roll(x, bit, 1), -16 * bit, 2)
            up = roll(roll(x, -bit, 1), 16 * bit, 2)
            x = jnp.where(s_set == t_set, x, jnp.where(s_set, down, up))
        pairs = x.reshape(GY // 2, 2, 8, 128)
        even, odds = pairs[:, 0], pairs[:, 1]
        low = lax.broadcasted_iota(jnp.int32, even.shape, 1) < 4
        red = jnp.where(low, even, roll(odds, 4, 1))
        black = jnp.where(low, roll(even, 4, 1), odds)
        return red.reshape(64, 128), black.reshape(64, 128)

    row_k = message(k3_rows)

    pl.semaphore_wait(known.at[0], len(NEAR))
    for dy in (-4, 4):
        pl.semaphore_signal(known.at[1], inc=1, device_id=peer(dy, 0), device_id_type=MESH)

    def faces0(r, j):
        stores = []
        ok = row_mask(r, 5)
        for c in range(2):
            k = K0[c, r]
            take = pick(c, j)
            edge = x_edge(take)
            near = list(near0(K0, c, r, j))
            near[3] = jnp.where(edge, 0.0, near[3])
            f = [0.5 * (k + value) for value in near]
            d = ((f[0] + f[1]) + (f[2] + f[3])) + (f[4] + f[5])
            inv = jnp.where(ok, 1.0 / d, 0.0)
            for n in range(6):
                g = f[n] * inv
                stores.append((G0, (c, r, n), jnp.where(edge, 0.0, g) if n == 3 else g))
            stores.append((BD0, (c, r), jnp.where(ok, S0[c, r], 0.0) * inv))
            stores.append((D0, (c, r), d))
        return stores

    loop(4, R0 - 4, faces0)

    def update0(c, r, j):
        near = near0(V0, c, r, j)
        t = [G0[c, r, n] * near[n] for n in range(6)]
        return BD0[c, r] + (((t[0] + t[1]) + (t[2] + t[3])) + (t[4] + t[5]))

    def sweep0(c, lo, hi):
        def body(r, j):
            return [(V0, (c, r), update0(c, r, j % 2))]

        loop(lo, hi, body, 4)

    sweep0(0, 4, R0 - 4)
    sweep0(1, 4, R0 - 4)
    sweep0(0, 6, R0 - 6)
    sweep0(1, 6, R0 - 6)

    def defect0(r, j):
        return (D0[0, r] * (update0(0, r, j) - V0[0, r]))[:, :128]

    def right1(yp, j):
        rows = []
        for j in range(2):
            r = HY + 4 * yp + 2 * j
            t = defect0(r, 0) + defect0(r + 1, 1)
            rows.append(0.125 * (t + swap_lanes(t, 1)))
        red, black = split(p1, rows[0], rows[1])
        return [(b1, (8 + yp,), jnp.where(odd, black, red))]

    loop(0, 8, right1, 2)
    for k in range(4):
        first, second = b1[8 + 2 * k], b1[9 + 2 * k]
        zp1[k] = jnp.where(lane < 64, roll(first, 32, 1), roll(second, 96, 1))

    def b1_pieces(dy, dz):
        if dz == 0 and dy < 0:
            return b1.at[pl.ds(8, 6)], b1.at[pl.ds(16, 6)]
        if dz == 0:
            return b1.at[pl.ds(10, 6)], b1.at[pl.ds(2, 6)]
        side = 0 if dz > 0 else 1
        if dy == 0:
            return zp1, zb1.at[side, pl.ds(4, 4)]
        if dy > 0:
            return zp1.at[pl.ds(1, 3)], zb1.at[side, pl.ds(1, 3)]
        return zp1.at[pl.ds(0, 3)], zb1.at[side, pl.ds(8, 3)]

    x_b1 = exchange(X_B1, b1_pieces)

    pl.semaphore_wait(known.at[1], 2)
    gather(msg_k, GK, 0, row_k)
    received(x_k)

    def joined(ref, yb, r):
        a = ref[yb, 1, r]
        b = jnp.where(lane < 64, ref[yb, 2, r], ref[yb, 0, r])
        return cat(a, b)

    def apart(x):
        a, b = x[:, :128], x[:, 128:]
        red = cat(jnp.where(odd, roll(a, 1, 1), a), jnp.where(odd, roll(b, 1, 1), b))
        black = cat(jnp.where(odd, a, roll(a, -1, 1)), jnp.where(odd, b, roll(b, -1, 1)))
        return red, black

    for yb in range(3):
        row_ok = (up_in, True, down_in)[yb]
        ok = ring_in & row_ok

        def spread1(r, carry, yb=yb, ok=ok):
            red, black = apart(joined(KX, yb, r))
            K1[0, 8 * yb + r] = jnp.where(ok, red, 0.0)
            K1[1, 8 * yb + r] = jnp.where(ok, black, 0.0)
            return carry

        lax.fori_loop(0, 8, spread1, 0)
        for r in range(4):
            red, black = apart(joined(KX, yb, 8 + r))
            K2[0, 1 + 4 * yb + r] = jnp.where(ok, red, 0.0)
            K2[1, 1 + 4 * yb + r] = jnp.where(ok, black, 0.0)

    def near_y(level, ref, c, r):
        dx, dz = (1, 2) if level == 1 else (2, 4)
        p = parity_y(level, lane2, sub2)
        o, low, high = ref[1 - c, r], ref[1 - c, r - 1], ref[1 - c, r + 1]
        outer = jnp.where(p, high, low) if c == 0 else jnp.where(p, low, high)
        ahead, behind = ring(o, dz)
        return (o, outer, roll(o, -dx, 0), roll(o, dx, 0), ahead, behind)

    def faces_y(level, K, G, I, D, r):
        dx = 1 if level == 1 else 2
        s = 0.25**level
        stores = []
        for c in range(2):
            k = K[c, r]
            near = list(near_y(level, K, c, r))
            last, first = sub2 >= 8 - dx, sub2 < dx
            near[2] = jnp.where(last, 0.0, near[2])
            near[3] = jnp.where(first, 0.0, near[3])
            f = [0.5 * (k + value) for value in near]
            d = ((f[0] + f[1]) + (f[2] + f[3])) + (f[4] + f[5])
            inv = jnp.where(k > 0.0, 1.0 / d, 0.0)
            for n in range(6):
                g = f[n] * inv
                if n == 2:
                    g = jnp.where(last, 0.0, g)
                if n == 3:
                    g = jnp.where(first, 0.0, g)
                stores.append((G, (c, r, n), g))
            stores.append((I, (c, r), inv * (1.0 / s)))
            if c == 0:
                stores.append((D, (r,), s * d))
        return stores

    loop(2, R1 - 2, lambda r, j: faces_y(1, K1, G1, I1, D1, r))
    loop(1, R2 - 1, lambda r, j: faces_y(2, K2, G2, I2, D2, r))

    received(x_b1)

    def v0_pieces(dy, dz):
        def at(r, n):
            return V0.at[1, pl.ds(r, n), :, pl.ds(0, 128)]

        lo, n, to = {-1: (HY, 5, HY + NY), 0: (HY, NY, HY), 1: (HY + NY - 5, 5, HY - 5)}[dy]
        if dz == 0:
            return at(lo, n), at(to, n)
        return at(lo, n), zv.at[0 if dz > 0 else 1, pl.ds(to, n)]

    def spread_b(k, j):
        stores = []
        merged = jnp.where(lane % 64 < 32, zb1[0, k], zb1[1, k])
        for q in range(2):
            r = 2 * k + q
            red, black = apart(cat(b1[r], roll(merged, -64 * q - 32, 1)))
            stores.append((BD1, (0, r), jnp.where(I1[0, r] > 0.0, red, 0.0) * I1[0, r]))
            stores.append((BD1, (1, r), jnp.where(I1[1, r] > 0.0, black, 0.0) * I1[1, r]))
            stores.append((V1, (0, r), stores[-2][2]))
        return stores

    loop(1, 11, spread_b, 2)

    def update_y(level, V, G, BD, c, r):
        near = near_y(level, V, c, r)
        t = [G[c, r, n] * near[n] for n in range(6)]
        return BD[c, r] + (((t[0] + t[1]) + (t[2] + t[3])) + (t[4] + t[5]))

    def sweep_y(level, V, G, BD, c, lo, hi):
        def body(r, j):
            return [(V, (c, r), update_y(level, V, G, BD, c, r))]

        loop(lo, hi, body, 4)

    sweep_y(1, V1, G1, BD1, 1, 2, 22)
    sweep_y(1, V1, G1, BD1, 0, 2, 22)
    sweep_y(1, V1, G1, BD1, 1, 2, 22)

    p2w = parity_y(2, lane2, sub2)

    def right2(i, j):
        rows = []
        for j in range(2):
            r = 4 + 2 * i + j
            t = D1[r] * (update_y(1, V1, G1, BD1, 0, r) - V1[0, r])
            t = t + swap_subs(t, 1)
            a, b = t[:, :128], t[:, 128:]
            rows.append(0.125 * cat(a + swap_lanes(a, 2), b + swap_lanes(b, 2)))
        red, black = split(p2w, rows[0], rows[1])
        row = 3 + i
        first = red * I2[0, row]
        return [
            (BD2, (0, row), first),
            (V2, (0, row), first),
            (BD2, (1, row), black * I2[1, row]),
            (pair2, (i,), jnp.where(odd, black[:, :128], red[:, :128])),
        ]

    V2[0, 2] = zero_row
    V2[0, 11] = zero_row
    V2[1, 2] = zero_row
    V2[1, 11] = zero_row
    loop(0, 8, right2, 2)

    sweep_y(2, V2, G2, BD2, 1, 3, 11)
    sweep_y(2, V2, G2, BD2, 0, 3, 11)
    sweep_y(2, V2, G2, BD2, 1, 3, 11)
    rows = []
    for y in range(4):
        r = 5 + y
        t = (D2[r] * (update_y(2, V2, G2, BD2, 0, r) - V2[0, r]))[:, :128]
        t = t + swap_subs(t, 2)
        rows.append(0.125 * (t + swap_lanes(t, 4)))
    gather(msg_b, GB, 1, message(rows))

    for y in range(4):
        CX[1, 1, y] = jnp.where(lane % 4 < 2, pair2[2 + y], V2[1, 5 + y, :, :128])
    x_b2 = exchange(X_B2, block_pieces(CX))
    x_v0 = exchange(X_V0, v0_pieces)

    def new_ice(r, j):
        both = jnp.concatenate([und[0, r, :, :128], und[1, r, :, :128]], axis=0)
        return [(outb, (r - HY,), both.astype(BF16))]

    loop(HY, HY + NY, new_ice, 4)
    copy = pltpu.make_async_copy(outb, ice_o, osem.at[4])
    copy.start()
    stores_out = [copy]
    all_bytes(GK, gr.at[0])
    k3r, k3b = global_level3(GK)
    row3 = lax.broadcasted_iota(jnp.int32, (64, 128), 0)
    lane3 = lax.broadcasted_iota(jnp.int32, (64, 128), 1)
    odd3 = (row3 + lane3) % 2 == 1
    edges3 = (row3 == 0, row3 == 63, lane3 == 0, lane3 == 127)

    def near3(o):
        return (roll(o, 1, 0), roll(o, -1, 0), roll(o, 1, 1), roll(o, -1, 1), o)

    def faces3(c, k, o):
        s = 0.25**3
        near = [jnp.where(e, 0.0, v) for e, v in zip(edges3, near3(o))] + [o]
        f = [0.5 * (k + value) for value in near] + [0.5 * k]
        d = ((f[0] + f[1]) + (f[2] + f[3])) + (f[4] + f[5])
        inv = 1.0 / d
        for n in range(5):
            g = f[n] * inv
            G3[c, n] = jnp.where(edges3[n], 0.0, g) if n < 4 else g
        I3[c] = inv * (1.0 / s)
        if c == 0:
            D3[...] = s * d

    faces3(0, k3r, k3b)
    faces3(1, k3b, k3r)

    lane4 = lax.broadcasted_iota(jnp.int32, (16, 128), 1)
    row4 = lax.broadcasted_iota(jnp.int32, (16, 128), 0)
    p4 = (lane4 // 2) % 2 == 1

    def level4_of(total):
        t = total + swap_subs(total, 1)
        buf4[...] = 0.125 * (t + swap_lanes(t, 1))
        low, high = buf4[pl.ds(0, 16, stride=4), :], buf4[pl.ds(2, 16, stride=4), :]
        return split(p4, low, high)

    k4 = level4_of(k3r + k3b)

    def near4(c, o):
        low, high = roll(o, 1, 0), roll(o, -1, 0)
        outer = jnp.where(p4, high, low) if c == 0 else jnp.where(p4, low, high)
        return (o, outer, roll(o, -2, 1), roll(o, 2, 1))

    def faces4(c):
        s = 0.25**4
        k = k4[c]
        take = p4 if c == 0 else jnp.logical_not(p4)
        edges = (None, jnp.where(take, row4, 15 - row4) == 15, lane4 >= 126, lane4 < 2)
        near = near4(c, k4[1 - c])
        near = [v if e is None else jnp.where(e, 0.0, v) for e, v in zip(edges, near)]
        f = [0.5 * (k + value) for value in near]
        d = ((f[0] + f[1]) + (f[2] + f[3])) + k
        inv = 1.0 / d
        g = [v * inv if e is None else jnp.where(e, 0.0, v * inv) for e, v in zip(edges, f)]
        return g, inv * (1.0 / s)

    g4r, i4r = faces4(0)
    g4b, i4b = faces4(1)

    received(x_b2)
    for yb in range(3):
        row_ok = (up_in, True, down_in)[yb]
        for r in range(4):
            x = joined(CX, yb, r)
            row = 1 + 4 * yb + r

            def fill(x):
                a, b = x[:, :128], x[:, 128:]
                first = cat(jnp.where(odd, roll(a, 1, 1), a), jnp.where(odd, roll(b, 1, 1), b))
                second = cat(jnp.where(odd, a, roll(a, -1, 1)), jnp.where(odd, b, roll(b, -1, 1)))
                return first, second

            first, second = fill(x)
            head = lane2 % 4 < 2

            def pair_up(y):
                return cat(roll(y[:, :128], 2, 1), roll(y[:, 128:], 2, 1))

            def pair_down(y):
                return cat(roll(y[:, :128], -2, 1), roll(y[:, 128:], -2, 1))

            BD2[0, row] = jnp.where(head, first, pair_up(first)) * I2[0, row]
            BD2[1, row] = jnp.where(head, second, pair_up(second)) * I2[1, row]
            V2[1, row] = jnp.where(ring_in & row_ok, jnp.where(head, pair_down(x), x), 0.0)

    received(x_v0)
    for copy in x_v0:
        copy.wait_send()

    def v0_sides(r, j):
        ok = ((r >= HY) | up_in) & ((r < HY + NY) | down_in)
        side = jnp.where(
            ok & (((lane < 5) & right_in) | ((lane >= 123) & left_in)), jnp.where(lane < 64, zv[1, r], zv[0, r]), 0.0
        )
        return [(V0, (1, r), cat(jnp.where(ok, V0[1, r, :, :128], 0.0), side))]

    loop(HY - 5, HY + NY + 5, v0_sides, 3)
    zrow = lax.broadcasted_iota(jnp.int32, (128, 256), 0)
    zcol = lax.broadcasted_iota(jnp.int32, (128, 256), 1)
    expand = (zrow == gz * 16 + zcol // 8 - jnp.where(zcol >= 192, 32, 0)).astype(F32)

    all_bytes(GB, gr.at[1])
    b3r, b3b = global_level3(GB)
    bd3 = (b3r * I3[0], b3b * I3[1])

    def update3(c, o):
        near = near3(o)
        t = [G3[c, n] * near[n] for n in range(5)]
        return bd3[c] + (((t[0] + t[1]) + (t[2] + t[3])) + t[4])

    v_r = bd3[0]
    v_b = update3(1, v_r)
    v_r = update3(0, v_b)
    v_b = update3(1, v_r)
    r3 = D3[...] * (update3(0, v_b) - v_r)
    b4 = level4_of(r3)
    bd4r, bd4b = b4[0] * i4r, b4[1] * i4b

    def update4(c, g, bd, o):
        near = near4(c, o)
        return bd + ((g[0] * near[0] + g[1] * near[1]) + (g[2] * near[2] + g[3] * near[3]))

    def sweep4(i, carry):
        red, black = carry
        red = update4(0, g4r, bd4r, black)
        black = update4(1, g4b, bd4b, red)
        return red, black

    zero4 = jnp.zeros((16, 128), F32)
    e_r, e_b = lax.fori_loop(0, COARSE_SWEEPS, sweep4, (zero4, zero4))
    low, high = split(p4, e_r, e_b)
    buf4[pl.ds(0, 16, stride=4), :] = low
    buf4[pl.ds(1, 16, stride=4), :] = low
    buf4[pl.ds(2, 16, stride=4), :] = high
    buf4[pl.ds(3, 16, stride=4), :] = high
    v_b = v_b + buf4[...]
    v_r = update3(0, v_b)
    v_b = update3(1, v_r)
    v_r = update3(0, v_b)
    v_b = update3(1, v_r)

    x_low, x_high = split(odd3, v_r, v_b)
    e3x[0, pl.ds(8, 64), :] = x_low
    e3x[1, pl.ds(8, 64), :] = x_high
    parts = []
    for n in range(2):
        for i in range(12):
            parts.append(e3x[n, pl.ds(gy * 4 + (4 + i), 1), :])
    wide = dot(jnp.concatenate(parts, axis=0), expand)
    for i in range(12):
        e = jnp.where(sub2 < 4, wide[i : i + 1], wide[12 + i : 13 + i])
        row_ok = up_in if i < 4 else (down_in if i >= 8 else True)
        V2[1, 1 + i] = V2[1, 1 + i] + jnp.where(ring_in & row_ok, e, 0.0)
    sweep_y(2, V2, G2, BD2, 0, 1, 13)
    sweep_y(2, V2, G2, BD2, 1, 1, 13)
    sweep_y(2, V2, G2, BD2, 0, 1, 13)
    sweep_y(2, V2, G2, BD2, 1, 3, 11)

    p1w = parity_y(1, lane2, sub2)

    def correct1(i, j):
        low, high = split(p2w, V2[0, 3 + i], V2[1, 3 + i])
        return [(V1, (1, 4 + 2 * i + n), V1[1, 4 + 2 * i + n] + e) for n, e in ((0, low), (1, high))]

    loop(0, 8, correct1, 4)
    sweep_y(1, V1, G1, BD1, 0, 4, 20)
    sweep_y(1, V1, G1, BD1, 1, 4, 20)
    sweep_y(1, V1, G1, BD1, 0, 4, 20)
    sweep_y(1, V1, G1, BD1, 1, 6, 18)

    def correct0(i, j):
        low, high = split(p1w, V1[0, 6 + i], V1[1, 6 + i])
        return [
            (V0, (1, 4 * i + n), V0[1, 4 * i + n] + e) for n, e in ((0, low), (1, low), (2, high), (3, high))
        ]

    loop(0, 12, correct0, 2)
    sweep0(0, 4, R0 - 4)
    sweep0(1, 4, R0 - 4)
    sweep0(0, 6, R0 - 6)
    sweep0(1, 6, R0 - 6)

    def results(r, j):
        stores = []
        for c in range(2):
            v = V0[c, r]
            res = D0[c, r] * (update0(c, r, j % 2) - v)
            stores.append((outf, (r - HY, c), v[:, :128]))
            stores.append((outf, (r - HY, 2 + c), res[:, :128]))
        return stores

    for k in range(4):
        lo = 8 * k
        loop(HY + lo, HY + lo + 8, results, 4)
        copy = pltpu.make_async_copy(outf.at[pl.ds(lo, 8)], fin_o.at[pl.ds(lo, 8)], osem.at[k])
        copy.start()
        stores_out.append(copy)

    for copies in (x_in, x_f, x_k, x_b1, x_b2):
        for copy in copies:
            copy.wait_send()
    all_bytes(GK, gs.at[0])
    all_bytes(GB, gs.at[1])
    for copy in stores_out:
        copy.wait()


def unpair(ice, fin, phase_o, pres_o, res_o, tmp):
    odd = lax.broadcasted_iota(jnp.int32, (8, 128), 1) % 2 == 1

    def row(y, j):
        par = odd if j % 2 == 0 else jnp.logical_not(odd)
        both = ice[y].astype(F32)
        stores = []
        for ref, red, black in (
            (tmp, both[:8], both[8:]),
            (pres_o, fin[y, 0], fin[y, 1]),
            (res_o, fin[y, 2], fin[y, 3]),
        ):
            stores.append((ref, (pl.ds(y, 8, stride=2 * NY), slice(None)), jnp.where(par, black, red)))
            stores.append((ref, (pl.ds(NY + y, 8, stride=2 * NY), slice(None)), jnp.where(par, red, black)))
        return stores

    loop(0, NY, row, 4)
    phase_o[...] = tmp[...].astype(BF16)


def per_device(GY, GZ, phase, undercool, perm_base, source, pressure):
    def vm(*shape):
        return pltpu.VMEM(shape, F32)

    scratch = [
        pltpu.VMEM((3, NX * NY, NZ), BF16),
        vm(5, NX * NY, NZ),
        pltpu.VMEM((NY, 16, 128), BF16),
        vm(NY, 4, 8, 128),
        pltpu.VMEM((R0, 48, 128), BF16),
        vm(R0, 24, 128),
        pltpu.VMEM((4, 48, 128), BF16),
        vm(4, 24, 128),
        pltpu.VMEM((2, 6, 48, 128), BF16),
        vm(2, 6, 24, 128),
        vm(2, R0, 8, 256),
        vm(2, R0, 8, 256),
        vm(2, R0, 8, 256),
        vm(2, R0, 8, 256),
        vm(2, R0, 8, 256),
        vm(2, R0, 8, 256),
        vm(2, R0, 6, 8, 256),
        vm(2, R0, 8, 256),
        vm(2, R0, 8, 256),
        vm(2, R0, 8, 128),
        vm(3, 3, 12, 8, 128),
        vm(3, 3, 4, 8, 128),
        vm(2, R1, 8, 256),
        vm(2, R1, 8, 256),
        vm(2, R1, 6, 8, 256),
        vm(2, R1, 8, 256),
        vm(2, R1, 8, 256),
        vm(R1, 8, 256),
        vm(2, R2, 8, 256),
        vm(2, R2, 8, 256),
        vm(2, R2, 6, 8, 256),
        vm(2, R2, 8, 256),
        vm(2, R2, 8, 256),
        vm(R2, 8, 256),
        vm(R1, 8, 128),
        vm(4, 8, 128),
        vm(2, 12, 8, 128),
        vm(1, 1, 128),
        vm(1, 1, 128),
        vm(GY * GZ, 1, 128),
        vm(GY * GZ, 1, 128),
        vm(2, 64, 128),
        vm(2, 5, 64, 128),
        vm(2, 64, 128),
        vm(64, 128),
        vm(64, 128),
        vm(2, 80, 128),
        vm(8, 8, 128),
        pltpu.SemaphoreType.DMA((N_X, 8)),
        pltpu.SemaphoreType.DMA((N_X, 8)),
        pltpu.SemaphoreType.DMA((2,)),
        pltpu.SemaphoreType.DMA((2,)),
        pltpu.SemaphoreType.DMA((5,)),
        pltpu.SemaphoreType.DMA((5,)),
        pltpu.SemaphoreType.REGULAR((2,)),
    ]
    hbm = pl.BlockSpec(memory_space=pltpu.HBM)
    vmem = pl.BlockSpec(memory_space=pltpu.VMEM)
    flat = (NX * NY, NZ)
    packed_ice, packed = pl.pallas_call(
        functools.partial(kernel, GY, GZ),
        out_shape=(jax.ShapeDtypeStruct((NY, 16, NZ), BF16), jax.ShapeDtypeStruct((NY, 4, 8, NZ), F32)),
        in_specs=[hbm] * 5,
        out_specs=(hbm, hbm),
        scratch_shapes=scratch,
        compiler_params=pltpu.CompilerParams(
            collective_id=0, has_side_effects=True, vmem_limit_bytes=63 * 2**20
        ),
    )(*[a.reshape(flat) for a in (phase, undercool, perm_base, source, pressure)])
    outs = pl.pallas_call(
        unpair,
        out_shape=(
            jax.ShapeDtypeStruct(flat, BF16),
            jax.ShapeDtypeStruct(flat, F32),
            jax.ShapeDtypeStruct(flat, F32),
        ),
        in_specs=[vmem] * 2,
        out_specs=(vmem, vmem, vmem),
        scratch_shapes=[vm(NX * NY, NZ)],
        compiler_params=pltpu.CompilerParams(vmem_limit_bytes=63 * 2**20),
    )(packed_ice, packed)
    return tuple(a.reshape(NX, NY, NZ) for a in outs)


def solution(mesh):
    spec = P(None, "gy", "gz")
    return jax.shard_map(
        functools.partial(per_device, mesh.shape["gy"], mesh.shape["gz"]),
        mesh=mesh,
        in_specs=(spec,) * 5,
        out_specs=(spec,) * 3,
        check_vma=False,
    )
```

```python
import functools
import jax
import jax.numpy as jnp
from jax import lax
from jax.experimental import pallas as pl
from jax.experimental.pallas import tpu as pltpu
from jax.sharding import PartitionSpec as P

MESH = pl.DeviceIdType.MESH
F32 = jnp.float32
BF16 = jnp.bfloat16
COARSE_SWEEPS = 20
NX, NY, NZ = 16, 32, 128
HY = 8
R0 = NY + 2 * HY
R1 = 24
R2 = 14
NEAR = [(dy, dz) for dy in (-1, 0, 1) for dz in (-1, 0, 1) if (dy, dz) != (0, 0)]
X_IN, X_F, X_K, X_B1, X_V0, X_B2 = range(6)
N_X = 6


def roll(x, shift, axis):
    size = x.shape[axis]
    shift = shift % size
    return x if shift == 0 else pltpu.roll(x, shift, axis)


def loop(lo, hi, body, step=2):
    def trip(i, carry):
        stores = []
        for j in range(step):
            stores.extend(body(lo + i * step + j, j))
        for ref, index, value in stores:
            ref[index] = value
        return carry

    trips = (hi - lo) // step
    assert trips * step == hi - lo
    if trips == 1:
        trip(0, 0)
    else:
        lax.fori_loop(0, trips, trip, 0)


def kernel(
    GY, GZ, phase_h, under_h, perm_h, src_h, pres_h, ice_o, fin_o,
    inb, tmp, outb, outf,
    ha, hf, zp, zpf, zb, zbf,
    ice, und, prm, S0, V0, K0, G0, BD0, D0, zv,
    KX, CX, K1, V1, G1, I1, BD1, D1, K2, V2, G2, I2, BD2, D2,
    b1, zp1, zb1, msg_k, msg_b, GK, GB, K3, G3, I3, D3, buf4, e3x, pair2,
    ssem, rsem, gs, gr, lsem, osem, known,
):
    gy, gz = lax.axis_index("gy"), lax.axis_index("gz")
    me = gy * GZ + gz

    def peer(dy, dz):
        return (lax.rem(gy + dy + GY, GY), lax.rem(gz + dz + GZ, GZ))

    barrier = pltpu.get_barrier_semaphore()

    for dy, dz in NEAR:
        pl.semaphore_signal(barrier, inc=1, device_id=peer(dy, dz), device_id_type=MESH)

    loads = []
    for n, (src, dst) in enumerate(
        ((phase_h, inb.at[0]), (under_h, inb.at[1]), (perm_h, inb.at[2]), (src_h, tmp.at[3]), (pres_h, tmp.at[4]))
    ):
        copy = pltpu.make_async_copy(src, dst, lsem.at[n])
        copy.start()
        loads.append(copy)

    lane = lax.broadcasted_iota(jnp.int32, (8, 128), 1)
    sub = lax.broadcasted_iota(jnp.int32, (8, 128), 0)
    lane2 = lax.broadcasted_iota(jnp.int32, (8, 256), 1)
    sub2 = lax.broadcasted_iota(jnp.int32, (8, 256), 0)
    odd = lane % 2 == 1
    odd2 = lane2 % 2 == 1
    right_in, left_in = gz < GZ - 1, gz > 0
    up_in, down_in = gy > 0, gy < GY - 1
    ring_in = (lane2 < 128) | ((lane2 < 192) & right_in) | ((lane2 >= 192) & left_in)

    def cat(a, b):
        return jnp.concatenate([a, b], axis=-1)

    def ring(o, d):
        a, b = o[:, :128], o[:, 128:]
        fa, fb = roll(a, -d, 1), roll(b, -d, 1)
        ba, bb = roll(a, d, 1), roll(b, d, 1)
        end, start = lane >= 128 - d, lane < d
        ahead = cat(jnp.where(end, fb, fa), jnp.where(end, fa, fb))
        behind = cat(jnp.where(start, bb, ba), jnp.where(start, ba, bb))
        return ahead, behind

    for copy in loads:
        copy.wait()
    for n in range(3):
        tmp[n] = inb[n].astype(F32)

    def red_black_of(n, y, j):
        even = tmp[n, pl.ds(y, 8, stride=2 * NY), :]
        odds = tmp[n, pl.ds(NY + y, 8, stride=2 * NY), :]
        par = odd if j % 2 == 0 else jnp.logical_not(odd)
        return jnp.where(par, odds, even), jnp.where(par, even, odds)

    zp[...] = jnp.zeros_like(zp)
    zpf[...] = jnp.zeros_like(zpf)

    def prepare(k, carry):
        packed = jnp.zeros((48, 128), F32)
        packed_f = jnp.zeros((24, 128), F32)
        group = lax.broadcasted_iota(jnp.int32, (48, 128), 1) // 16
        for q in range(8):
            y = 8 * k + q
            parts = []
            for n in range(3):
                parts.extend(red_black_of(n, y, q))
            row = jnp.concatenate(parts, axis=0)
            ha[HY + y] = row.astype(BF16)
            s_r, s_b = red_black_of(3, y, q)
            _, v_b = red_black_of(4, y, q)
            row_f = jnp.concatenate([s_r, s_b, v_b], axis=0)
            hf[HY + y] = row_f
            packed = jnp.where(group == q, roll(row, 16 * q + 8, 1), packed)
            packed_f = jnp.where(group[:24] == q, roll(row_f, 16 * q + 8, 1), packed_f)
        zp[k] = packed.astype(BF16)
        zpf[k] = packed_f
        return carry

    lax.fori_loop(0, 4, prepare, 0)

    pl.semaphore_wait(barrier, len(NEAR))

    def exchange(ex, pieces):
        copies = []
        for n, (dy, dz) in enumerate(NEAR):
            src, dst = pieces(dy, dz)
            copy = pltpu.make_async_remote_copy(
                src, dst, ssem.at[ex, n], rsem.at[ex, n], device_id=peer(dy, dz), device_id_type=MESH
            )
            copy.start()
            copies.append(copy)
        return copies

    def received(copies):
        for copy in copies:
            copy.wait_recv()

    def input_pieces(rows, packed, landing, width):
        def pieces(dy, dz):
            if dz == 0 and dy < 0:
                return rows.at[pl.ds(HY, width)], rows.at[pl.ds(HY + NY, width)]
            if dz == 0:
                return rows.at[pl.ds(HY + NY - width, width)], rows.at[pl.ds(HY - width, width)]
            side = 0 if dz > 0 else 1
            if dy == 0:
                return packed, landing.at[side, pl.ds(1, 4)]
            if dy > 0:
                return packed.at[pl.ds(3, 1)], landing.at[side, pl.ds(0, 1)]
            return packed.at[pl.ds(0, 1)], landing.at[side, pl.ds(5, 1)]

        return pieces

    x_in = exchange(X_IN, input_pieces(ha, zp, zb, 6))
    x_f = exchange(X_F, input_pieces(hf, zpf, zbf, 5))

    zero_row = jnp.zeros((8, 256), F32)
    e3x[...] = jnp.zeros_like(e3x)
    for c in range(2):
        for r in (0, R2 - 1):
            K2[c, r] = zero_row
            V2[c, r] = zero_row
        for r in (0, 1, R1 - 2, R1 - 1):
            V1[c, r] = zero_row
        for r in (3, R0 - 4):
            V0[c, r] = zero_row

    received(x_in)
    received(x_f)
    for dy, dz in NEAR:
        pl.semaphore_signal(known.at[0], inc=1, device_id=peer(2 * dy, 2 * dz), device_id_type=MESH)

    def row_mask(r, width):
        ok = ((r >= HY) | up_in) & ((r < HY + NY) | down_in)
        lanes = (lane2 < 128) | ((lane2 < 128 + width) & right_in) | ((lane2 >= 256 - width) & left_in)
        return lanes & ok

    def unpack(k, carry):
        group = lax.broadcasted_iota(jnp.int32, (48, 128), 1) % 16 < 8
        merged = jnp.where(group, zb[0, k].astype(F32), zb[1, k].astype(F32))
        merged_f = jnp.where(group[:24], zbf[0, k], zbf[1, k])
        for q in range(8):
            r = 8 * k + q
            ok = row_mask(r, 6) & (r >= 2) & (r < R0 - 2)
            ok5 = row_mask(r, 5) & (r >= 3) & (r < R0 - 3)
            side = roll(merged, 120 - 16 * q, 1)
            side_f = roll(merged_f, 120 - 16 * q, 1)
            a = ha[r].astype(F32)
            f = hf[r]
            for c in range(2):
                s = slice(8 * c, 8 * c + 8)
                ice[c, r] = jnp.where(ok, cat(a[s], side[s]), 0.0)
                s = slice(16 + 8 * c, 24 + 8 * c)
                und[c, r] = cat(a[s], side[s])
                s = slice(32 + 8 * c, 40 + 8 * c)
                prm[c, r] = jnp.where(ok5, cat(a[s], side[s]), 0.0)
                s = slice(8 * c, 8 * c + 8)
                S0[c, r] = cat(f[s], side_f[s])
            V0[1, r] = jnp.where(ok5, cat(f[16:24], side_f[16:24]), 0.0)
        return carry

    lax.fori_loop(0, 6, unpack, 0)

    def pick(c, j):
        return odd2 if (c + j) % 2 == 0 else jnp.logical_not(odd2)

    def x_outer(o, take):
        return jnp.where(take, roll(o, -1, 0), roll(o, 1, 0))

    def x_edge(take):
        return jnp.where(take, sub2, 7 - sub2) == 7

    def near0(ref, c, r, j):
        o = ref[1 - c, r]
        take = pick(c, j)
        ahead, behind = ring(o, 1)
        return (ref[1 - c, r - 1], ref[1 - c, r + 1], o, x_outer(o, take), ahead, behind)

    def permeability(r, j):
        j = j % 2
        stores = []
        for c in range(2):
            now = ice[c, r]
            near = list(near0(ice, c, r, j))
            near[3] = jnp.where(x_edge(pick(c, j)), 0.0, near[3])
            lap = near[0]
            for value in near[1:]:
                lap = lap + value
            lap = lap - 6.0 * now
            well = 2.0 * now * (1.0 - now) * (1.0 - 2.0 * now)
            drive = 30.0 * now * now * (1.0 - now) * (1.0 - now) * und[c, r]
            new = jnp.clip(now + 0.12 * lap - 0.5 * well + 0.25 * drive, 0.0, 1.0)
            stores.append((K0, (c, r), jnp.where(prm[c, r] > 0.0, prm[c, r] * jnp.exp(-1.5 * new), 0.0)))
            stores.append((und, (c, r), new))
        return stores

    loop(2, R0 - 2, permeability, 4)

    def swap_lanes(x, d):
        return jnp.where((lax.broadcasted_iota(jnp.int32, x.shape, 1) // d) % 2 == 0, roll(x, -d, 1), roll(x, d, 1))

    def swap_subs(x, d):
        return jnp.where((lax.broadcasted_iota(jnp.int32, x.shape, 0) // d) % 2 == 0, roll(x, -d, 0), roll(x, d, 0))

    def parity_y(level, ln, sb):
        return (sb // (1 if level == 1 else 2) + ln // (2 if level == 1 else 4)) % 2 == 1

    def own0(c, r):
        return K0[c, r, :, :128]

    def coarse0(y):
        r = HY + 2 * y
        t = (own0(0, r) + own0(1, r)) + (own0(0, r + 1) + own0(1, r + 1))
        return 0.125 * (t + swap_lanes(t, 1))

    p1, p2 = parity_y(1, lane, sub), parity_y(2, lane, sub)

    def split(p, low, high):
        return jnp.where(p, high, low), jnp.where(p, low, high)

    k2_rows = []
    for yp in range(8):
        red, black = split(p1, coarse0(2 * yp), coarse0(2 * yp + 1))
        KX[1, 1, yp] = jnp.where(odd, black, red)
        t = red + black
        t = t + swap_subs(t, 1)
        k2_rows.append(0.125 * (t + swap_lanes(t, 2)))
    k3_rows = []
    for yp in range(4):
        red, black = split(p2, k2_rows[2 * yp], k2_rows[2 * yp + 1])
        KX[1, 1, 8 + yp] = jnp.where(odd, black, red)
        t = red + black
        t = t + swap_subs(t, 2)
        k3_rows.append(0.125 * (t + swap_lanes(t, 4)))

    def block_pieces(ref):
        return lambda dy, dz: (ref.at[1, 1], ref.at[1 - dy, 1 - dz])

    x_k = exchange(X_K, block_pieces(KX))

    squeeze = (
        lax.broadcasted_iota(jnp.int32, (128, 128), 0) == 8 * (lax.broadcasted_iota(jnp.int32, (128, 128), 1) % 16)
    ).astype(F32)

    def dot(a, b):
        return lax.dot_general(
            a, b, (((1,), (0,)), ((), ())), precision=lax.Precision.HIGHEST, preferred_element_type=F32
        )

    def message(rows):
        piece = jnp.zeros((8, 128), F32)
        for y in range(4):
            u = rows[y]
            t = jnp.where((y + lane // 8) % 2 == 0, u, roll(u, 4, 0))
            piece = jnp.where(sub % 4 == y, t, piece)
        wide = dot(piece, squeeze)
        return jnp.sum(jnp.where(lane // 16 == sub, wide, 0.0), axis=0, keepdims=True)

    def gather(msg, landing, n, row):
        msg[0] = row
        landing[pl.ds(me, 1)] = row.reshape(1, 1, 128)

        def start(y, z):
            pltpu.make_async_remote_copy(
                msg, landing.at[pl.ds(me, 1)], gs.at[n], gr.at[n], device_id=(y, z), device_id_type=MESH
            ).start()

        columns = [lax.rem(gz + i, GZ) for i in (4, 3, 5, 2, 6, 1, 7, 0)]

        def send(i, carry):
            y = lax.rem(gy + i, GY)
            for z in columns:
                start(y, z)
            return carry

        lax.fori_loop(1, GY, send, 0)
        for z in columns[:-1]:
            start(gy, z)

    def all_bytes(landing, sem):
        part = landing.at[pl.ds(0, GY * GZ - 1)]
        pltpu.make_async_copy(part, part, sem).wait()

    def global_level3(landing):
        x = landing[...].reshape(GY, GZ, 128)
        ln = lax.broadcasted_iota(jnp.int32, x.shape, 2)
        sb = lax.broadcasted_iota(jnp.int32, x.shape, 1)
        for bit in (1, 2, 4):
            s_set, t_set = (sb // bit) % 2 == 1, (ln // (16 * bit)) % 2 == 1
            down = roll(roll(x, bit, 1), -16 * bit, 2)
            up = roll(roll(x, -bit, 1), 16 * bit, 2)
            x = jnp.where(s_set == t_set, x, jnp.where(s_set, down, up))
        pairs = x.reshape(GY // 2, 2, 8, 128)
        even, odds = pairs[:, 0], pairs[:, 1]
        low = lax.broadcasted_iota(jnp.int32, even.shape, 1) < 4
        red = jnp.where(low, even, roll(odds, 4, 1))
        black = jnp.where(low, roll(even, 4, 1), odds)
        return red.reshape(64, 128), black.reshape(64, 128)

    row_k = message(k3_rows)

    pl.semaphore_wait(known.at[0], len(NEAR))
    for dy in (-4, 4):
        pl.semaphore_signal(known.at[1], inc=1, device_id=peer(dy, 0), device_id_type=MESH)

    def faces0(r, j):
        j = j % 2
        stores = []
        ok = row_mask(r, 5)
        for c in range(2):
            k = K0[c, r]
            take = pick(c, j)
            edge = x_edge(take)
            near = list(near0(K0, c, r, j))
            near[3] = jnp.where(edge, 0.0, near[3])
            f = [0.5 * (k + value) for value in near]
            d = ((f[0] + f[1]) + (f[2] + f[3])) + (f[4] + f[5])
            inv = jnp.where(ok, 1.0 / d, 0.0)
            for n in range(6):
                g = f[n] * inv
                stores.append((G0, (c, r, n), jnp.where(edge, 0.0, g) if n == 3 else g))
            stores.append((BD0, (c, r), jnp.where(ok, S0[c, r], 0.0) * inv))
            stores.append((D0, (c, r), d))
        return stores

    loop(4, R0 - 4, faces0, 4)

    def update0(c, r, j):
        near = near0(V0, c, r, j)
        t = [G0[c, r, n] * near[n] for n in range(6)]
        return BD0[c, r] + (((t[0] + t[1]) + (t[2] + t[3])) + (t[4] + t[5]))

    def sweep0(c, lo, hi):
        def body(r, j):
            return [(V0, (c, r), update0(c, r, j % 2))]

        loop(lo, hi, body, 10 if hi - lo == 40 else 12)

    sweep0(0, 4, R0 - 4)
    sweep0(1, 4, R0 - 4)
    sweep0(0, 6, R0 - 6)
    sweep0(1, 6, R0 - 6)

    def defect0(r, j):
        return (D0[0, r] * (update0(0, r, j) - V0[0, r]))[:, :128]

    def right1(yp, j):
        rows = []
        for j in range(2):
            r = HY + 4 * yp + 2 * j
            t = defect0(r, 0) + defect0(r + 1, 1)
            rows.append(0.125 * (t + swap_lanes(t, 1)))
        red, black = split(p1, rows[0], rows[1])
        return [(b1, (8 + yp,), jnp.where(odd, black, red))]

    loop(0, 8, right1, 2)
    for k in range(4):
        first, second = b1[8 + 2 * k], b1[9 + 2 * k]
        zp1[k] = jnp.where(lane < 64, roll(first, 32, 1), roll(second, 96, 1))

    def b1_pieces(dy, dz):
        if dz == 0 and dy < 0:
            return b1.at[pl.ds(8, 6)], b1.at[pl.ds(16, 6)]
        if dz == 0:
            return b1.at[pl.ds(10, 6)], b1.at[pl.ds(2, 6)]
        side = 0 if dz > 0 else 1
        if dy == 0:
            return zp1, zb1.at[side, pl.ds(4, 4)]
        if dy > 0:
            return zp1.at[pl.ds(1, 3)], zb1.at[side, pl.ds(1, 3)]
        return zp1.at[pl.ds(0, 3)], zb1.at[side, pl.ds(8, 3)]

    x_b1 = exchange(X_B1, b1_pieces)

    pl.semaphore_wait(known.at[1], 2)
    gather(msg_k, GK, 0, row_k)
    received(x_k)

    def joined(ref, yb, r):
        a = ref[yb, 1, r]
        b = jnp.where(lane < 64, ref[yb, 2, r], ref[yb, 0, r])
        return cat(a, b)

    def apart(x):
        a, b = x[:, :128], x[:, 128:]
        red = cat(jnp.where(odd, roll(a, 1, 1), a), jnp.where(odd, roll(b, 1, 1), b))
        black = cat(jnp.where(odd, a, roll(a, -1, 1)), jnp.where(odd, b, roll(b, -1, 1)))
        return red, black

    for yb in range(3):
        row_ok = (up_in, True, down_in)[yb]
        ok = ring_in & row_ok

        def spread1(r, carry, yb=yb, ok=ok):
            red, black = apart(joined(KX, yb, r))
            K1[0, 8 * yb + r] = jnp.where(ok, red, 0.0)
            K1[1, 8 * yb + r] = jnp.where(ok, black, 0.0)
            return carry

        lax.fori_loop(0, 8, spread1, 0)
        for r in range(4):
            red, black = apart(joined(KX, yb, 8 + r))
            K2[0, 1 + 4 * yb + r] = jnp.where(ok, red, 0.0)
            K2[1, 1 + 4 * yb + r] = jnp.where(ok, black, 0.0)

    def near_y(level, ref, c, r):
        dx, dz = (1, 2) if level == 1 else (2, 4)
        p = parity_y(level, lane2, sub2)
        o, low, high = ref[1 - c, r], ref[1 - c, r - 1], ref[1 - c, r + 1]
        outer = jnp.where(p, high, low) if c == 0 else jnp.where(p, low, high)
        ahead, behind = ring(o, dz)
        return (o, outer, roll(o, -dx, 0), roll(o, dx, 0), ahead, behind)

    def faces_y(level, K, G, I, D, r):
        dx = 1 if level == 1 else 2
        s = 0.25**level
        stores = []
        for c in range(2):
            k = K[c, r]
            near = list(near_y(level, K, c, r))
            last, first = sub2 >= 8 - dx, sub2 < dx
            near[2] = jnp.where(last, 0.0, near[2])
            near[3] = jnp.where(first, 0.0, near[3])
            f = [0.5 * (k + value) for value in near]
            d = ((f[0] + f[1]) + (f[2] + f[3])) + (f[4] + f[5])
            inv = jnp.where(k > 0.0, 1.0 / d, 0.0)
            for n in range(6):
                g = f[n] * inv
                if n == 2:
                    g = jnp.where(last, 0.0, g)
                if n == 3:
                    g = jnp.where(first, 0.0, g)
                stores.append((G, (c, r, n), g))
            stores.append((I, (c, r), inv * (1.0 / s)))
            if c == 0:
                stores.append((D, (r,), s * d))
        return stores

    loop(2, R1 - 2, lambda r, j: faces_y(1, K1, G1, I1, D1, r))
    loop(1, R2 - 1, lambda r, j: faces_y(2, K2, G2, I2, D2, r))

    received(x_b1)

    def v0_pieces(dy, dz):
        def at(r, n):
            return V0.at[1, pl.ds(r, n), :, pl.ds(0, 128)]

        lo, n, to = {-1: (HY, 5, HY + NY), 0: (HY, NY, HY), 1: (HY + NY - 5, 5, HY - 5)}[dy]
        if dz == 0:
            return at(lo, n), at(to, n)
        return at(lo, n), zv.at[0 if dz > 0 else 1, pl.ds(to, n)]

    def spread_b(k, j):
        stores = []
        merged = jnp.where(lane % 64 < 32, zb1[0, k], zb1[1, k])
        for q in range(2):
            r = 2 * k + q
            red, black = apart(cat(b1[r], roll(merged, -64 * q - 32, 1)))
            stores.append((BD1, (0, r), jnp.where(I1[0, r] > 0.0, red, 0.0) * I1[0, r]))
            stores.append((BD1, (1, r), jnp.where(I1[1, r] > 0.0, black, 0.0) * I1[1, r]))
            stores.append((V1, (0, r), stores[-2][2]))
        return stores

    loop(1, 11, spread_b, 10)

    def update_y(level, V, G, BD, c, r):
        near = near_y(level, V, c, r)
        t = [G[c, r, n] * near[n] for n in range(6)]
        return BD[c, r] + (((t[0] + t[1]) + (t[2] + t[3])) + (t[4] + t[5]))

    def sweep_y(level, V, G, BD, c, lo, hi):
        def body(r, j):
            return [(V, (c, r), update_y(level, V, G, BD, c, r))]

        loop(lo, hi, body, hi - lo)

    sweep_y(1, V1, G1, BD1, 1, 2, 22)
    sweep_y(1, V1, G1, BD1, 0, 2, 22)
    sweep_y(1, V1, G1, BD1, 1, 2, 22)

    p2w = parity_y(2, lane2, sub2)

    def right2(i, j):
        rows = []
        for j in range(2):
            r = 4 + 2 * i + j
            t = D1[r] * (update_y(1, V1, G1, BD1, 0, r) - V1[0, r])
            t = t + swap_subs(t, 1)
            a, b = t[:, :128], t[:, 128:]
            rows.append(0.125 * cat(a + swap_lanes(a, 2), b + swap_lanes(b, 2)))
        red, black = split(p2w, rows[0], rows[1])
        row = 3 + i
        first = red * I2[0, row]
        return [
            (BD2, (0, row), first),
            (V2, (0, row), first),
            (BD2, (1, row), black * I2[1, row]),
            (pair2, (i,), jnp.where(odd, black[:, :128], red[:, :128])),
        ]

    V2[0, 2] = zero_row
    V2[0, 11] = zero_row
    V2[1, 2] = zero_row
    V2[1, 11] = zero_row
    loop(0, 8, right2, 8)

    sweep_y(2, V2, G2, BD2, 1, 3, 11)
    sweep_y(2, V2, G2, BD2, 0, 3, 11)
    sweep_y(2, V2, G2, BD2, 1, 3, 11)
    rows = []
    for y in range(4):
        r = 5 + y
        t = (D2[r] * (update_y(2, V2, G2, BD2, 0, r) - V2[0, r]))[:, :128]
        t = t + swap_subs(t, 2)
        rows.append(0.125 * (t + swap_lanes(t, 4)))
    gather(msg_b, GB, 1, message(rows))

    for y in range(4):
        CX[1, 1, y] = jnp.where(lane % 4 < 2, pair2[2 + y], V2[1, 5 + y, :, :128])
    x_b2 = exchange(X_B2, block_pieces(CX))
    x_v0 = exchange(X_V0, v0_pieces)

    def new_ice(r, j):
        both = jnp.concatenate([und[0, r, :, :128], und[1, r, :, :128]], axis=0)
        return [(outb, (r - HY,), both.astype(BF16))]

    loop(HY, HY + NY, new_ice, 4)
    copy = pltpu.make_async_copy(outb, ice_o, osem.at[4])
    copy.start()
    stores_out = [copy]
    all_bytes(GK, gr.at[0])
    k3r, k3b = global_level3(GK)
    row3 = lax.broadcasted_iota(jnp.int32, (64, 128), 0)
    lane3 = lax.broadcasted_iota(jnp.int32, (64, 128), 1)
    odd3 = (row3 + lane3) % 2 == 1
    edges3 = (row3 == 0, row3 == 63, lane3 == 0, lane3 == 127)

    def near3(o):
        return (roll(o, 1, 0), roll(o, -1, 0), roll(o, 1, 1), roll(o, -1, 1), o)

    def faces3(c, k, o):
        s = 0.25**3
        near = [jnp.where(e, 0.0, v) for e, v in zip(edges3, near3(o))] + [o]
        f = [0.5 * (k + value) for value in near] + [0.5 * k]
        d = ((f[0] + f[1]) + (f[2] + f[3])) + (f[4] + f[5])
        inv = 1.0 / d
        for n in range(5):
            g = f[n] * inv
            G3[c, n] = jnp.where(edges3[n], 0.0, g) if n < 4 else g
        I3[c] = inv * (1.0 / s)
        if c == 0:
            D3[...] = s * d

    faces3(0, k3r, k3b)
    faces3(1, k3b, k3r)

    lane4 = lax.broadcasted_iota(jnp.int32, (16, 128), 1)
    row4 = lax.broadcasted_iota(jnp.int32, (16, 128), 0)
    p4 = (lane4 // 2) % 2 == 1

    def level4_of(total):
        t = total + swap_subs(total, 1)
        buf4[...] = 0.125 * (t + swap_lanes(t, 1))
        low, high = buf4[pl.ds(0, 16, stride=4), :], buf4[pl.ds(2, 16, stride=4), :]
        return split(p4, low, high)

    k4 = level4_of(k3r + k3b)

    def near4(c, o):
        low, high = roll(o, 1, 0), roll(o, -1, 0)
        outer = jnp.where(p4, high, low) if c == 0 else jnp.where(p4, low, high)
        return (o, outer, roll(o, -2, 1), roll(o, 2, 1))

    def faces4(c):
        s = 0.25**4
        k = k4[c]
        take = p4 if c == 0 else jnp.logical_not(p4)
        edges = (None, jnp.where(take, row4, 15 - row4) == 15, lane4 >= 126, lane4 < 2)
        near = near4(c, k4[1 - c])
        near = [v if e is None else jnp.where(e, 0.0, v) for e, v in zip(edges, near)]
        f = [0.5 * (k + value) for value in near]
        d = ((f[0] + f[1]) + (f[2] + f[3])) + k
        inv = 1.0 / d
        g = [v * inv if e is None else jnp.where(e, 0.0, v * inv) for e, v in zip(edges, f)]
        return g, inv * (1.0 / s)

    g4r, i4r = faces4(0)
    g4b, i4b = faces4(1)

    received(x_b2)
    for yb in range(3):
        row_ok = (up_in, True, down_in)[yb]
        for r in range(4):
            x = joined(CX, yb, r)
            row = 1 + 4 * yb + r

            def fill(x):
                a, b = x[:, :128], x[:, 128:]
                first = cat(jnp.where(odd, roll(a, 1, 1), a), jnp.where(odd, roll(b, 1, 1), b))
                second = cat(jnp.where(odd, a, roll(a, -1, 1)), jnp.where(odd, b, roll(b, -1, 1)))
                return first, second

            first, second = fill(x)
            head = lane2 % 4 < 2

            def pair_up(y):
                return cat(roll(y[:, :128], 2, 1), roll(y[:, 128:], 2, 1))

            def pair_down(y):
                return cat(roll(y[:, :128], -2, 1), roll(y[:, 128:], -2, 1))

            BD2[0, row] = jnp.where(head, first, pair_up(first)) * I2[0, row]
            BD2[1, row] = jnp.where(head, second, pair_up(second)) * I2[1, row]
            V2[1, row] = jnp.where(ring_in & row_ok, jnp.where(head, pair_down(x), x), 0.0)

    received(x_v0)
    for copy in x_v0:
        copy.wait_send()

    def v0_sides(r, j):
        ok = ((r >= HY) | up_in) & ((r < HY + NY) | down_in)
        side = jnp.where(
            ok & (((lane < 5) & right_in) | ((lane >= 123) & left_in)), jnp.where(lane < 64, zv[1, r], zv[0, r]), 0.0
        )
        return [(V0, (1, r), cat(jnp.where(ok, V0[1, r, :, :128], 0.0), side))]

    loop(HY - 5, HY + NY + 5, v0_sides, 3)
    zrow = lax.broadcasted_iota(jnp.int32, (128, 256), 0)
    zcol = lax.broadcasted_iota(jnp.int32, (128, 256), 1)
    expand = (zrow == gz * 16 + zcol // 8 - jnp.where(zcol >= 192, 32, 0)).astype(F32)

    all_bytes(GB, gr.at[1])
    b3r, b3b = global_level3(GB)
    bd3 = (b3r * I3[0], b3b * I3[1])

    def update3(c, o):
        near = near3(o)
        t = [G3[c, n] * near[n] for n in range(5)]
        return bd3[c] + (((t[0] + t[1]) + (t[2] + t[3])) + t[4])

    v_r = bd3[0]
    v_b = update3(1, v_r)
    v_r = update3(0, v_b)
    v_b = update3(1, v_r)
    r3 = D3[...] * (update3(0, v_b) - v_r)
    b4 = level4_of(r3)
    bd4r, bd4b = b4[0] * i4r, b4[1] * i4b

    def update4(c, g, bd, o):
        near = near4(c, o)
        return bd + ((g[0] * near[0] + g[1] * near[1]) + (g[2] * near[2] + g[3] * near[3]))

    def sweep4(i, carry):
        red, black = carry
        red = update4(0, g4r, bd4r, black)
        black = update4(1, g4b, bd4b, red)
        return red, black

    zero4 = jnp.zeros((16, 128), F32)
    e_r, e_b = lax.fori_loop(0, COARSE_SWEEPS, sweep4, (zero4, zero4))
    low, high = split(p4, e_r, e_b)
    buf4[pl.ds(0, 16, stride=4), :] = low
    buf4[pl.ds(1, 16, stride=4), :] = low
    buf4[pl.ds(2, 16, stride=4), :] = high
    buf4[pl.ds(3, 16, stride=4), :] = high
    v_b = v_b + buf4[...]
    v_r = update3(0, v_b)
    v_b = update3(1, v_r)
    v_r = update3(0, v_b)
    v_b = update3(1, v_r)

    x_low, x_high = split(odd3, v_r, v_b)
    e3x[0, pl.ds(8, 64), :] = x_low
    e3x[1, pl.ds(8, 64), :] = x_high
    parts = []
    for n in range(2):
        for i in range(12):
            parts.append(e3x[n, pl.ds(gy * 4 + (4 + i), 1), :])
    wide = dot(jnp.concatenate(parts, axis=0), expand)
    for i in range(12):
        e = jnp.where(sub2 < 4, wide[i : i + 1], wide[12 + i : 13 + i])
        row_ok = up_in if i < 4 else (down_in if i >= 8 else True)
        V2[1, 1 + i] = V2[1, 1 + i] + jnp.where(ring_in & row_ok, e, 0.0)
    sweep_y(2, V2, G2, BD2, 0, 1, 13)
    sweep_y(2, V2, G2, BD2, 1, 1, 13)
    sweep_y(2, V2, G2, BD2, 0, 1, 13)
    sweep_y(2, V2, G2, BD2, 1, 3, 11)

    p1w = parity_y(1, lane2, sub2)

    def correct1(i, j):
        low, high = split(p2w, V2[0, 3 + i], V2[1, 3 + i])
        return [(V1, (1, 4 + 2 * i + n), V1[1, 4 + 2 * i + n] + e) for n, e in ((0, low), (1, high))]

    loop(0, 8, correct1, 4)
    sweep_y(1, V1, G1, BD1, 0, 4, 20)
    sweep_y(1, V1, G1, BD1, 1, 4, 20)
    sweep_y(1, V1, G1, BD1, 0, 4, 20)
    sweep_y(1, V1, G1, BD1, 1, 6, 18)

    def correct0(i, j):
        low, high = split(p1w, V1[0, 6 + i], V1[1, 6 + i])
        return [
            (V0, (1, 4 * i + n), V0[1, 4 * i + n] + e) for n, e in ((0, low), (1, low), (2, high), (3, high))
        ]

    loop(0, 12, correct0, 2)
    sweep0(0, 4, R0 - 4)
    sweep0(1, 4, R0 - 4)
    sweep0(0, 6, R0 - 6)
    sweep0(1, 6, R0 - 6)

    def results(r, j):
        stores = []
        for c in range(2):
            v = V0[c, r]
            res = D0[c, r] * (update0(c, r, j % 2) - v)
            stores.append((outf, (r - HY, c), v[:, :128]))
            stores.append((outf, (r - HY, 2 + c), res[:, :128]))
        return stores

    for k in range(4):
        lo = 8 * k
        loop(HY + lo, HY + lo + 8, results, 4)
        copy = pltpu.make_async_copy(outf.at[pl.ds(lo, 8)], fin_o.at[pl.ds(lo, 8)], osem.at[k])
        copy.start()
        stores_out.append(copy)

    for copies in (x_in, x_f, x_k, x_b1, x_b2):
        for copy in copies:
            copy.wait_send()
    all_bytes(GK, gs.at[0])
    all_bytes(GB, gs.at[1])
    for copy in stores_out:
        copy.wait()


def unpair(ice, fin, phase_o, pres_o, res_o, tmp):
    odd = lax.broadcasted_iota(jnp.int32, (8, 128), 1) % 2 == 1

    def row(y, j):
        par = odd if j % 2 == 0 else jnp.logical_not(odd)
        both = ice[y].astype(F32)
        stores = []
        for ref, red, black in (
            (tmp, both[:8], both[8:]),
            (pres_o, fin[y, 0], fin[y, 1]),
            (res_o, fin[y, 2], fin[y, 3]),
        ):
            stores.append((ref, (pl.ds(y, 8, stride=2 * NY), slice(None)), jnp.where(par, black, red)))
            stores.append((ref, (pl.ds(NY + y, 8, stride=2 * NY), slice(None)), jnp.where(par, red, black)))
        return stores

    loop(0, NY, row, 4)
    phase_o[...] = tmp[...].astype(BF16)


def per_device(GY, GZ, phase, undercool, perm_base, source, pressure):
    def vm(*shape):
        return pltpu.VMEM(shape, F32)

    scratch = [
        pltpu.VMEM((3, NX * NY, NZ), BF16),
        vm(5, NX * NY, NZ),
        pltpu.VMEM((NY, 16, 128), BF16),
        vm(NY, 4, 8, 128),
        pltpu.VMEM((R0, 48, 128), BF16),
        vm(R0, 24, 128),
        pltpu.VMEM((4, 48, 128), BF16),
        vm(4, 24, 128),
        pltpu.VMEM((2, 6, 48, 128), BF16),
        vm(2, 6, 24, 128),
        vm(2, R0, 8, 256),
        vm(2, R0, 8, 256),
        vm(2, R0, 8, 256),
        vm(2, R0, 8, 256),
        vm(2, R0, 8, 256),
        vm(2, R0, 8, 256),
        vm(2, R0, 6, 8, 256),
        vm(2, R0, 8, 256),
        vm(2, R0, 8, 256),
        vm(2, R0, 8, 128),
        vm(3, 3, 12, 8, 128),
        vm(3, 3, 4, 8, 128),
        vm(2, R1, 8, 256),
        vm(2, R1, 8, 256),
        vm(2, R1, 6, 8, 256),
        vm(2, R1, 8, 256),
        vm(2, R1, 8, 256),
        vm(R1, 8, 256),
        vm(2, R2, 8, 256),
        vm(2, R2, 8, 256),
        vm(2, R2, 6, 8, 256),
        vm(2, R2, 8, 256),
        vm(2, R2, 8, 256),
        vm(R2, 8, 256),
        vm(R1, 8, 128),
        vm(4, 8, 128),
        vm(2, 12, 8, 128),
        vm(1, 1, 128),
        vm(1, 1, 128),
        vm(GY * GZ, 1, 128),
        vm(GY * GZ, 1, 128),
        vm(2, 64, 128),
        vm(2, 5, 64, 128),
        vm(2, 64, 128),
        vm(64, 128),
        vm(64, 128),
        vm(2, 80, 128),
        vm(8, 8, 128),
        pltpu.SemaphoreType.DMA((N_X, 8)),
        pltpu.SemaphoreType.DMA((N_X, 8)),
        pltpu.SemaphoreType.DMA((2,)),
        pltpu.SemaphoreType.DMA((2,)),
        pltpu.SemaphoreType.DMA((5,)),
        pltpu.SemaphoreType.DMA((5,)),
        pltpu.SemaphoreType.REGULAR((2,)),
    ]
    hbm = pl.BlockSpec(memory_space=pltpu.HBM)
    vmem = pl.BlockSpec(memory_space=pltpu.VMEM)
    flat = (NX * NY, NZ)
    packed_ice, packed = pl.pallas_call(
        functools.partial(kernel, GY, GZ),
        out_shape=(jax.ShapeDtypeStruct((NY, 16, NZ), BF16), jax.ShapeDtypeStruct((NY, 4, 8, NZ), F32)),
        in_specs=[hbm] * 5,
        out_specs=(hbm, hbm),
        scratch_shapes=scratch,
        compiler_params=pltpu.CompilerParams(
            collective_id=0, has_side_effects=True, vmem_limit_bytes=63 * 2**20
        ),
    )(*[a.reshape(flat) for a in (phase, undercool, perm_base, source, pressure)])
    outs = pl.pallas_call(
        unpair,
        out_shape=(
            jax.ShapeDtypeStruct(flat, BF16),
            jax.ShapeDtypeStruct(flat, F32),
            jax.ShapeDtypeStruct(flat, F32),
        ),
        in_specs=[vmem] * 2,
        out_specs=(vmem, vmem, vmem),
        scratch_shapes=[vm(NX * NY, NZ)],
        compiler_params=pltpu.CompilerParams(vmem_limit_bytes=63 * 2**20),
    )(packed_ice, packed)
    return tuple(a.reshape(NX, NY, NZ) for a in outs)


def solution(mesh):
    spec = P(None, "gy", "gz")
    return jax.shard_map(
        functools.partial(per_device, mesh.shape["gy"], mesh.shape["gz"]),
        mesh=mesh,
        in_specs=(spec,) * 5,
        out_specs=(spec,) * 3,
        check_vma=False,
    )
```

```python
import functools
import jax
import jax.numpy as jnp
from jax import lax
from jax.experimental import pallas as pl
from jax.experimental.pallas import tpu as pltpu
from jax.sharding import PartitionSpec as P

MESH = pl.DeviceIdType.MESH
F32 = jnp.float32
BF16 = jnp.bfloat16
COARSE_SWEEPS = 20
NX, NY, NZ = 16, 32, 128
HY = 8
R0 = NY + 2 * HY
R1 = 24
R2 = 14
NEAR = [(dy, dz) for dy in (-1, 0, 1) for dz in (-1, 0, 1) if (dy, dz) != (0, 0)]
X_IN, X_F, X_K, X_B1, X_V0, X_B2 = range(6)
N_X = 6


def roll(x, shift, axis):
    size = x.shape[axis]
    shift = shift % size
    return x if shift == 0 else pltpu.roll(x, shift, axis)


def loop(lo, hi, body, step=2):
    def trip(i, carry):
        stores = []
        for j in range(step):
            stores.extend(body(lo + i * step + j, j))
        for ref, index, value in stores:
            ref[index] = value
        return carry

    trips = (hi - lo) // step
    assert trips * step == hi - lo
    if trips == 1:
        trip(0, 0)
    else:
        lax.fori_loop(0, trips, trip, 0)


def kernel(
    GY, GZ, phase_h, under_h, perm_h, src_h, pres_h, ice_o, fin_o,
    inb, tmp, outb, outf,
    ha, hf, zp, zpf, zb, zbf,
    ice, und, prm, S0, V0, K0, G0, BD0, D0, zv,
    KX, CX, K1, V1, G1, I1, BD1, D1, K2, V2, G2, I2, BD2, D2,
    b1, zp1, zb1, msg_k, msg_b, GK, GB, K3, G3, I3, D3, buf4, e3x, pair2,
    ssem, rsem, gs, gr, lsem, osem, known,
):
    gy, gz = lax.axis_index("gy"), lax.axis_index("gz")
    me = gy * GZ + gz

    def peer(dy, dz):
        return (lax.rem(gy + dy + GY, GY), lax.rem(gz + dz + GZ, GZ))

    barrier = pltpu.get_barrier_semaphore()

    for dy, dz in NEAR:
        pl.semaphore_signal(barrier, inc=1, device_id=peer(dy, dz), device_id_type=MESH)

    loads = []
    for n, (src, dst) in enumerate(
        ((phase_h, inb.at[0]), (under_h, inb.at[1]), (perm_h, inb.at[2]), (src_h, tmp.at[3]), (pres_h, tmp.at[4]))
    ):
        copy = pltpu.make_async_copy(src, dst, lsem.at[n])
        copy.start()
        loads.append(copy)

    lane = lax.broadcasted_iota(jnp.int32, (8, 128), 1)
    sub = lax.broadcasted_iota(jnp.int32, (8, 128), 0)
    lane2 = lax.broadcasted_iota(jnp.int32, (8, 256), 1)
    sub2 = lax.broadcasted_iota(jnp.int32, (8, 256), 0)
    odd = lane % 2 == 1
    odd2 = lane2 % 2 == 1
    right_in, left_in = gz < GZ - 1, gz > 0
    up_in, down_in = gy > 0, gy < GY - 1
    ring_in = (lane2 < 128) | ((lane2 < 192) & right_in) | ((lane2 >= 192) & left_in)

    def cat(a, b):
        return jnp.concatenate([a, b], axis=-1)

    def ring(o, d):
        a, b = o[:, :128], o[:, 128:]
        fa, fb = roll(a, -d, 1), roll(b, -d, 1)
        ba, bb = roll(a, d, 1), roll(b, d, 1)
        end, start = lane >= 128 - d, lane < d
        ahead = cat(jnp.where(end, fb, fa), jnp.where(end, fa, fb))
        behind = cat(jnp.where(start, bb, ba), jnp.where(start, ba, bb))
        return ahead, behind

    for copy in loads:
        copy.wait()
    for n in range(3):
        tmp[n] = inb[n].astype(F32)

    def red_black_of(n, y, j):
        even = tmp[n, pl.ds(y, 8, stride=2 * NY), :]
        odds = tmp[n, pl.ds(NY + y, 8, stride=2 * NY), :]
        par = odd if j % 2 == 0 else jnp.logical_not(odd)
        return jnp.where(par, odds, even), jnp.where(par, even, odds)

    zp[...] = jnp.zeros_like(zp)
    zpf[...] = jnp.zeros_like(zpf)

    def prepare(k, carry):
        packed = jnp.zeros((48, 128), F32)
        packed_f = jnp.zeros((24, 128), F32)
        group = lax.broadcasted_iota(jnp.int32, (48, 128), 1) // 16
        for q in range(8):
            y = 8 * k + q
            parts = []
            for n in range(3):
                parts.extend(red_black_of(n, y, q))
            row = jnp.concatenate(parts, axis=0)
            ha[HY + y] = row.astype(BF16)
            s_r, s_b = red_black_of(3, y, q)
            _, v_b = red_black_of(4, y, q)
            row_f = jnp.concatenate([s_r, s_b, v_b], axis=0)
            hf[HY + y] = row_f
            packed = jnp.where(group == q, roll(row, 16 * q + 8, 1), packed)
            packed_f = jnp.where(group[:24] == q, roll(row_f, 16 * q + 8, 1), packed_f)
        zp[k] = packed.astype(BF16)
        zpf[k] = packed_f
        return carry

    lax.fori_loop(0, 4, prepare, 0)

    pl.semaphore_wait(barrier, len(NEAR))

    def exchange(ex, pieces):
        copies = []
        for n, (dy, dz) in enumerate(NEAR):
            src, dst = pieces(dy, dz)
            copy = pltpu.make_async_remote_copy(
                src, dst, ssem.at[ex, n], rsem.at[ex, n], device_id=peer(dy, dz), device_id_type=MESH
            )
            copy.start()
            copies.append(copy)
        return copies

    def received(copies):
        for copy in copies:
            copy.wait_recv()

    def input_pieces(rows, packed, landing, width):
        def pieces(dy, dz):
            if dz == 0 and dy < 0:
                return rows.at[pl.ds(HY, width)], rows.at[pl.ds(HY + NY, width)]
            if dz == 0:
                return rows.at[pl.ds(HY + NY - width, width)], rows.at[pl.ds(HY - width, width)]
            side = 0 if dz > 0 else 1
            if dy == 0:
                return packed, landing.at[side, pl.ds(1, 4)]
            if dy > 0:
                return packed.at[pl.ds(3, 1)], landing.at[side, pl.ds(0, 1)]
            return packed.at[pl.ds(0, 1)], landing.at[side, pl.ds(5, 1)]

        return pieces

    x_in = exchange(X_IN, input_pieces(ha, zp, zb, 6))
    x_f = exchange(X_F, input_pieces(hf, zpf, zbf, 5))

    zero_row = jnp.zeros((8, 256), F32)
    e3x[...] = jnp.zeros_like(e3x)
    for c in range(2):
        for r in (0, R2 - 1):
            K2[c, r] = zero_row
            V2[c, r] = zero_row
        for r in (0, 1, R1 - 2, R1 - 1):
            V1[c, r] = zero_row
        for r in (3, R0 - 4):
            V0[c, r] = zero_row

    received(x_in)
    for dy, dz in NEAR:
        pl.semaphore_signal(known.at[0], inc=1, device_id=peer(2 * dy, 2 * dz), device_id_type=MESH)

    def row_mask(r, width):
        ok = ((r >= HY) | up_in) & ((r < HY + NY) | down_in)
        lanes = (lane2 < 128) | ((lane2 < 128 + width) & right_in) | ((lane2 >= 256 - width) & left_in)
        return lanes & ok

    def unpack(k, carry):
        group = lax.broadcasted_iota(jnp.int32, (48, 128), 1) % 16 < 8
        merged = jnp.where(group, zb[0, k].astype(F32), zb[1, k].astype(F32))
        for q in range(8):
            r = 8 * k + q
            ok = row_mask(r, 6) & (r >= 2) & (r < R0 - 2)
            ok5 = row_mask(r, 5) & (r >= 3) & (r < R0 - 3)
            side = roll(merged, 120 - 16 * q, 1)
            a = ha[r].astype(F32)
            for c in range(2):
                s = slice(8 * c, 8 * c + 8)
                ice[c, r] = jnp.where(ok, cat(a[s], side[s]), 0.0)
                s = slice(16 + 8 * c, 24 + 8 * c)
                und[c, r] = cat(a[s], side[s])
                s = slice(32 + 8 * c, 40 + 8 * c)
                prm[c, r] = jnp.where(ok5, cat(a[s], side[s]), 0.0)
        return carry

    def unpack_f(k, carry):
        group = lax.broadcasted_iota(jnp.int32, (24, 128), 1) % 16 < 8
        merged = jnp.where(group, zbf[0, k], zbf[1, k])
        for q in range(8):
            r = 8 * k + q
            ok5 = row_mask(r, 5) & (r >= 3) & (r < R0 - 3)
            side = roll(merged, 120 - 16 * q, 1)
            f = hf[r]
            for c in range(2):
                s = slice(8 * c, 8 * c + 8)
                S0[c, r] = cat(f[s], side[s])
            V0[1, r] = jnp.where(ok5, cat(f[16:24], side[16:24]), 0.0)
        return carry

    lax.fori_loop(0, 6, unpack, 0)

    def pick(c, j):
        return odd2 if (c + j) % 2 == 0 else jnp.logical_not(odd2)

    def x_outer(o, take):
        return jnp.where(take, roll(o, -1, 0), roll(o, 1, 0))

    def x_edge(take):
        return jnp.where(take, sub2, 7 - sub2) == 7

    def near0(ref, c, r, j):
        o = ref[1 - c, r]
        take = pick(c, j)
        ahead, behind = ring(o, 1)
        return (ref[1 - c, r - 1], ref[1 - c, r + 1], o, x_outer(o, take), ahead, behind)

    def permeability(r, j):
        j = j % 2
        stores = []
        for c in range(2):
            now = ice[c, r]
            near = list(near0(ice, c, r, j))
            near[3] = jnp.where(x_edge(pick(c, j)), 0.0, near[3])
            lap = near[0]
            for value in near[1:]:
                lap = lap + value
            lap = lap - 6.0 * now
            well = 2.0 * now * (1.0 - now) * (1.0 - 2.0 * now)
            drive = 30.0 * now * now * (1.0 - now) * (1.0 - now) * und[c, r]
            new = jnp.clip(now + 0.12 * lap - 0.5 * well + 0.25 * drive, 0.0, 1.0)
            stores.append((K0, (c, r), jnp.where(prm[c, r] > 0.0, prm[c, r] * jnp.exp(-1.5 * new), 0.0)))
            stores.append((und, (c, r), new))
        return stores

    loop(2, R0 - 2, permeability, 4)

    def swap_lanes(x, d):
        return jnp.where((lax.broadcasted_iota(jnp.int32, x.shape, 1) // d) % 2 == 0, roll(x, -d, 1), roll(x, d, 1))

    def swap_subs(x, d):
        return jnp.where((lax.broadcasted_iota(jnp.int32, x.shape, 0) // d) % 2 == 0, roll(x, -d, 0), roll(x, d, 0))

    def parity_y(level, ln, sb):
        return (sb // (1 if level == 1 else 2) + ln // (2 if level == 1 else 4)) % 2 == 1

    def own0(c, r):
        return K0[c, r, :, :128]

    def coarse0(y):
        r = HY + 2 * y
        t = (own0(0, r) + own0(1, r)) + (own0(0, r + 1) + own0(1, r + 1))
        return 0.125 * (t + swap_lanes(t, 1))

    p1, p2 = parity_y(1, lane, sub), parity_y(2, lane, sub)

    def split(p, low, high):
        return jnp.where(p, high, low), jnp.where(p, low, high)

    k2_rows = []
    for yp in range(8):
        red, black = split(p1, coarse0(2 * yp), coarse0(2 * yp + 1))
        KX[1, 1, yp] = jnp.where(odd, black, red)
        t = red + black
        t = t + swap_subs(t, 1)
        k2_rows.append(0.125 * (t + swap_lanes(t, 2)))
    k3_rows = []
    for yp in range(4):
        red, black = split(p2, k2_rows[2 * yp], k2_rows[2 * yp + 1])
        KX[1, 1, 8 + yp] = jnp.where(odd, black, red)
        t = red + black
        t = t + swap_subs(t, 2)
        k3_rows.append(0.125 * (t + swap_lanes(t, 4)))

    def block_pieces(ref):
        return lambda dy, dz: (ref.at[1, 1], ref.at[1 - dy, 1 - dz])

    x_k = exchange(X_K, block_pieces(KX))

    squeeze = (
        lax.broadcasted_iota(jnp.int32, (128, 128), 0) == 8 * (lax.broadcasted_iota(jnp.int32, (128, 128), 1) % 16)
    ).astype(F32)

    def dot(a, b):
        return lax.dot_general(
            a, b, (((1,), (0,)), ((), ())), precision=lax.Precision.HIGHEST, preferred_element_type=F32
        )

    def message(rows):
        piece = jnp.zeros((8, 128), F32)
        for y in range(4):
            u = rows[y]
            t = jnp.where((y + lane // 8) % 2 == 0, u, roll(u, 4, 0))
            piece = jnp.where(sub % 4 == y, t, piece)
        wide = dot(piece, squeeze)
        return jnp.sum(jnp.where(lane // 16 == sub, wide, 0.0), axis=0, keepdims=True)

    def gather(msg, landing, n, row):
        msg[0] = row
        landing[pl.ds(me, 1)] = row.reshape(1, 1, 128)

        def start(y, z):
            pltpu.make_async_remote_copy(
                msg, landing.at[pl.ds(me, 1)], gs.at[n], gr.at[n], device_id=(y, z), device_id_type=MESH
            ).start()

        columns = [lax.rem(gz + i, GZ) for i in (4, 3, 5, 2, 6, 1, 7, 0)]

        def send(i, carry):
            y = lax.rem(gy + i, GY)
            for z in columns:
                start(y, z)
            return carry

        lax.fori_loop(1, GY, send, 0)
        for z in columns[:-1]:
            start(gy, z)

    def all_bytes(landing, sem):
        part = landing.at[pl.ds(0, GY * GZ - 1)]
        pltpu.make_async_copy(part, part, sem).wait()

    def global_level3(landing):
        x = landing[...].reshape(GY, GZ, 128)
        ln = lax.broadcasted_iota(jnp.int32, x.shape, 2)
        sb = lax.broadcasted_iota(jnp.int32, x.shape, 1)
        for bit in (1, 2, 4):
            s_set, t_set = (sb // bit) % 2 == 1, (ln // (16 * bit)) % 2 == 1
            down = roll(roll(x, bit, 1), -16 * bit, 2)
            up = roll(roll(x, -bit, 1), 16 * bit, 2)
            x = jnp.where(s_set == t_set, x, jnp.where(s_set, down, up))
        pairs = x.reshape(GY // 2, 2, 8, 128)
        even, odds = pairs[:, 0], pairs[:, 1]
        low = lax.broadcasted_iota(jnp.int32, even.shape, 1) < 4
        red = jnp.where(low, even, roll(odds, 4, 1))
        black = jnp.where(low, roll(even, 4, 1), odds)
        return red.reshape(64, 128), black.reshape(64, 128)

    row_k = message(k3_rows)

    received(x_f)
    lax.fori_loop(0, 6, unpack_f, 0)

    pl.semaphore_wait(known.at[0], len(NEAR))
    for dy in (-4, 4):
        pl.semaphore_signal(known.at[1], inc=1, device_id=peer(dy, 0), device_id_type=MESH)

    def faces0(r, j):
        j = j % 2
        stores = []
        ok = row_mask(r, 5)
        for c in range(2):
            k = K0[c, r]
            take = pick(c, j)
            edge = x_edge(take)
            near = list(near0(K0, c, r, j))
            near[3] = jnp.where(edge, 0.0, near[3])
            f = [0.5 * (k + value) for value in near]
            d = ((f[0] + f[1]) + (f[2] + f[3])) + (f[4] + f[5])
            inv = jnp.where(ok, 1.0 / d, 0.0)
            for n in range(6):
                g = f[n] * inv
                stores.append((G0, (c, r, n), jnp.where(edge, 0.0, g) if n == 3 else g))
            stores.append((BD0, (c, r), jnp.where(ok, S0[c, r], 0.0) * inv))
            stores.append((D0, (c, r), d))
        return stores

    loop(4, R0 - 4, faces0, 4)

    def update0(c, r, j):
        near = near0(V0, c, r, j)
        t = [G0[c, r, n] * near[n] for n in range(6)]
        return BD0[c, r] + (((t[0] + t[1]) + (t[2] + t[3])) + (t[4] + t[5]))

    def sweep0(c, lo, hi):
        def body(r, j):
            return [(V0, (c, r), update0(c, r, j % 2))]

        loop(lo, hi, body, 10 if hi - lo == 40 else 12)

    sweep0(0, 4, R0 - 4)
    sweep0(1, 4, R0 - 4)
    sweep0(0, 6, R0 - 6)
    sweep0(1, 6, R0 - 6)

    def defect0(r, j):
        return (D0[0, r] * (update0(0, r, j) - V0[0, r]))[:, :128]

    def right1(yp, j):
        rows = []
        for j in range(2):
            r = HY + 4 * yp + 2 * j
            t = defect0(r, 0) + defect0(r + 1, 1)
            rows.append(0.125 * (t + swap_lanes(t, 1)))
        red, black = split(p1, rows[0], rows[1])
        return [(b1, (8 + yp,), jnp.where(odd, black, red))]

    loop(0, 8, right1, 2)
    for k in range(4):
        first, second = b1[8 + 2 * k], b1[9 + 2 * k]
        zp1[k] = jnp.where(lane < 64, roll(first, 32, 1), roll(second, 96, 1))

    def b1_pieces(dy, dz):
        if dz == 0 and dy < 0:
            return b1.at[pl.ds(8, 6)], b1.at[pl.ds(16, 6)]
        if dz == 0:
            return b1.at[pl.ds(10, 6)], b1.at[pl.ds(2, 6)]
        side = 0 if dz > 0 else 1
        if dy == 0:
            return zp1, zb1.at[side, pl.ds(4, 4)]
        if dy > 0:
            return zp1.at[pl.ds(1, 3)], zb1.at[side, pl.ds(1, 3)]
        return zp1.at[pl.ds(0, 3)], zb1.at[side, pl.ds(8, 3)]

    x_b1 = exchange(X_B1, b1_pieces)

    pl.semaphore_wait(known.at[1], 2)
    gather(msg_k, GK, 0, row_k)
    received(x_k)

    def joined(ref, yb, r):
        a = ref[yb, 1, r]
        b = jnp.where(lane < 64, ref[yb, 2, r], ref[yb, 0, r])
        return cat(a, b)

    def apart(x):
        a, b = x[:, :128], x[:, 128:]
        red = cat(jnp.where(odd, roll(a, 1, 1), a), jnp.where(odd, roll(b, 1, 1), b))
        black = cat(jnp.where(odd, a, roll(a, -1, 1)), jnp.where(odd, b, roll(b, -1, 1)))
        return red, black

    for yb in range(3):
        row_ok = (up_in, True, down_in)[yb]
        ok = ring_in & row_ok

        def spread1(r, carry, yb=yb, ok=ok):
            red, black = apart(joined(KX, yb, r))
            K1[0, 8 * yb + r] = jnp.where(ok, red, 0.0)
            K1[1, 8 * yb + r] = jnp.where(ok, black, 0.0)
            return carry

        lax.fori_loop(0, 8, spread1, 0)
        for r in range(4):
            red, black = apart(joined(KX, yb, 8 + r))
            K2[0, 1 + 4 * yb + r] = jnp.where(ok, red, 0.0)
            K2[1, 1 + 4 * yb + r] = jnp.where(ok, black, 0.0)

    def near_y(level, ref, c, r):
        dx, dz = (1, 2) if level == 1 else (2, 4)
        p = parity_y(level, lane2, sub2)
        o, low, high = ref[1 - c, r], ref[1 - c, r - 1], ref[1 - c, r + 1]
        outer = jnp.where(p, high, low) if c == 0 else jnp.where(p, low, high)
        ahead, behind = ring(o, dz)
        return (o, outer, roll(o, -dx, 0), roll(o, dx, 0), ahead, behind)

    def faces_y(level, K, G, I, D, r):
        dx = 1 if level == 1 else 2
        s = 0.25**level
        stores = []
        for c in range(2):
            k = K[c, r]
            near = list(near_y(level, K, c, r))
            last, first = sub2 >= 8 - dx, sub2 < dx
            near[2] = jnp.where(last, 0.0, near[2])
            near[3] = jnp.where(first, 0.0, near[3])
            f = [0.5 * (k + value) for value in near]
            d = ((f[0] + f[1]) + (f[2] + f[3])) + (f[4] + f[5])
            inv = jnp.where(k > 0.0, 1.0 / d, 0.0)
            for n in range(6):
                g = f[n] * inv
                if n == 2:
                    g = jnp.where(last, 0.0, g)
                if n == 3:
                    g = jnp.where(first, 0.0, g)
                stores.append((G, (c, r, n), g))
            stores.append((I, (c, r), inv * (1.0 / s)))
            if c == 0:
                stores.append((D, (r,), s * d))
        return stores

    loop(2, R1 - 2, lambda r, j: faces_y(1, K1, G1, I1, D1, r))
    loop(1, R2 - 1, lambda r, j: faces_y(2, K2, G2, I2, D2, r))

    received(x_b1)

    def v0_pieces(dy, dz):
        def at(r, n):
            return V0.at[1, pl.ds(r, n), :, pl.ds(0, 128)]

        lo, n, to = {-1: (HY, 5, HY + NY), 0: (HY, NY, HY), 1: (HY + NY - 5, 5, HY - 5)}[dy]
        if dz == 0:
            return at(lo, n), at(to, n)
        return at(lo, n), zv.at[0 if dz > 0 else 1, pl.ds(to, n)]

    def spread_b(k, j):
        stores = []
        merged = jnp.where(lane % 64 < 32, zb1[0, k], zb1[1, k])
        for q in range(2):
            r = 2 * k + q
            red, black = apart(cat(b1[r], roll(merged, -64 * q - 32, 1)))
            stores.append((BD1, (0, r), jnp.where(I1[0, r] > 0.0, red, 0.0) * I1[0, r]))
            stores.append((BD1, (1, r), jnp.where(I1[1, r] > 0.0, black, 0.0) * I1[1, r]))
            stores.append((V1, (0, r), stores[-2][2]))
        return stores

    loop(1, 11, spread_b, 10)

    def update_y(level, V, G, BD, c, r):
        near = near_y(level, V, c, r)
        t = [G[c, r, n] * near[n] for n in range(6)]
        return BD[c, r] + (((t[0] + t[1]) + (t[2] + t[3])) + (t[4] + t[5]))

    def sweep_y(level, V, G, BD, c, lo, hi):
        def body(r, j):
            return [(V, (c, r), update_y(level, V, G, BD, c, r))]

        loop(lo, hi, body, hi - lo)

    sweep_y(1, V1, G1, BD1, 1, 2, 22)
    sweep_y(1, V1, G1, BD1, 0, 2, 22)
    sweep_y(1, V1, G1, BD1, 1, 2, 22)

    p2w = parity_y(2, lane2, sub2)

    def right2(i, j):
        rows = []
        for j in range(2):
            r = 4 + 2 * i + j
            t = D1[r] * (update_y(1, V1, G1, BD1, 0, r) - V1[0, r])
            t = t + swap_subs(t, 1)
            a, b = t[:, :128], t[:, 128:]
            rows.append(0.125 * cat(a + swap_lanes(a, 2), b + swap_lanes(b, 2)))
        red, black = split(p2w, rows[0], rows[1])
        row = 3 + i
        first = red * I2[0, row]
        return [
            (BD2, (0, row), first),
            (V2, (0, row), first),
            (BD2, (1, row), black * I2[1, row]),
            (pair2, (i,), jnp.where(odd, black[:, :128], red[:, :128])),
        ]

    V2[0, 2] = zero_row
    V2[0, 11] = zero_row
    V2[1, 2] = zero_row
    V2[1, 11] = zero_row
    loop(0, 8, right2, 8)

    sweep_y(2, V2, G2, BD2, 1, 3, 11)
    sweep_y(2, V2, G2, BD2, 0, 3, 11)
    sweep_y(2, V2, G2, BD2, 1, 3, 11)
    rows = []
    for y in range(4):
        r = 5 + y
        t = (D2[r] * (update_y(2, V2, G2, BD2, 0, r) - V2[0, r]))[:, :128]
        t = t + swap_subs(t, 2)
        rows.append(0.125 * (t + swap_lanes(t, 4)))
    gather(msg_b, GB, 1, message(rows))

    for y in range(4):
        CX[1, 1, y] = jnp.where(lane % 4 < 2, pair2[2 + y], V2[1, 5 + y, :, :128])
    x_b2 = exchange(X_B2, block_pieces(CX))
    x_v0 = exchange(X_V0, v0_pieces)

    def new_ice(r, j):
        both = jnp.concatenate([und[0, r, :, :128], und[1, r, :, :128]], axis=0)
        return [(outb, (r - HY,), both.astype(BF16))]

    loop(HY, HY + NY, new_ice, 4)
    copy = pltpu.make_async_copy(outb, ice_o, osem.at[4])
    copy.start()
    stores_out = [copy]
    all_bytes(GK, gr.at[0])
    k3r, k3b = global_level3(GK)
    row3 = lax.broadcasted_iota(jnp.int32, (64, 128), 0)
    lane3 = lax.broadcasted_iota(jnp.int32, (64, 128), 1)
    odd3 = (row3 + lane3) % 2 == 1
    edges3 = (row3 == 0, row3 == 63, lane3 == 0, lane3 == 127)

    def near3(o):
        return (roll(o, 1, 0), roll(o, -1, 0), roll(o, 1, 1), roll(o, -1, 1), o)

    def faces3(c, k, o):
        s = 0.25**3
        near = [jnp.where(e, 0.0, v) for e, v in zip(edges3, near3(o))] + [o]
        f = [0.5 * (k + value) for value in near] + [0.5 * k]
        d = ((f[0] + f[1]) + (f[2] + f[3])) + (f[4] + f[5])
        inv = 1.0 / d
        for n in range(5):
            g = f[n] * inv
            G3[c, n] = jnp.where(edges3[n], 0.0, g) if n < 4 else g
        I3[c] = inv * (1.0 / s)
        if c == 0:
            D3[...] = s * d

    faces3(0, k3r, k3b)
    faces3(1, k3b, k3r)

    lane4 = lax.broadcasted_iota(jnp.int32, (16, 128), 1)
    row4 = lax.broadcasted_iota(jnp.int32, (16, 128), 0)
    p4 = (lane4 // 2) % 2 == 1

    def level4_of(total):
        t = total + swap_subs(total, 1)
        buf4[...] = 0.125 * (t + swap_lanes(t, 1))
        low, high = buf4[pl.ds(0, 16, stride=4), :], buf4[pl.ds(2, 16, stride=4), :]
        return split(p4, low, high)

    k4 = level4_of(k3r + k3b)

    def near4(c, o):
        low, high = roll(o, 1, 0), roll(o, -1, 0)
        outer = jnp.where(p4, high, low) if c == 0 else jnp.where(p4, low, high)
        return (o, outer, roll(o, -2, 1), roll(o, 2, 1))

    def faces4(c):
        s = 0.25**4
        k = k4[c]
        take = p4 if c == 0 else jnp.logical_not(p4)
        edges = (None, jnp.where(take, row4, 15 - row4) == 15, lane4 >= 126, lane4 < 2)
        near = near4(c, k4[1 - c])
        near = [v if e is None else jnp.where(e, 0.0, v) for e, v in zip(edges, near)]
        f = [0.5 * (k + value) for value in near]
        d = ((f[0] + f[1]) + (f[2] + f[3])) + k
        inv = 1.0 / d
        g = [v * inv if e is None else jnp.where(e, 0.0, v * inv) for e, v in zip(edges, f)]
        return g, inv * (1.0 / s)

    g4r, i4r = faces4(0)
    g4b, i4b = faces4(1)

    def shifts4(o):
        return near4(1, o)

    back4 = [shifts4(g) for g in g4r]
    m4 = (
        (g4b[0] * back4[0][0] + g4b[1] * back4[1][1]) + (g4b[2] * back4[3][2] + g4b[3] * back4[2][3]),
        g4b[0] * back4[1][0],
        g4b[1] * back4[0][1],
        g4b[0] * back4[2][0] + g4b[2] * back4[0][2],
        g4b[0] * back4[3][0] + g4b[3] * back4[0][3],
        g4b[1] * back4[2][1] + g4b[2] * back4[1][2],
        g4b[1] * back4[3][1] + g4b[3] * back4[1][3],
        g4b[2] * back4[2][2],
        g4b[3] * back4[3][3],
    )

    received(x_b2)
    for yb in range(3):
        row_ok = (up_in, True, down_in)[yb]
        for r in range(4):
            x = joined(CX, yb, r)
            row = 1 + 4 * yb + r

            def fill(x):
                a, b = x[:, :128], x[:, 128:]
                first = cat(jnp.where(odd, roll(a, 1, 1), a), jnp.where(odd, roll(b, 1, 1), b))
                second = cat(jnp.where(odd, a, roll(a, -1, 1)), jnp.where(odd, b, roll(b, -1, 1)))
                return first, second

            first, second = fill(x)
            head = lane2 % 4 < 2

            def pair_up(y):
                return cat(roll(y[:, :128], 2, 1), roll(y[:, 128:], 2, 1))

            def pair_down(y):
                return cat(roll(y[:, :128], -2, 1), roll(y[:, 128:], -2, 1))

            BD2[0, row] = jnp.where(head, first, pair_up(first)) * I2[0, row]
            BD2[1, row] = jnp.where(head, second, pair_up(second)) * I2[1, row]
            V2[1, row] = jnp.where(ring_in & row_ok, jnp.where(head, pair_down(x), x), 0.0)

    received(x_v0)
    for copy in x_v0:
        copy.wait_send()

    def v0_sides(r, j):
        ok = ((r >= HY) | up_in) & ((r < HY + NY) | down_in)
        side = jnp.where(
            ok & (((lane < 5) & right_in) | ((lane >= 123) & left_in)), jnp.where(lane < 64, zv[1, r], zv[0, r]), 0.0
        )
        return [(V0, (1, r), cat(jnp.where(ok, V0[1, r, :, :128], 0.0), side))]

    loop(HY - 5, HY + NY + 5, v0_sides, 3)
    zrow = lax.broadcasted_iota(jnp.int32, (128, 256), 0)
    zcol = lax.broadcasted_iota(jnp.int32, (128, 256), 1)
    expand = (zrow == gz * 16 + zcol // 8 - jnp.where(zcol >= 192, 32, 0)).astype(F32)

    all_bytes(GB, gr.at[1])
    b3r, b3b = global_level3(GB)
    bd3 = (b3r * I3[0], b3b * I3[1])

    def update3(c, o):
        near = near3(o)
        t = [G3[c, n] * near[n] for n in range(5)]
        return bd3[c] + (((t[0] + t[1]) + (t[2] + t[3])) + t[4])

    v_r = bd3[0]
    v_b = update3(1, v_r)
    v_r = update3(0, v_b)
    v_b = update3(1, v_r)
    r3 = D3[...] * (update3(0, v_b) - v_r)
    b4 = level4_of(r3)
    bd4r, bd4b = b4[0] * i4r, b4[1] * i4b

    def update4(c, g, bd, o):
        near = near4(c, o)
        return bd + ((g[0] * near[0] + g[1] * near[1]) + (g[2] * near[2] + g[3] * near[3]))

    c4 = update4(1, g4b, bd4b, bd4r)

    def sweep4(i, black):
        low, high = roll(black, 1, 0), roll(black, -1, 0)
        outer, inner = jnp.where(p4, high, low), jnp.where(p4, low, high)
        t = [
            m * v
            for m, v in zip(
                m4,
                (
                    black, outer, inner, roll(black, -2, 1), roll(black, 2, 1),
                    roll(outer, -2, 1), roll(outer, 2, 1), roll(black, -4, 1), roll(black, 4, 1),
                ),
            )
        ]
        near = ((c4 + t[0]) + (t[1] + t[2])) + ((t[3] + t[4]) + (t[7] + t[8]))
        return near + (t[5] + t[6])

    black4 = lax.fori_loop(0, COARSE_SWEEPS - 2, sweep4, c4)
    e_r = update4(0, g4r, bd4r, black4)
    e_b = update4(1, g4b, bd4b, e_r)
    low, high = split(p4, e_r, e_b)
    buf4[pl.ds(0, 16, stride=4), :] = low
    buf4[pl.ds(1, 16, stride=4), :] = low
    buf4[pl.ds(2, 16, stride=4), :] = high
    buf4[pl.ds(3, 16, stride=4), :] = high
    v_b = v_b + buf4[...]
    v_r = update3(0, v_b)
    v_b = update3(1, v_r)
    v_r = update3(0, v_b)
    v_b = update3(1, v_r)

    x_low, x_high = split(odd3, v_r, v_b)
    e3x[0, pl.ds(8, 64), :] = x_low
    e3x[1, pl.ds(8, 64), :] = x_high
    parts = []
    for n in range(2):
        for i in range(12):
            parts.append(e3x[n, pl.ds(gy * 4 + (4 + i), 1), :])
    wide = dot(jnp.concatenate(parts, axis=0), expand)
    for i in range(12):
        e = jnp.where(sub2 < 4, wide[i : i + 1], wide[12 + i : 13 + i])
        row_ok = up_in if i < 4 else (down_in if i >= 8 else True)
        V2[1, 1 + i] = V2[1, 1 + i] + jnp.where(ring_in & row_ok, e, 0.0)
    sweep_y(2, V2, G2, BD2, 0, 1, 13)
    sweep_y(2, V2, G2, BD2, 1, 1, 13)
    sweep_y(2, V2, G2, BD2, 0, 1, 13)
    sweep_y(2, V2, G2, BD2, 1, 3, 11)

    p1w = parity_y(1, lane2, sub2)

    def correct1(i, j):
        low, high = split(p2w, V2[0, 3 + i], V2[1, 3 + i])
        return [(V1, (1, 4 + 2 * i + n), V1[1, 4 + 2 * i + n] + e) for n, e in ((0, low), (1, high))]

    loop(0, 8, correct1, 4)
    sweep_y(1, V1, G1, BD1, 0, 4, 20)
    sweep_y(1, V1, G1, BD1, 1, 4, 20)
    sweep_y(1, V1, G1, BD1, 0, 4, 20)
    sweep_y(1, V1, G1, BD1, 1, 6, 18)

    def correct0(i, j):
        low, high = split(p1w, V1[0, 6 + i], V1[1, 6 + i])
        return [
            (V0, (1, 4 * i + n), V0[1, 4 * i + n] + e) for n, e in ((0, low), (1, low), (2, high), (3, high))
        ]

    loop(0, 12, correct0, 2)
    sweep0(0, 4, R0 - 4)
    sweep0(1, 4, R0 - 4)
    sweep0(0, 6, R0 - 6)
    sweep0(1, 6, R0 - 6)

    def results(r, j):
        stores = []
        for c in range(2):
            v = V0[c, r]
            res = D0[c, r] * (update0(c, r, j % 2) - v)
            stores.append((outf, (0, r - HY, c), v[:, :128]))
            stores.append((outf, (1, r - HY, c), res[:, :128]))
        return stores

    for k in range(4):
        lo = 8 * k
        loop(HY + lo, HY + lo + 8, results, 8)
        copy = pltpu.make_async_copy(outf.at[:, pl.ds(lo, 8)], fin_o.at[:, pl.ds(lo, 8)], osem.at[k])
        copy.start()
        stores_out.append(copy)

    for copies in (x_in, x_f, x_k, x_b1, x_b2):
        for copy in copies:
            copy.wait_send()
    all_bytes(GK, gs.at[0])
    all_bytes(GB, gs.at[1])
    for copy in stores_out:
        copy.wait()


def unpair(ice_h, fin_h, phase_o, pres_o, res_o, ice, fin, tmp, narrow, isem, osem):
    loads = [
        pltpu.make_async_copy(src, dst, isem.at[n])
        for n, (src, dst) in enumerate(((ice_h, ice), (fin_h.at[0], fin.at[0]), (fin_h.at[1], fin.at[1])))
    ]
    for copy in loads:
        copy.start()
    odd = lax.broadcasted_iota(jnp.int32, (8, 128), 1) % 2 == 1
    stores = []
    for n, out in enumerate((phase_o, pres_o, res_o)):
        loads[n].wait()

        def row(y, j, n=n):
            par = odd if j % 2 == 0 else jnp.logical_not(odd)
            if n == 0:
                both = ice[y].astype(F32)
                red, black = both[:8], both[8:]
            else:
                red, black = fin[n - 1, y, 0], fin[n - 1, y, 1]
            return [
                (tmp, (n, pl.ds(y, 8, stride=2 * NY), slice(None)), jnp.where(par, black, red)),
                (tmp, (n, pl.ds(NY + y, 8, stride=2 * NY), slice(None)), jnp.where(par, red, black)),
            ]

        loop(0, NY, row, 16)
        if n == 0:
            narrow[...] = tmp[0].astype(BF16)
        copy = pltpu.make_async_copy(narrow if n == 0 else tmp.at[n], out, osem.at[n])
        copy.start()
        stores.append(copy)
    for copy in stores:
        copy.wait()


def per_device(GY, GZ, phase, undercool, perm_base, source, pressure):
    def vm(*shape):
        return pltpu.VMEM(shape, F32)

    scratch = [
        pltpu.VMEM((3, NX * NY, NZ), BF16),
        vm(5, NX * NY, NZ),
        pltpu.VMEM((NY, 16, 128), BF16),
        vm(2, NY, 2, 8, 128),
        pltpu.VMEM((R0, 48, 128), BF16),
        vm(R0, 24, 128),
        pltpu.VMEM((4, 48, 128), BF16),
        vm(4, 24, 128),
        pltpu.VMEM((2, 6, 48, 128), BF16),
        vm(2, 6, 24, 128),
        vm(2, R0, 8, 256),
        vm(2, R0, 8, 256),
        vm(2, R0, 8, 256),
        vm(2, R0, 8, 256),
        vm(2, R0, 8, 256),
        vm(2, R0, 8, 256),
        vm(2, R0, 6, 8, 256),
        vm(2, R0, 8, 256),
        vm(2, R0, 8, 256),
        vm(2, R0, 8, 128),
        vm(3, 3, 12, 8, 128),
        vm(3, 3, 4, 8, 128),
        vm(2, R1, 8, 256),
        vm(2, R1, 8, 256),
        vm(2, R1, 6, 8, 256),
        vm(2, R1, 8, 256),
        vm(2, R1, 8, 256),
        vm(R1, 8, 256),
        vm(2, R2, 8, 256),
        vm(2, R2, 8, 256),
        vm(2, R2, 6, 8, 256),
        vm(2, R2, 8, 256),
        vm(2, R2, 8, 256),
        vm(R2, 8, 256),
        vm(R1, 8, 128),
        vm(4, 8, 128),
        vm(2, 12, 8, 128),
        vm(1, 1, 128),
        vm(1, 1, 128),
        vm(GY * GZ, 1, 128),
        vm(GY * GZ, 1, 128),
        vm(2, 64, 128),
        vm(2, 5, 64, 128),
        vm(2, 64, 128),
        vm(64, 128),
        vm(64, 128),
        vm(2, 80, 128),
        vm(8, 8, 128),
        pltpu.SemaphoreType.DMA((N_X, 8)),
        pltpu.SemaphoreType.DMA((N_X, 8)),
        pltpu.SemaphoreType.DMA((2,)),
        pltpu.SemaphoreType.DMA((2,)),
        pltpu.SemaphoreType.DMA((5,)),
        pltpu.SemaphoreType.DMA((5,)),
        pltpu.SemaphoreType.REGULAR((2,)),
    ]
    hbm = pl.BlockSpec(memory_space=pltpu.HBM)
    flat = (NX * NY, NZ)
    packed_ice, packed = pl.pallas_call(
        functools.partial(kernel, GY, GZ),
        out_shape=(jax.ShapeDtypeStruct((NY, 16, NZ), BF16), jax.ShapeDtypeStruct((2, NY, 2, 8, NZ), F32)),
        in_specs=[hbm] * 5,
        out_specs=(hbm, hbm),
        scratch_shapes=scratch,
        compiler_params=pltpu.CompilerParams(
            collective_id=0, has_side_effects=True, vmem_limit_bytes=63 * 2**20
        ),
    )(*[a.reshape(flat) for a in (phase, undercool, perm_base, source, pressure)])
    outs = pl.pallas_call(
        unpair,
        out_shape=(
            jax.ShapeDtypeStruct(flat, BF16),
            jax.ShapeDtypeStruct(flat, F32),
            jax.ShapeDtypeStruct(flat, F32),
        ),
        in_specs=[hbm] * 2,
        out_specs=(hbm, hbm, hbm),
        scratch_shapes=[
            pltpu.VMEM((NY, 16, NZ), BF16),
            vm(2, NY, 2, 8, NZ),
            vm(3, NX * NY, NZ),
            pltpu.VMEM(flat, BF16),
            pltpu.SemaphoreType.DMA((3,)),
            pltpu.SemaphoreType.DMA((3,)),
        ],
        compiler_params=pltpu.CompilerParams(vmem_limit_bytes=63 * 2**20),
    )(packed_ice, packed)
    return tuple(a.reshape(NX, NY, NZ) for a in outs)


def solution(mesh):
    spec = P(None, "gy", "gz")
    return jax.shard_map(
        functools.partial(per_device, mesh.shape["gy"], mesh.shape["gz"]),
        mesh=mesh,
        in_specs=(spec,) * 5,
        out_specs=(spec,) * 3,
        check_vma=False,
    )
```

```python
import functools
import jax
import jax.numpy as jnp
from jax import lax
from jax.experimental import pallas as pl
from jax.experimental.pallas import tpu as pltpu
from jax.sharding import PartitionSpec as P

MESH = pl.DeviceIdType.MESH
F32 = jnp.float32
BF16 = jnp.bfloat16
COARSE_SWEEPS = 20
NX, NY, NZ = 16, 32, 128
HY = 8
R0 = NY + 2 * HY
R1 = 24
R2 = 14
NEAR = [(dy, dz) for dy in (-1, 0, 1) for dz in (-1, 0, 1) if (dy, dz) != (0, 0)]
X_IN, X_F, X_K, X_B1, X_V0, X_B2 = range(6)
N_X = 6


def roll(x, shift, axis):
    size = x.shape[axis]
    shift = shift % size
    return x if shift == 0 else pltpu.roll(x, shift, axis)


def loop(lo, hi, body, step=2):
    def trip(i, carry):
        stores = []
        for j in range(step):
            stores.extend(body(lo + i * step + j, j))
        for ref, index, value in stores:
            ref[index] = value
        return carry

    trips = (hi - lo) // step
    assert trips * step == hi - lo
    if trips == 1:
        trip(0, 0)
    else:
        lax.fori_loop(0, trips, trip, 0)


def kernel(
    GY, GZ, phase_h, under_h, perm_h, src_h, pres_h, ice_o, fin_o,
    inb, tmp, outb, outf,
    ha, hf, zp, zpf, zb, zbf,
    ice, und, prm, S0, V0, K0, G0, BD0, D0, zv,
    KX, CX, K1, V1, G1, I1, BD1, D1, K2, V2, G2, I2, BD2, D2,
    b1, zp1, zb1, msg_k, msg_b, GK, GB, K3, G3, I3, D3, buf4, e3x, pair2,
    ssem, rsem, gs, gr, lsem, osem, known,
):
    gy, gz = lax.axis_index("gy"), lax.axis_index("gz")
    me = gy * GZ + gz

    def peer(dy, dz):
        return (lax.rem(gy + dy + GY, GY), lax.rem(gz + dz + GZ, GZ))

    barrier = pltpu.get_barrier_semaphore()

    for dy, dz in NEAR:
        pl.semaphore_signal(barrier, inc=1, device_id=peer(dy, dz), device_id_type=MESH)

    loads = []
    for n, (src, dst) in enumerate(
        ((phase_h, inb.at[0]), (under_h, inb.at[1]), (perm_h, inb.at[2]), (src_h, tmp.at[3]), (pres_h, tmp.at[4]))
    ):
        copy = pltpu.make_async_copy(src, dst, lsem.at[n])
        copy.start()
        loads.append(copy)

    lane = lax.broadcasted_iota(jnp.int32, (8, 128), 1)
    sub = lax.broadcasted_iota(jnp.int32, (8, 128), 0)
    lane2 = lax.broadcasted_iota(jnp.int32, (8, 256), 1)
    sub2 = lax.broadcasted_iota(jnp.int32, (8, 256), 0)
    odd = lane % 2 == 1
    odd2 = lane2 % 2 == 1
    right_in, left_in = gz < GZ - 1, gz > 0
    up_in, down_in = gy > 0, gy < GY - 1
    ring_in = (lane2 < 128) | ((lane2 < 192) & right_in) | ((lane2 >= 192) & left_in)

    def cat(a, b):
        return jnp.concatenate([a, b], axis=-1)

    def ring(o, d):
        a, b = o[:, :128], o[:, 128:]
        fa, fb = roll(a, -d, 1), roll(b, -d, 1)
        ba, bb = roll(a, d, 1), roll(b, d, 1)
        end, start = lane >= 128 - d, lane < d
        ahead = cat(jnp.where(end, fb, fa), jnp.where(end, fa, fb))
        behind = cat(jnp.where(start, bb, ba), jnp.where(start, ba, bb))
        return ahead, behind

    for n in range(3):
        loads[n].wait()
        tmp[n] = inb[n].astype(F32)

    def red_black_of(n, y, j):
        even = tmp[n, pl.ds(y, 8, stride=2 * NY), :]
        odds = tmp[n, pl.ds(NY + y, 8, stride=2 * NY), :]
        par = odd if j % 2 == 0 else jnp.logical_not(odd)
        return jnp.where(par, odds, even), jnp.where(par, even, odds)

    def prepare(rows, packed_rows, high, parts_of):
        group = lax.broadcasted_iota(jnp.int32, (high, 128), 1) // 16

        def block(k, carry):
            packed = jnp.zeros((high, 128), F32)
            stores = []
            for q in range(8):
                y = 8 * k + q
                row = jnp.concatenate(parts_of(y, q), axis=0)
                stores.append((HY + y, row))
                packed = jnp.where(group == q, roll(row, 16 * q + 8, 1), packed)
            for r, row in stores:
                rows[r] = row.astype(rows.dtype)
            packed_rows[k] = packed.astype(rows.dtype)
            return carry

        lax.fori_loop(0, 4, block, 0)

    def parts_in(y, q):
        return red_black_of(0, y, q) + red_black_of(1, y, q) + red_black_of(2, y, q)

    def parts_f(y, q):
        return red_black_of(3, y, q) + red_black_of(4, y, q)[1:]

    prepare(ha, zp, 48, parts_in)
    pl.semaphore_wait(barrier, len(NEAR))
    for dy, dz in NEAR:
        pl.semaphore_signal(known.at[2], inc=1, device_id=peer(dy, dz), device_id_type=MESH)

    def exchange(ex, pieces):
        copies = []
        for n, (dy, dz) in enumerate(NEAR):
            src, dst = pieces(dy, dz)
            copy = pltpu.make_async_remote_copy(
                src, dst, ssem.at[ex, n], rsem.at[ex, n], device_id=peer(dy, dz), device_id_type=MESH
            )
            copy.start()
            copies.append(copy)
        return copies

    def received(copies):
        for copy in copies:
            copy.wait_recv()

    def input_pieces(rows, packed, landing, width):
        def pieces(dy, dz):
            if dz == 0 and dy < 0:
                return rows.at[pl.ds(HY, width)], rows.at[pl.ds(HY + NY, width)]
            if dz == 0:
                return rows.at[pl.ds(HY + NY - width, width)], rows.at[pl.ds(HY - width, width)]
            side = 0 if dz > 0 else 1
            if dy == 0:
                return packed, landing.at[side, pl.ds(1, 4)]
            if dy > 0:
                return packed.at[pl.ds(3, 1)], landing.at[side, pl.ds(0, 1)]
            return packed.at[pl.ds(0, 1)], landing.at[side, pl.ds(5, 1)]

        return pieces

    x_in = exchange(X_IN, input_pieces(ha, zp, zb, 6))
    loads[3].wait()
    loads[4].wait()
    prepare(hf, zpf, 24, parts_f)
    x_f = exchange(X_F, input_pieces(hf, zpf, zbf, 5))

    zero_row = jnp.zeros((8, 256), F32)
    e3x[...] = jnp.zeros_like(e3x)
    for c in range(2):
        for r in (0, R2 - 1):
            K2[c, r] = zero_row
            V2[c, r] = zero_row
        for r in (0, 1, R1 - 2, R1 - 1):
            V1[c, r] = zero_row
        for r in (3, R0 - 4):
            V0[c, r] = zero_row

    pl.semaphore_wait(known.at[2], len(NEAR))
    for dy, dz in NEAR:
        pl.semaphore_signal(known.at[0], inc=1, device_id=peer(2 * dy, 2 * dz), device_id_type=MESH)

    received(x_in)
    def row_mask(r, width):
        ok = ((r >= HY) | up_in) & ((r < HY + NY) | down_in)
        lanes = (lane2 < 128) | ((lane2 < 128 + width) & right_in) | ((lane2 >= 256 - width) & left_in)
        return lanes & ok

    def unpack(k, carry):
        group = lax.broadcasted_iota(jnp.int32, (48, 128), 1) % 16 < 8
        merged = jnp.where(group, zb[0, k].astype(F32), zb[1, k].astype(F32))
        for q in range(8):
            r = 8 * k + q
            ok = row_mask(r, 6) & (r >= 2) & (r < R0 - 2)
            ok5 = row_mask(r, 5) & (r >= 3) & (r < R0 - 3)
            side = roll(merged, 120 - 16 * q, 1)
            a = ha[r].astype(F32)
            for c in range(2):
                s = slice(8 * c, 8 * c + 8)
                ice[c, r] = jnp.where(ok, cat(a[s], side[s]), 0.0)
                s = slice(16 + 8 * c, 24 + 8 * c)
                und[c, r] = cat(a[s], side[s])
                s = slice(32 + 8 * c, 40 + 8 * c)
                prm[c, r] = jnp.where(ok5, cat(a[s], side[s]), 0.0)
        return carry

    def unpack_f(k, carry):
        group = lax.broadcasted_iota(jnp.int32, (24, 128), 1) % 16 < 8
        merged = jnp.where(group, zbf[0, k], zbf[1, k])
        for q in range(8):
            r = 8 * k + q
            ok5 = row_mask(r, 5) & (r >= 3) & (r < R0 - 3)
            side = roll(merged, 120 - 16 * q, 1)
            f = hf[r]
            for c in range(2):
                s = slice(8 * c, 8 * c + 8)
                S0[c, r] = cat(f[s], side[s])
            V0[1, r] = jnp.where(ok5, cat(f[16:24], side[16:24]), 0.0)
        return carry

    for k in range(6):
        unpack(k, 0)

    def pick(c, j):
        return odd2 if (c + j) % 2 == 0 else jnp.logical_not(odd2)

    def x_outer(o, take):
        return jnp.where(take, roll(o, -1, 0), roll(o, 1, 0))

    def x_edge(take):
        return jnp.where(take, sub2, 7 - sub2) == 7

    def near0(ref, c, r, j):
        o = ref[1 - c, r]
        take = pick(c, j)
        ahead, behind = ring(o, 1)
        return (ref[1 - c, r - 1], ref[1 - c, r + 1], o, x_outer(o, take), ahead, behind)

    def permeability(r, j):
        j = j % 2
        stores = []
        for c in range(2):
            now = ice[c, r]
            near = list(near0(ice, c, r, j))
            near[3] = jnp.where(x_edge(pick(c, j)), 0.0, near[3])
            lap = near[0]
            for value in near[1:]:
                lap = lap + value
            lap = lap - 6.0 * now
            well = 2.0 * now * (1.0 - now) * (1.0 - 2.0 * now)
            drive = 30.0 * now * now * (1.0 - now) * (1.0 - now) * und[c, r]
            new = jnp.clip(now + 0.12 * lap - 0.5 * well + 0.25 * drive, 0.0, 1.0)
            stores.append((K0, (c, r), jnp.where(prm[c, r] > 0.0, prm[c, r] * jnp.exp(-1.5 * new), 0.0)))
            stores.append((und, (c, r), new))
        return stores

    loop(2, R0 - 2, permeability, 22)

    def swap_lanes(x, d):
        return jnp.where((lax.broadcasted_iota(jnp.int32, x.shape, 1) // d) % 2 == 0, roll(x, -d, 1), roll(x, d, 1))

    def swap_subs(x, d):
        return jnp.where((lax.broadcasted_iota(jnp.int32, x.shape, 0) // d) % 2 == 0, roll(x, -d, 0), roll(x, d, 0))

    def parity_y(level, ln, sb):
        return (sb // (1 if level == 1 else 2) + ln // (2 if level == 1 else 4)) % 2 == 1

    def own0(c, r):
        return K0[c, r, :, :128]

    def coarse0(y):
        r = HY + 2 * y
        t = (own0(0, r) + own0(1, r)) + (own0(0, r + 1) + own0(1, r + 1))
        return 0.125 * (t + swap_lanes(t, 1))

    p1, p2 = parity_y(1, lane, sub), parity_y(2, lane, sub)

    def split(p, low, high):
        return jnp.where(p, high, low), jnp.where(p, low, high)

    k2_rows = []
    for yp in range(8):
        red, black = split(p1, coarse0(2 * yp), coarse0(2 * yp + 1))
        KX[1, 1, yp] = jnp.where(odd, black, red)
        t = red + black
        t = t + swap_subs(t, 1)
        k2_rows.append(0.125 * (t + swap_lanes(t, 2)))
    k3_rows = []
    for yp in range(4):
        red, black = split(p2, k2_rows[2 * yp], k2_rows[2 * yp + 1])
        KX[1, 1, 8 + yp] = jnp.where(odd, black, red)
        t = red + black
        t = t + swap_subs(t, 2)
        k3_rows.append(0.125 * (t + swap_lanes(t, 4)))

    def block_pieces(ref):
        return lambda dy, dz: (ref.at[1, 1], ref.at[1 - dy, 1 - dz])

    x_k = exchange(X_K, block_pieces(KX))

    squeeze = (
        lax.broadcasted_iota(jnp.int32, (128, 128), 0) == 8 * (lax.broadcasted_iota(jnp.int32, (128, 128), 1) % 16)
    ).astype(F32)

    def dot(a, b):
        return lax.dot_general(
            a, b, (((1,), (0,)), ((), ())), precision=lax.Precision.HIGHEST, preferred_element_type=F32
        )

    def message(rows):
        piece = jnp.zeros((8, 128), F32)
        for y in range(4):
            u = rows[y]
            t = jnp.where((y + lane // 8) % 2 == 0, u, roll(u, 4, 0))
            piece = jnp.where(sub % 4 == y, t, piece)
        wide = dot(piece, squeeze)
        return jnp.sum(jnp.where(lane // 16 == sub, wide, 0.0), axis=0, keepdims=True)

    def gather(msg, landing, n, row):
        msg[0] = row
        landing[pl.ds(me, 1)] = row.reshape(1, 1, 128)

        def start(y, z):
            pltpu.make_async_remote_copy(
                msg, landing.at[pl.ds(me, 1)], gs.at[n], gr.at[n], device_id=(y, z), device_id_type=MESH
            ).start()

        columns = [lax.rem(gz + i, GZ) for i in (4, 3, 5, 2, 6, 1, 7, 0)]

        def send(i, carry):
            y = lax.rem(gy + i, GY)
            for z in columns:
                start(y, z)
            return carry

        lax.fori_loop(1, GY, send, 0)
        for z in columns[:-1]:
            start(gy, z)

    def all_bytes(landing, sem):
        part = landing.at[pl.ds(0, GY * GZ - 1)]
        pltpu.make_async_copy(part, part, sem).wait()

    def global_level3(landing):
        x = landing[...].reshape(GY, GZ, 128)
        ln = lax.broadcasted_iota(jnp.int32, x.shape, 2)
        sb = lax.broadcasted_iota(jnp.int32, x.shape, 1)
        for bit in (1, 2, 4):
            s_set, t_set = (sb // bit) % 2 == 1, (ln // (16 * bit)) % 2 == 1
            down = roll(roll(x, bit, 1), -16 * bit, 2)
            up = roll(roll(x, -bit, 1), 16 * bit, 2)
            x = jnp.where(s_set == t_set, x, jnp.where(s_set, down, up))
        pairs = x.reshape(GY // 2, 2, 8, 128)
        even, odds = pairs[:, 0], pairs[:, 1]
        low = lax.broadcasted_iota(jnp.int32, even.shape, 1) < 4
        red = jnp.where(low, even, roll(odds, 4, 1))
        black = jnp.where(low, roll(even, 4, 1), odds)
        return red.reshape(64, 128), black.reshape(64, 128)

    row_k = message(k3_rows)

    received(x_f)
    lax.fori_loop(0, 6, unpack_f, 0)

    pl.semaphore_wait(known.at[0], len(NEAR))
    for dy in (-4, 4):
        pl.semaphore_signal(known.at[1], inc=1, device_id=peer(dy, 0), device_id_type=MESH)

    def faces0(r, j):
        j = j % 2
        stores = []
        ok = row_mask(r, 5)
        for c in range(2):
            k = K0[c, r]
            take = pick(c, j)
            edge = x_edge(take)
            near = list(near0(K0, c, r, j))
            near[3] = jnp.where(edge, 0.0, near[3])
            f = [0.5 * (k + value) for value in near]
            d = ((f[0] + f[1]) + (f[2] + f[3])) + (f[4] + f[5])
            inv = jnp.where(ok, 1.0 / d, 0.0)
            for n in range(6):
                g = f[n] * inv
                stores.append((G0, (c, r, n), jnp.where(edge, 0.0, g) if n == 3 else g))
            stores.append((BD0, (c, r), jnp.where(ok, S0[c, r], 0.0) * inv))
            stores.append((D0, (c, r), d))
        return stores

    loop(4, R0 - 4, faces0, 4)

    def update0(c, r, j):
        near = near0(V0, c, r, j)
        t = [G0[c, r, n] * near[n] for n in range(6)]
        return BD0[c, r] + (((t[0] + t[1]) + (t[2] + t[3])) + (t[4] + t[5]))

    def sweep0(c, lo, hi):
        def body(r, j):
            return [(V0, (c, r), update0(c, r, j % 2))]

        loop(lo, hi, body, 10 if hi - lo == 40 else 12)

    sweep0(0, 4, R0 - 4)
    sweep0(1, 4, R0 - 4)
    sweep0(0, 6, R0 - 6)
    sweep0(1, 6, R0 - 6)

    def defect0(r, j):
        return (D0[0, r] * (update0(0, r, j) - V0[0, r]))[:, :128]

    def right1(yp, j):
        rows = []
        for j in range(2):
            r = HY + 4 * yp + 2 * j
            t = defect0(r, 0) + defect0(r + 1, 1)
            rows.append(0.125 * (t + swap_lanes(t, 1)))
        red, black = split(p1, rows[0], rows[1])
        return [(b1, (8 + yp,), jnp.where(odd, black, red))]

    loop(0, 8, right1, 2)
    for k in range(4):
        first, second = b1[8 + 2 * k], b1[9 + 2 * k]
        zp1[k] = jnp.where(lane < 64, roll(first, 32, 1), roll(second, 96, 1))

    def b1_pieces(dy, dz):
        if dz == 0 and dy < 0:
            return b1.at[pl.ds(8, 6)], b1.at[pl.ds(16, 6)]
        if dz == 0:
            return b1.at[pl.ds(10, 6)], b1.at[pl.ds(2, 6)]
        side = 0 if dz > 0 else 1
        if dy == 0:
            return zp1, zb1.at[side, pl.ds(4, 4)]
        if dy > 0:
            return zp1.at[pl.ds(1, 3)], zb1.at[side, pl.ds(1, 3)]
        return zp1.at[pl.ds(0, 3)], zb1.at[side, pl.ds(8, 3)]

    x_b1 = exchange(X_B1, b1_pieces)

    received(x_k)

    def joined(ref, yb, r):
        a = ref[yb, 1, r]
        b = jnp.where(lane < 64, ref[yb, 2, r], ref[yb, 0, r])
        return cat(a, b)

    def apart(x):
        a, b = x[:, :128], x[:, 128:]
        red = cat(jnp.where(odd, roll(a, 1, 1), a), jnp.where(odd, roll(b, 1, 1), b))
        black = cat(jnp.where(odd, a, roll(a, -1, 1)), jnp.where(odd, b, roll(b, -1, 1)))
        return red, black

    for yb in range(3):
        row_ok = (up_in, True, down_in)[yb]
        ok = ring_in & row_ok

        def spread1(r, carry, yb=yb, ok=ok):
            red, black = apart(joined(KX, yb, r))
            K1[0, 8 * yb + r] = jnp.where(ok, red, 0.0)
            K1[1, 8 * yb + r] = jnp.where(ok, black, 0.0)
            return carry

        lax.fori_loop(0, 8, spread1, 0)
        for r in range(4):
            red, black = apart(joined(KX, yb, 8 + r))
            K2[0, 1 + 4 * yb + r] = jnp.where(ok, red, 0.0)
            K2[1, 1 + 4 * yb + r] = jnp.where(ok, black, 0.0)

    def near_y(level, ref, c, r):
        dx, dz = (1, 2) if level == 1 else (2, 4)
        p = parity_y(level, lane2, sub2)
        o, low, high = ref[1 - c, r], ref[1 - c, r - 1], ref[1 - c, r + 1]
        outer = jnp.where(p, high, low) if c == 0 else jnp.where(p, low, high)
        ahead, behind = ring(o, dz)
        return (o, outer, roll(o, -dx, 0), roll(o, dx, 0), ahead, behind)

    def faces_y(level, K, G, I, D, r):
        dx = 1 if level == 1 else 2
        s = 0.25**level
        stores = []
        for c in range(2):
            k = K[c, r]
            near = list(near_y(level, K, c, r))
            last, first = sub2 >= 8 - dx, sub2 < dx
            near[2] = jnp.where(last, 0.0, near[2])
            near[3] = jnp.where(first, 0.0, near[3])
            f = [0.5 * (k + value) for value in near]
            d = ((f[0] + f[1]) + (f[2] + f[3])) + (f[4] + f[5])
            inv = jnp.where(k > 0.0, 1.0 / d, 0.0)
            for n in range(6):
                g = f[n] * inv
                if n == 2:
                    g = jnp.where(last, 0.0, g)
                if n == 3:
                    g = jnp.where(first, 0.0, g)
                stores.append((G, (c, r, n), g))
            stores.append((I, (c, r), inv * (1.0 / s)))
            if c == 0:
                stores.append((D, (r,), s * d))
        return stores

    loop(2, R1 - 2, lambda r, j: faces_y(1, K1, G1, I1, D1, r))
    loop(1, R2 - 1, lambda r, j: faces_y(2, K2, G2, I2, D2, r))

    pl.semaphore_wait(known.at[1], 2)
    gather(msg_k, GK, 0, row_k)

    received(x_b1)

    def v0_pieces(dy, dz):
        def at(r, n):
            return V0.at[1, pl.ds(r, n), :, pl.ds(0, 128)]

        lo, n, to = {-1: (HY, 5, HY + NY), 0: (HY, NY, HY), 1: (HY + NY - 5, 5, HY - 5)}[dy]
        if dz == 0:
            return at(lo, n), at(to, n)
        return at(lo, n), zv.at[0 if dz > 0 else 1, pl.ds(to, n)]

    def spread_b(k, j):
        stores = []
        merged = jnp.where(lane % 64 < 32, zb1[0, k], zb1[1, k])
        for q in range(2):
            r = 2 * k + q
            red, black = apart(cat(b1[r], roll(merged, -64 * q - 32, 1)))
            stores.append((BD1, (0, r), jnp.where(I1[0, r] > 0.0, red, 0.0) * I1[0, r]))
            stores.append((BD1, (1, r), jnp.where(I1[1, r] > 0.0, black, 0.0) * I1[1, r]))
            stores.append((V1, (0, r), stores[-2][2]))
        return stores

    loop(1, 11, spread_b, 10)

    def update_y(level, V, G, BD, c, r):
        near = near_y(level, V, c, r)
        t = [G[c, r, n] * near[n] for n in range(6)]
        return BD[c, r] + (((t[0] + t[1]) + (t[2] + t[3])) + (t[4] + t[5]))

    def sweep_y(level, V, G, BD, c, lo, hi):
        def body(r, j):
            return [(V, (c, r), update_y(level, V, G, BD, c, r))]

        loop(lo, hi, body, hi - lo)

    sweep_y(1, V1, G1, BD1, 1, 2, 22)
    sweep_y(1, V1, G1, BD1, 0, 2, 22)
    sweep_y(1, V1, G1, BD1, 1, 2, 22)

    p2w = parity_y(2, lane2, sub2)

    def right2(i, j):
        rows = []
        for j in range(2):
            r = 4 + 2 * i + j
            t = D1[r] * (update_y(1, V1, G1, BD1, 0, r) - V1[0, r])
            t = t + swap_subs(t, 1)
            a, b = t[:, :128], t[:, 128:]
            rows.append(0.125 * cat(a + swap_lanes(a, 2), b + swap_lanes(b, 2)))
        red, black = split(p2w, rows[0], rows[1])
        row = 3 + i
        first = red * I2[0, row]
        return [
            (BD2, (0, row), first),
            (V2, (0, row), first),
            (BD2, (1, row), black * I2[1, row]),
            (pair2, (i,), jnp.where(odd, black[:, :128], red[:, :128])),
        ]

    V2[0, 2] = zero_row
    V2[0, 11] = zero_row
    V2[1, 2] = zero_row
    V2[1, 11] = zero_row
    loop(0, 8, right2, 8)

    sweep_y(2, V2, G2, BD2, 1, 3, 11)
    sweep_y(2, V2, G2, BD2, 0, 3, 11)
    sweep_y(2, V2, G2, BD2, 1, 3, 11)
    rows = []
    for y in range(4):
        r = 5 + y
        t = (D2[r] * (update_y(2, V2, G2, BD2, 0, r) - V2[0, r]))[:, :128]
        t = t + swap_subs(t, 2)
        rows.append(0.125 * (t + swap_lanes(t, 4)))
    gather(msg_b, GB, 1, message(rows))

    for y in range(4):
        CX[1, 1, y] = jnp.where(lane % 4 < 2, pair2[2 + y], V2[1, 5 + y, :, :128])
    x_b2 = exchange(X_B2, block_pieces(CX))
    x_v0 = exchange(X_V0, v0_pieces)

    def new_ice(r, j):
        both = jnp.concatenate([und[0, r, :, :128], und[1, r, :, :128]], axis=0)
        return [(outb, (r - HY,), both.astype(BF16))]

    loop(HY, HY + NY, new_ice, 4)
    copy = pltpu.make_async_copy(outb, ice_o, osem.at[4])
    copy.start()
    stores_out = [copy]
    all_bytes(GK, gr.at[0])
    k3r, k3b = global_level3(GK)
    row3 = lax.broadcasted_iota(jnp.int32, (64, 128), 0)
    lane3 = lax.broadcasted_iota(jnp.int32, (64, 128), 1)
    odd3 = (row3 + lane3) % 2 == 1
    edges3 = (row3 == 0, row3 == 63, lane3 == 0, lane3 == 127)

    def near3(o):
        return (roll(o, 1, 0), roll(o, -1, 0), roll(o, 1, 1), roll(o, -1, 1), o)

    def faces3(c, k, o):
        s = 0.25**3
        near = [jnp.where(e, 0.0, v) for e, v in zip(edges3, near3(o))] + [o]
        f = [0.5 * (k + value) for value in near] + [0.5 * k]
        d = ((f[0] + f[1]) + (f[2] + f[3])) + (f[4] + f[5])
        inv = 1.0 / d
        for n in range(5):
            g = f[n] * inv
            G3[c, n] = jnp.where(edges3[n], 0.0, g) if n < 4 else g
        I3[c] = inv * (1.0 / s)
        if c == 0:
            D3[...] = s * d

    faces3(0, k3r, k3b)
    faces3(1, k3b, k3r)

    lane4 = lax.broadcasted_iota(jnp.int32, (16, 128), 1)
    row4 = lax.broadcasted_iota(jnp.int32, (16, 128), 0)
    p4 = (lane4 // 2) % 2 == 1

    def level4_of(total):
        t = total + swap_subs(total, 1)
        buf4[...] = 0.125 * (t + swap_lanes(t, 1))
        low, high = buf4[pl.ds(0, 16, stride=4), :], buf4[pl.ds(2, 16, stride=4), :]
        return split(p4, low, high)

    k4 = level4_of(k3r + k3b)

    def near4(c, o):
        low, high = roll(o, 1, 0), roll(o, -1, 0)
        outer = jnp.where(p4, high, low) if c == 0 else jnp.where(p4, low, high)
        return (o, outer, roll(o, -2, 1), roll(o, 2, 1))

    def faces4(c):
        s = 0.25**4
        k = k4[c]
        take = p4 if c == 0 else jnp.logical_not(p4)
        edges = (None, jnp.where(take, row4, 15 - row4) == 15, lane4 >= 126, lane4 < 2)
        near = near4(c, k4[1 - c])
        near = [v if e is None else jnp.where(e, 0.0, v) for e, v in zip(edges, near)]
        f = [0.5 * (k + value) for value in near]
        d = ((f[0] + f[1]) + (f[2] + f[3])) + k
        inv = 1.0 / d
        g = [v * inv if e is None else jnp.where(e, 0.0, v * inv) for e, v in zip(edges, f)]
        return g, inv * (1.0 / s)

    g4r, i4r = faces4(0)
    g4b, i4b = faces4(1)

    def shifts4(o):
        return near4(1, o)

    back4 = [shifts4(g) for g in g4r]
    m4 = (
        (g4b[0] * back4[0][0] + g4b[1] * back4[1][1]) + (g4b[2] * back4[3][2] + g4b[3] * back4[2][3]),
        g4b[0] * back4[1][0],
        g4b[1] * back4[0][1],
        g4b[0] * back4[2][0] + g4b[2] * back4[0][2],
        g4b[0] * back4[3][0] + g4b[3] * back4[0][3],
        g4b[1] * back4[2][1] + g4b[2] * back4[1][2],
        g4b[1] * back4[3][1] + g4b[3] * back4[1][3],
        g4b[2] * back4[2][2],
        g4b[3] * back4[3][3],
    )

    received(x_b2)
    for yb in range(3):
        row_ok = (up_in, True, down_in)[yb]
        for r in range(4):
            x = joined(CX, yb, r)
            row = 1 + 4 * yb + r

            def fill(x):
                a, b = x[:, :128], x[:, 128:]
                first = cat(jnp.where(odd, roll(a, 1, 1), a), jnp.where(odd, roll(b, 1, 1), b))
                second = cat(jnp.where(odd, a, roll(a, -1, 1)), jnp.where(odd, b, roll(b, -1, 1)))
                return first, second

            first, second = fill(x)
            head = lane2 % 4 < 2

            def pair_up(y):
                return cat(roll(y[:, :128], 2, 1), roll(y[:, 128:], 2, 1))

            def pair_down(y):
                return cat(roll(y[:, :128], -2, 1), roll(y[:, 128:], -2, 1))

            BD2[0, row] = jnp.where(head, first, pair_up(first)) * I2[0, row]
            BD2[1, row] = jnp.where(head, second, pair_up(second)) * I2[1, row]
            V2[1, row] = jnp.where(ring_in & row_ok, jnp.where(head, pair_down(x), x), 0.0)

    received(x_v0)
    for copy in x_v0:
        copy.wait_send()

    def v0_sides(r, j):
        ok = ((r >= HY) | up_in) & ((r < HY + NY) | down_in)
        side = jnp.where(
            ok & (((lane < 5) & right_in) | ((lane >= 123) & left_in)), jnp.where(lane < 64, zv[1, r], zv[0, r]), 0.0
        )
        return [(V0, (1, r), cat(jnp.where(ok, V0[1, r, :, :128], 0.0), side))]

    loop(HY - 5, HY + NY + 5, v0_sides, 3)
    zrow = lax.broadcasted_iota(jnp.int32, (128, 256), 0)
    zcol = lax.broadcasted_iota(jnp.int32, (128, 256), 1)
    expand = (zrow == gz * 16 + zcol // 8 - jnp.where(zcol >= 192, 32, 0)).astype(F32)

    all_bytes(GB, gr.at[1])
    b3r, b3b = global_level3(GB)
    bd3 = (b3r * I3[0], b3b * I3[1])

    def update3(c, o):
        near = near3(o)
        t = [G3[c, n] * near[n] for n in range(5)]
        return bd3[c] + (((t[0] + t[1]) + (t[2] + t[3])) + t[4])

    v_r = bd3[0]
    v_b = update3(1, v_r)
    v_r = update3(0, v_b)
    v_b = update3(1, v_r)
    r3 = D3[...] * (update3(0, v_b) - v_r)
    b4 = level4_of(r3)
    bd4r, bd4b = b4[0] * i4r, b4[1] * i4b

    def update4(c, g, bd, o):
        near = near4(c, o)
        return bd + ((g[0] * near[0] + g[1] * near[1]) + (g[2] * near[2] + g[3] * near[3]))

    c4 = update4(1, g4b, bd4b, bd4r)

    def sweep4(i, black):
        low, high = roll(black, 1, 0), roll(black, -1, 0)
        outer, inner = jnp.where(p4, high, low), jnp.where(p4, low, high)
        t = [
            m * v
            for m, v in zip(
                m4,
                (
                    black, outer, inner, roll(black, -2, 1), roll(black, 2, 1),
                    roll(outer, -2, 1), roll(outer, 2, 1), roll(black, -4, 1), roll(black, 4, 1),
                ),
            )
        ]
        near = ((c4 + t[0]) + (t[1] + t[2])) + ((t[3] + t[4]) + (t[7] + t[8]))
        return near + (t[5] + t[6])

    black4 = lax.fori_loop(0, COARSE_SWEEPS - 2, sweep4, c4)
    e_r = update4(0, g4r, bd4r, black4)
    e_b = update4(1, g4b, bd4b, e_r)
    low, high = split(p4, e_r, e_b)
    buf4[pl.ds(0, 16, stride=4), :] = low
    buf4[pl.ds(1, 16, stride=4), :] = low
    buf4[pl.ds(2, 16, stride=4), :] = high
    buf4[pl.ds(3, 16, stride=4), :] = high
    v_b = v_b + buf4[...]
    v_r = update3(0, v_b)
    v_b = update3(1, v_r)
    v_r = update3(0, v_b)
    v_b = update3(1, v_r)

    x_low, x_high = split(odd3, v_r, v_b)
    e3x[0, pl.ds(8, 64), :] = x_low
    e3x[1, pl.ds(8, 64), :] = x_high
    parts = []
    for n in range(2):
        for i in range(12):
            parts.append(e3x[n, pl.ds(gy * 4 + (4 + i), 1), :])
    wide = dot(jnp.concatenate(parts, axis=0), expand)
    for i in range(12):
        e = jnp.where(sub2 < 4, wide[i : i + 1], wide[12 + i : 13 + i])
        row_ok = up_in if i < 4 else (down_in if i >= 8 else True)
        V2[1, 1 + i] = V2[1, 1 + i] + jnp.where(ring_in & row_ok, e, 0.0)
    sweep_y(2, V2, G2, BD2, 0, 1, 13)
    sweep_y(2, V2, G2, BD2, 1, 1, 13)
    sweep_y(2, V2, G2, BD2, 0, 1, 13)
    sweep_y(2, V2, G2, BD2, 1, 3, 11)

    p1w = parity_y(1, lane2, sub2)

    def correct1(i, j):
        low, high = split(p2w, V2[0, 3 + i], V2[1, 3 + i])
        return [(V1, (1, 4 + 2 * i + n), V1[1, 4 + 2 * i + n] + e) for n, e in ((0, low), (1, high))]

    loop(0, 8, correct1, 4)
    sweep_y(1, V1, G1, BD1, 0, 4, 20)
    sweep_y(1, V1, G1, BD1, 1, 4, 20)
    sweep_y(1, V1, G1, BD1, 0, 4, 20)
    sweep_y(1, V1, G1, BD1, 1, 6, 18)

    def correct0(i, j):
        low, high = split(p1w, V1[0, 6 + i], V1[1, 6 + i])
        return [
            (V0, (1, 4 * i + n), V0[1, 4 * i + n] + e) for n, e in ((0, low), (1, low), (2, high), (3, high))
        ]

    loop(0, 12, correct0, 2)
    sweep0(0, 4, R0 - 4)
    sweep0(1, 4, R0 - 4)
    sweep0(0, 6, R0 - 6)
    sweep0(1, 6, R0 - 6)

    def results(r, j):
        stores = []
        for c in range(2):
            v = V0[c, r]
            res = D0[c, r] * (update0(c, r, j % 2) - v)
            stores.append((outf, (0, r - HY, c), v[:, :128]))
            stores.append((outf, (1, r - HY, c), res[:, :128]))
        return stores

    for k in range(4):
        lo = 8 * k
        loop(HY + lo, HY + lo + 8, results, 8)
        copy = pltpu.make_async_copy(outf.at[:, pl.ds(lo, 8)], fin_o.at[:, pl.ds(lo, 8)], osem.at[k])
        copy.start()
        stores_out.append(copy)

    for copies in (x_in, x_f, x_k, x_b1, x_b2):
        for copy in copies:
            copy.wait_send()
    all_bytes(GK, gs.at[0])
    all_bytes(GB, gs.at[1])
    for copy in stores_out:
        copy.wait()


def unpair(ice_h, fin_h, phase_o, pres_o, res_o, ice, fin, tmp, narrow, isem, osem):
    loads = [
        pltpu.make_async_copy(src, dst, isem.at[n])
        for n, (src, dst) in enumerate(((ice_h, ice), (fin_h.at[0], fin.at[0]), (fin_h.at[1], fin.at[1])))
    ]
    for copy in loads:
        copy.start()
    odd = lax.broadcasted_iota(jnp.int32, (8, 128), 1) % 2 == 1
    stores = []
    for n, out in enumerate((phase_o, pres_o, res_o)):
        loads[n].wait()

        def row(y, j, n=n):
            par = odd if j % 2 == 0 else jnp.logical_not(odd)
            if n == 0:
                both = ice[y].astype(F32)
                red, black = both[:8], both[8:]
            else:
                red, black = fin[n - 1, y, 0], fin[n - 1, y, 1]
            return [
                (tmp, (n, pl.ds(y, 8, stride=2 * NY), slice(None)), jnp.where(par, black, red)),
                (tmp, (n, pl.ds(NY + y, 8, stride=2 * NY), slice(None)), jnp.where(par, red, black)),
            ]

        loop(0, NY, row, 16)
        if n == 0:
            narrow[...] = tmp[0].astype(BF16)
        copy = pltpu.make_async_copy(narrow if n == 0 else tmp.at[n], out, osem.at[n])
        copy.start()
        stores.append(copy)
    for copy in stores:
        copy.wait()


def per_device(GY, GZ, phase, undercool, perm_base, source, pressure):
    def vm(*shape):
        return pltpu.VMEM(shape, F32)

    scratch = [
        pltpu.VMEM((3, NX * NY, NZ), BF16),
        vm(5, NX * NY, NZ),
        pltpu.VMEM((NY, 16, 128), BF16),
        vm(2, NY, 2, 8, 128),
        pltpu.VMEM((R0, 48, 128), BF16),
        vm(R0, 24, 128),
        pltpu.VMEM((4, 48, 128), BF16),
        vm(4, 24, 128),
        pltpu.VMEM((2, 6, 48, 128), BF16),
        vm(2, 6, 24, 128),
        vm(2, R0, 8, 256),
        vm(2, R0, 8, 256),
        vm(2, R0, 8, 256),
        vm(2, R0, 8, 256),
        vm(2, R0, 8, 256),
        vm(2, R0, 8, 256),
        vm(2, R0, 6, 8, 256),
        vm(2, R0, 8, 256),
        vm(2, R0, 8, 256),
        vm(2, R0, 8, 128),
        vm(3, 3, 12, 8, 128),
        vm(3, 3, 4, 8, 128),
        vm(2, R1, 8, 256),
        vm(2, R1, 8, 256),
        vm(2, R1, 6, 8, 256),
        vm(2, R1, 8, 256),
        vm(2, R1, 8, 256),
        vm(R1, 8, 256),
        vm(2, R2, 8, 256),
        vm(2, R2, 8, 256),
        vm(2, R2, 6, 8, 256),
        vm(2, R2, 8, 256),
        vm(2, R2, 8, 256),
        vm(R2, 8, 256),
        vm(R1, 8, 128),
        vm(4, 8, 128),
        vm(2, 12, 8, 128),
        vm(1, 1, 128),
        vm(1, 1, 128),
        vm(GY * GZ, 1, 128),
        vm(GY * GZ, 1, 128),
        vm(2, 64, 128),
        vm(2, 5, 64, 128),
        vm(2, 64, 128),
        vm(64, 128),
        vm(64, 128),
        vm(2, 80, 128),
        vm(8, 8, 128),
        pltpu.SemaphoreType.DMA((N_X, 8)),
        pltpu.SemaphoreType.DMA((N_X, 8)),
        pltpu.SemaphoreType.DMA((2,)),
        pltpu.SemaphoreType.DMA((2,)),
        pltpu.SemaphoreType.DMA((5,)),
        pltpu.SemaphoreType.DMA((5,)),
        pltpu.SemaphoreType.REGULAR((3,)),
    ]
    hbm = pl.BlockSpec(memory_space=pltpu.HBM)
    flat = (NX * NY, NZ)
    packed_ice, packed = pl.pallas_call(
        functools.partial(kernel, GY, GZ),
        out_shape=(jax.ShapeDtypeStruct((NY, 16, NZ), BF16), jax.ShapeDtypeStruct((2, NY, 2, 8, NZ), F32)),
        in_specs=[hbm] * 5,
        out_specs=(hbm, hbm),
        scratch_shapes=scratch,
        compiler_params=pltpu.CompilerParams(
            collective_id=0, has_side_effects=True, vmem_limit_bytes=63 * 2**20
        ),
    )(*[a.reshape(flat) for a in (phase, undercool, perm_base, source, pressure)])
    outs = pl.pallas_call(
        unpair,
        out_shape=(
            jax.ShapeDtypeStruct(flat, BF16),
            jax.ShapeDtypeStruct(flat, F32),
            jax.ShapeDtypeStruct(flat, F32),
        ),
        in_specs=[hbm] * 2,
        out_specs=(hbm, hbm, hbm),
        scratch_shapes=[
            pltpu.VMEM((NY, 16, NZ), BF16),
            vm(2, NY, 2, 8, NZ),
            vm(3, NX * NY, NZ),
            pltpu.VMEM(flat, BF16),
            pltpu.SemaphoreType.DMA((3,)),
            pltpu.SemaphoreType.DMA((3,)),
        ],
        compiler_params=pltpu.CompilerParams(vmem_limit_bytes=63 * 2**20),
    )(packed_ice, packed)
    return tuple(a.reshape(NX, NY, NZ) for a in outs)


def solution(mesh):
    spec = P(None, "gy", "gz")
    return jax.shard_map(
        functools.partial(per_device, mesh.shape["gy"], mesh.shape["gz"]),
        mesh=mesh,
        in_specs=(spec,) * 5,
        out_specs=(spec,) * 3,
        check_vma=False,
    )
```

```python
import functools
import jax
import jax.numpy as jnp
from jax import lax
from jax.experimental import pallas as pl
from jax.experimental.pallas import tpu as pltpu
from jax.sharding import PartitionSpec as P

MESH = pl.DeviceIdType.MESH
F32 = jnp.float32
BF16 = jnp.bfloat16
COARSE_SWEEPS = 20
NX, NY, NZ = 16, 32, 128
HY = 8
R0 = NY + 2 * HY
R1 = 24
R2 = 14
NEAR = [(dy, dz) for dy in (-1, 0, 1) for dz in (-1, 0, 1) if (dy, dz) != (0, 0)]
X_IN, X_F, X_K, X_B1, X_V0, X_B2 = range(6)
N_X = 6


def roll(x, shift, axis):
    size = x.shape[axis]
    shift = shift % size
    return x if shift == 0 else pltpu.roll(x, shift, axis)


def loop(lo, hi, body, step=2):
    def trip(i, carry):
        stores = []
        for j in range(step):
            stores.extend(body(lo + i * step + j, j))
        for ref, index, value in stores:
            ref[index] = value
        return carry

    trips = (hi - lo) // step
    assert trips * step == hi - lo
    if trips == 1:
        trip(0, 0)
    else:
        lax.fori_loop(0, trips, trip, 0)


def kernel(
    GY, GZ, phase_h, under_h, perm_h, src_h, pres_h, ice_o, fin_o,
    inb, tmp, outb, outf,
    ha, hf, zp, zpf, zb, zbf,
    ice, und, prm, S0, V0, K0, G0, BD0, D0, zv,
    KX, CX, K1, V1, G1, I1, BD1, D1, K2, V2, G2, I2, BD2, D2,
    b1, zp1, zb1, msg_k, msg_b, GK, GB, K3, G3, I3, D3, buf4, e3x, pair2,
    ssem, rsem, gs, gr, lsem, osem, known,
):
    gy, gz = lax.axis_index("gy"), lax.axis_index("gz")
    me = gy * GZ + gz

    def peer(dy, dz):
        return (lax.rem(gy + dy + GY, GY), lax.rem(gz + dz + GZ, GZ))

    barrier = pltpu.get_barrier_semaphore()

    for dy, dz in NEAR:
        pl.semaphore_signal(barrier, inc=1, device_id=peer(dy, dz), device_id_type=MESH)

    loads = []
    for n, (src, dst) in enumerate(
        ((phase_h, inb.at[0]), (under_h, inb.at[1]), (perm_h, inb.at[2]), (src_h, tmp.at[3]), (pres_h, tmp.at[4]))
    ):
        copy = pltpu.make_async_copy(src, dst, lsem.at[n])
        copy.start()
        loads.append(copy)

    lane = lax.broadcasted_iota(jnp.int32, (8, 128), 1)
    sub = lax.broadcasted_iota(jnp.int32, (8, 128), 0)
    lane2 = lax.broadcasted_iota(jnp.int32, (8, 256), 1)
    sub2 = lax.broadcasted_iota(jnp.int32, (8, 256), 0)
    odd = lane % 2 == 1
    odd2 = lane2 % 2 == 1
    right_in, left_in = gz < GZ - 1, gz > 0
    up_in, down_in = gy > 0, gy < GY - 1
    ring_in = (lane2 < 128) | ((lane2 < 192) & right_in) | ((lane2 >= 192) & left_in)

    def cat(a, b):
        return jnp.concatenate([a, b], axis=-1)

    def ring(o, d):
        a, b = o[:, :128], o[:, 128:]
        fa, fb = roll(a, -d, 1), roll(b, -d, 1)
        ba, bb = roll(a, d, 1), roll(b, d, 1)
        end, start = lane >= 128 - d, lane < d
        ahead = cat(jnp.where(end, fb, fa), jnp.where(end, fa, fb))
        behind = cat(jnp.where(start, bb, ba), jnp.where(start, ba, bb))
        return ahead, behind

    for n in range(3):
        loads[n].wait()
        tmp[n] = inb[n].astype(F32)

    def red_black_of(n, y, j):
        even = tmp[n, pl.ds(y, 8, stride=2 * NY), :]
        odds = tmp[n, pl.ds(NY + y, 8, stride=2 * NY), :]
        par = odd if j % 2 == 0 else jnp.logical_not(odd)
        return jnp.where(par, odds, even), jnp.where(par, even, odds)

    def prepare(rows, packed_rows, high, parts_of):
        group = lax.broadcasted_iota(jnp.int32, (high, 128), 1) // 16

        def block(k, carry):
            packed = jnp.zeros((high, 128), F32)
            stores = []
            for q in range(8):
                y = 8 * k + q
                row = jnp.concatenate(parts_of(y, q), axis=0)
                stores.append((HY + y, row))
                packed = jnp.where(group == q, roll(row, 16 * q + 8, 1), packed)
            for r, row in stores:
                rows[r] = row.astype(rows.dtype)
            packed_rows[k] = packed.astype(rows.dtype)
            return carry

        for k in range(4):
            block(k, 0)

    def parts_in(y, q):
        return red_black_of(0, y, q) + red_black_of(1, y, q) + red_black_of(2, y, q)

    def parts_f(y, q):
        return red_black_of(3, y, q) + red_black_of(4, y, q)[1:]

    prepare(ha, zp, 48, parts_in)
    pl.semaphore_wait(barrier, len(NEAR))
    for dy, dz in NEAR:
        pl.semaphore_signal(known.at[2], inc=1, device_id=peer(dy, dz), device_id_type=MESH)

    def exchange(ex, pieces):
        copies = []
        for n, (dy, dz) in enumerate(NEAR):
            src, dst = pieces(dy, dz)
            copy = pltpu.make_async_remote_copy(
                src, dst, ssem.at[ex, n], rsem.at[ex, n], device_id=peer(dy, dz), device_id_type=MESH
            )
            copy.start()
            copies.append(copy)
        return copies

    def received(copies):
        for copy in copies:
            copy.wait_recv()

    def input_pieces(rows, packed, landing, width):
        def pieces(dy, dz):
            if dz == 0 and dy < 0:
                return rows.at[pl.ds(HY, width)], rows.at[pl.ds(HY + NY, width)]
            if dz == 0:
                return rows.at[pl.ds(HY + NY - width, width)], rows.at[pl.ds(HY - width, width)]
            side = 0 if dz > 0 else 1
            if dy == 0:
                return packed, landing.at[side, pl.ds(1, 4)]
            if dy > 0:
                return packed.at[pl.ds(3, 1)], landing.at[side, pl.ds(0, 1)]
            return packed.at[pl.ds(0, 1)], landing.at[side, pl.ds(5, 1)]

        return pieces

    x_in = exchange(X_IN, input_pieces(ha, zp, zb, 6))
    loads[3].wait()
    loads[4].wait()
    prepare(hf, zpf, 24, parts_f)
    x_f = exchange(X_F, input_pieces(hf, zpf, zbf, 5))

    zero_row = jnp.zeros((8, 256), F32)
    e3x[...] = jnp.zeros_like(e3x)
    for c in range(2):
        for r in (0, R2 - 1):
            K2[c, r] = zero_row
            V2[c, r] = zero_row
        for r in (0, 1, R1 - 2, R1 - 1):
            V1[c, r] = zero_row
        for r in (3, R0 - 4):
            V0[c, r] = zero_row

    pl.semaphore_wait(known.at[2], len(NEAR))
    for dy, dz in NEAR:
        pl.semaphore_signal(known.at[0], inc=1, device_id=peer(2 * dy, 2 * dz), device_id_type=MESH)

    received(x_in)
    def row_mask(r, width):
        ok = ((r >= HY) | up_in) & ((r < HY + NY) | down_in)
        lanes = (lane2 < 128) | ((lane2 < 128 + width) & right_in) | ((lane2 >= 256 - width) & left_in)
        return lanes & ok

    def unpack(k, carry):
        group = lax.broadcasted_iota(jnp.int32, (48, 128), 1) % 16 < 8
        merged = jnp.where(group, zb[0, k].astype(F32), zb[1, k].astype(F32))
        for q in range(8):
            r = 8 * k + q
            ok = row_mask(r, 6) & (r >= 2) & (r < R0 - 2)
            ok5 = row_mask(r, 5) & (r >= 3) & (r < R0 - 3)
            side = roll(merged, 120 - 16 * q, 1)
            a = ha[r].astype(F32)
            for c in range(2):
                s = slice(8 * c, 8 * c + 8)
                ice[c, r] = jnp.where(ok, cat(a[s], side[s]), 0.0)
                s = slice(16 + 8 * c, 24 + 8 * c)
                und[c, r] = cat(a[s], side[s])
                s = slice(32 + 8 * c, 40 + 8 * c)
                prm[c, r] = jnp.where(ok5, cat(a[s], side[s]), 0.0)
        return carry

    def unpack_f(k, carry):
        group = lax.broadcasted_iota(jnp.int32, (24, 128), 1) % 16 < 8
        merged = jnp.where(group, zbf[0, k], zbf[1, k])
        for q in range(8):
            r = 8 * k + q
            ok5 = row_mask(r, 5) & (r >= 3) & (r < R0 - 3)
            side = roll(merged, 120 - 16 * q, 1)
            f = hf[r]
            for c in range(2):
                s = slice(8 * c, 8 * c + 8)
                S0[c, r] = cat(f[s], side[s])
            V0[1, r] = jnp.where(ok5, cat(f[16:24], side[16:24]), 0.0)
        return carry

    for k in range(6):
        unpack(k, 0)

    def pick(c, j):
        return odd2 if (c + j) % 2 == 0 else jnp.logical_not(odd2)

    def x_outer(o, take):
        return jnp.where(take, roll(o, -1, 0), roll(o, 1, 0))

    def x_edge(take):
        return jnp.where(take, sub2, 7 - sub2) == 7

    def near0(ref, c, r, j):
        o = ref[1 - c, r]
        take = pick(c, j)
        ahead, behind = ring(o, 1)
        return (ref[1 - c, r - 1], ref[1 - c, r + 1], o, x_outer(o, take), ahead, behind)

    def permeability(r, j):
        j = j % 2
        stores = []
        for c in range(2):
            now = ice[c, r]
            near = list(near0(ice, c, r, j))
            near[3] = jnp.where(x_edge(pick(c, j)), 0.0, near[3])
            lap = near[0]
            for value in near[1:]:
                lap = lap + value
            lap = lap - 6.0 * now
            well = 2.0 * now * (1.0 - now) * (1.0 - 2.0 * now)
            drive = 30.0 * now * now * (1.0 - now) * (1.0 - now) * und[c, r]
            new = jnp.clip(now + 0.12 * lap - 0.5 * well + 0.25 * drive, 0.0, 1.0)
            stores.append((K0, (c, r), jnp.where(prm[c, r] > 0.0, prm[c, r] * jnp.exp(-1.5 * new), 0.0)))
            stores.append((und, (c, r), new))
        return stores

    loop(2, R0 - 2, permeability, 22)

    def swap_lanes(x, d):
        return jnp.where((lax.broadcasted_iota(jnp.int32, x.shape, 1) // d) % 2 == 0, roll(x, -d, 1), roll(x, d, 1))

    def swap_subs(x, d):
        return jnp.where((lax.broadcasted_iota(jnp.int32, x.shape, 0) // d) % 2 == 0, roll(x, -d, 0), roll(x, d, 0))

    def parity_y(level, ln, sb):
        return (sb // (1 if level == 1 else 2) + ln // (2 if level == 1 else 4)) % 2 == 1

    def own0(c, r):
        return K0[c, r, :, :128]

    def coarse0(y):
        r = HY + 2 * y
        t = (own0(0, r) + own0(1, r)) + (own0(0, r + 1) + own0(1, r + 1))
        return 0.125 * (t + swap_lanes(t, 1))

    p1, p2 = parity_y(1, lane, sub), parity_y(2, lane, sub)

    def split(p, low, high):
        return jnp.where(p, high, low), jnp.where(p, low, high)

    k2_rows = []
    for yp in range(8):
        red, black = split(p1, coarse0(2 * yp), coarse0(2 * yp + 1))
        KX[1, 1, yp] = jnp.where(odd, black, red)
        t = red + black
        t = t + swap_subs(t, 1)
        k2_rows.append(0.125 * (t + swap_lanes(t, 2)))
    k3_rows = []
    for yp in range(4):
        red, black = split(p2, k2_rows[2 * yp], k2_rows[2 * yp + 1])
        KX[1, 1, 8 + yp] = jnp.where(odd, black, red)
        t = red + black
        t = t + swap_subs(t, 2)
        k3_rows.append(0.125 * (t + swap_lanes(t, 4)))

    def block_pieces(ref):
        return lambda dy, dz: (ref.at[1, 1], ref.at[1 - dy, 1 - dz])

    x_k = exchange(X_K, block_pieces(KX))

    squeeze = (
        lax.broadcasted_iota(jnp.int32, (128, 128), 0) == 8 * (lax.broadcasted_iota(jnp.int32, (128, 128), 1) % 16)
    ).astype(F32)

    def dot(a, b):
        return lax.dot_general(
            a, b, (((1,), (0,)), ((), ())), precision=lax.Precision.HIGHEST, preferred_element_type=F32
        )

    def message(rows):
        piece = jnp.zeros((8, 128), F32)
        for y in range(4):
            u = rows[y]
            t = jnp.where((y + lane // 8) % 2 == 0, u, roll(u, 4, 0))
            piece = jnp.where(sub % 4 == y, t, piece)
        wide = dot(piece, squeeze)
        return jnp.sum(jnp.where(lane // 16 == sub, wide, 0.0), axis=0, keepdims=True)

    def gather(msg, landing, n, row):
        msg[0] = row
        landing[pl.ds(me, 1)] = row.reshape(1, 1, 128)

        def start(y, z):
            pltpu.make_async_remote_copy(
                msg, landing.at[pl.ds(me, 1)], gs.at[n], gr.at[n], device_id=(y, z), device_id_type=MESH
            ).start()

        columns = [lax.rem(gz + i, GZ) for i in (4, 3, 5, 2, 6, 1, 7, 0)]

        def send(i, carry):
            y = lax.rem(gy + i, GY)
            for z in columns:
                start(y, z)
            return carry

        lax.fori_loop(1, GY, send, 0)
        for z in columns[:-1]:
            start(gy, z)

    def all_bytes(landing, sem):
        part = landing.at[pl.ds(0, GY * GZ - 1)]
        pltpu.make_async_copy(part, part, sem).wait()

    def global_level3(landing):
        x = landing[...].reshape(GY, GZ, 128)
        ln = lax.broadcasted_iota(jnp.int32, x.shape, 2)
        sb = lax.broadcasted_iota(jnp.int32, x.shape, 1)
        for bit in (1, 2, 4):
            s_set, t_set = (sb // bit) % 2 == 1, (ln // (16 * bit)) % 2 == 1
            down = roll(roll(x, bit, 1), -16 * bit, 2)
            up = roll(roll(x, -bit, 1), 16 * bit, 2)
            x = jnp.where(s_set == t_set, x, jnp.where(s_set, down, up))
        pairs = x.reshape(GY // 2, 2, 8, 128)
        even, odds = pairs[:, 0], pairs[:, 1]
        low = lax.broadcasted_iota(jnp.int32, even.shape, 1) < 4
        red = jnp.where(low, even, roll(odds, 4, 1))
        black = jnp.where(low, roll(even, 4, 1), odds)
        return red.reshape(64, 128), black.reshape(64, 128)

    row_k = message(k3_rows)

    received(x_f)
    lax.fori_loop(0, 6, unpack_f, 0)

    pl.semaphore_wait(known.at[0], len(NEAR))
    for dy in (-4, 4):
        pl.semaphore_signal(known.at[1], inc=1, device_id=peer(dy, 0), device_id_type=MESH)

    def faces0(r, j):
        j = j % 2
        stores = []
        ok = row_mask(r, 5)
        for c in range(2):
            k = K0[c, r]
            take = pick(c, j)
            edge = x_edge(take)
            near = list(near0(K0, c, r, j))
            near[3] = jnp.where(edge, 0.0, near[3])
            f = [0.5 * (k + value) for value in near]
            d = ((f[0] + f[1]) + (f[2] + f[3])) + (f[4] + f[5])
            inv = jnp.where(ok, 1.0 / d, 0.0)
            for n in range(6):
                g = f[n] * inv
                stores.append((G0, (c, r, n), jnp.where(edge, 0.0, g) if n == 3 else g))
            stores.append((BD0, (c, r), jnp.where(ok, S0[c, r], 0.0) * inv))
            stores.append((D0, (c, r), d))
        return stores

    loop(4, R0 - 4, faces0, 4)

    def update0(c, r, j):
        near = near0(V0, c, r, j)
        t = [G0[c, r, n] * near[n] for n in range(6)]
        return BD0[c, r] + (((t[0] + t[1]) + (t[2] + t[3])) + (t[4] + t[5]))

    def sweep0(c, lo, hi):
        def body(r, j):
            return [(V0, (c, r), update0(c, r, j % 2))]

        loop(lo, hi, body, 10 if hi - lo == 40 else 12)

    sweep0(0, 4, R0 - 4)
    sweep0(1, 4, R0 - 4)
    sweep0(0, 6, R0 - 6)
    sweep0(1, 6, R0 - 6)

    def defect0(r, j):
        return (D0[0, r] * (update0(0, r, j) - V0[0, r]))[:, :128]

    def right1(yp, j):
        rows = []
        for j in range(2):
            r = HY + 4 * yp + 2 * j
            t = defect0(r, 0) + defect0(r + 1, 1)
            rows.append(0.125 * (t + swap_lanes(t, 1)))
        red, black = split(p1, rows[0], rows[1])
        return [(b1, (8 + yp,), jnp.where(odd, black, red))]

    loop(0, 8, right1, 2)
    for k in range(4):
        first, second = b1[8 + 2 * k], b1[9 + 2 * k]
        zp1[k] = jnp.where(lane < 64, roll(first, 32, 1), roll(second, 96, 1))

    def b1_pieces(dy, dz):
        if dz == 0 and dy < 0:
            return b1.at[pl.ds(8, 6)], b1.at[pl.ds(16, 6)]
        if dz == 0:
            return b1.at[pl.ds(10, 6)], b1.at[pl.ds(2, 6)]
        side = 0 if dz > 0 else 1
        if dy == 0:
            return zp1, zb1.at[side, pl.ds(4, 4)]
        if dy > 0:
            return zp1.at[pl.ds(1, 3)], zb1.at[side, pl.ds(1, 3)]
        return zp1.at[pl.ds(0, 3)], zb1.at[side, pl.ds(8, 3)]

    x_b1 = exchange(X_B1, b1_pieces)

    received(x_k)

    def joined(ref, yb, r):
        a = ref[yb, 1, r]
        b = jnp.where(lane < 64, ref[yb, 2, r], ref[yb, 0, r])
        return cat(a, b)

    def apart(x):
        a, b = x[:, :128], x[:, 128:]
        red = cat(jnp.where(odd, roll(a, 1, 1), a), jnp.where(odd, roll(b, 1, 1), b))
        black = cat(jnp.where(odd, a, roll(a, -1, 1)), jnp.where(odd, b, roll(b, -1, 1)))
        return red, black

    for yb in range(3):
        row_ok = (up_in, True, down_in)[yb]
        ok = ring_in & row_ok

        def spread1(r, carry, yb=yb, ok=ok):
            red, black = apart(joined(KX, yb, r))
            K1[0, 8 * yb + r] = jnp.where(ok, red, 0.0)
            K1[1, 8 * yb + r] = jnp.where(ok, black, 0.0)
            return carry

        lax.fori_loop(0, 8, spread1, 0)
        for r in range(4):
            red, black = apart(joined(KX, yb, 8 + r))
            K2[0, 1 + 4 * yb + r] = jnp.where(ok, red, 0.0)
            K2[1, 1 + 4 * yb + r] = jnp.where(ok, black, 0.0)

    def near_y(level, ref, c, r):
        dx, dz = (1, 2) if level == 1 else (2, 4)
        p = parity_y(level, lane2, sub2)
        o, low, high = ref[1 - c, r], ref[1 - c, r - 1], ref[1 - c, r + 1]
        outer = jnp.where(p, high, low) if c == 0 else jnp.where(p, low, high)
        ahead, behind = ring(o, dz)
        return (o, outer, roll(o, -dx, 0), roll(o, dx, 0), ahead, behind)

    def faces_y(level, K, G, I, D, r):
        dx = 1 if level == 1 else 2
        s = 0.25**level
        stores = []
        for c in range(2):
            k = K[c, r]
            near = list(near_y(level, K, c, r))
            last, first = sub2 >= 8 - dx, sub2 < dx
            near[2] = jnp.where(last, 0.0, near[2])
            near[3] = jnp.where(first, 0.0, near[3])
            f = [0.5 * (k + value) for value in near]
            d = ((f[0] + f[1]) + (f[2] + f[3])) + (f[4] + f[5])
            inv = jnp.where(k > 0.0, 1.0 / d, 0.0)
            for n in range(6):
                g = f[n] * inv
                if n == 2:
                    g = jnp.where(last, 0.0, g)
                if n == 3:
                    g = jnp.where(first, 0.0, g)
                stores.append((G, (c, r, n), g))
            stores.append((I, (c, r), inv * (1.0 / s)))
            if c == 0:
                stores.append((D, (r,), s * d))
        return stores

    loop(2, R1 - 2, lambda r, j: faces_y(1, K1, G1, I1, D1, r))
    loop(1, R2 - 1, lambda r, j: faces_y(2, K2, G2, I2, D2, r))

    pl.semaphore_wait(known.at[1], 2)
    gather(msg_k, GK, 0, row_k)

    received(x_b1)

    def v0_pieces(dy, dz):
        def at(r, n):
            return V0.at[1, pl.ds(r, n), :, pl.ds(0, 128)]

        lo, n, to = {-1: (HY, 5, HY + NY), 0: (HY, NY, HY), 1: (HY + NY - 5, 5, HY - 5)}[dy]
        if dz == 0:
            return at(lo, n), at(to, n)
        return at(lo, n), zv.at[0 if dz > 0 else 1, pl.ds(to, n)]

    def spread_b(k, j):
        stores = []
        merged = jnp.where(lane % 64 < 32, zb1[0, k], zb1[1, k])
        for q in range(2):
            r = 2 * k + q
            red, black = apart(cat(b1[r], roll(merged, -64 * q - 32, 1)))
            stores.append((BD1, (0, r), jnp.where(I1[0, r] > 0.0, red, 0.0) * I1[0, r]))
            stores.append((BD1, (1, r), jnp.where(I1[1, r] > 0.0, black, 0.0) * I1[1, r]))
            stores.append((V1, (0, r), stores[-2][2]))
        return stores

    loop(1, 11, spread_b, 10)

    def update_y(level, V, G, BD, c, r):
        near = near_y(level, V, c, r)
        t = [G[c, r, n] * near[n] for n in range(6)]
        return BD[c, r] + (((t[0] + t[1]) + (t[2] + t[3])) + (t[4] + t[5]))

    def sweep_y(level, V, G, BD, c, lo, hi):
        def body(r, j):
            return [(V, (c, r), update_y(level, V, G, BD, c, r))]

        loop(lo, hi, body, hi - lo)

    sweep_y(1, V1, G1, BD1, 1, 2, 22)
    sweep_y(1, V1, G1, BD1, 0, 2, 22)
    sweep_y(1, V1, G1, BD1, 1, 2, 22)

    p2w = parity_y(2, lane2, sub2)

    def right2(i, j):
        rows = []
        for j in range(2):
            r = 4 + 2 * i + j
            t = D1[r] * (update_y(1, V1, G1, BD1, 0, r) - V1[0, r])
            t = t + swap_subs(t, 1)
            a, b = t[:, :128], t[:, 128:]
            rows.append(0.125 * cat(a + swap_lanes(a, 2), b + swap_lanes(b, 2)))
        red, black = split(p2w, rows[0], rows[1])
        row = 3 + i
        first = red * I2[0, row]
        return [
            (BD2, (0, row), first),
            (V2, (0, row), first),
            (BD2, (1, row), black * I2[1, row]),
            (pair2, (i,), jnp.where(odd, black[:, :128], red[:, :128])),
        ]

    V2[0, 2] = zero_row
    V2[0, 11] = zero_row
    V2[1, 2] = zero_row
    V2[1, 11] = zero_row
    loop(0, 8, right2, 8)

    sweep_y(2, V2, G2, BD2, 1, 3, 11)
    sweep_y(2, V2, G2, BD2, 0, 3, 11)
    sweep_y(2, V2, G2, BD2, 1, 3, 11)
    rows = []
    for y in range(4):
        r = 5 + y
        t = (D2[r] * (update_y(2, V2, G2, BD2, 0, r) - V2[0, r]))[:, :128]
        t = t + swap_subs(t, 2)
        rows.append(0.125 * (t + swap_lanes(t, 4)))
    gather(msg_b, GB, 1, message(rows))

    for y in range(4):
        CX[1, 1, y] = jnp.where(lane % 4 < 2, pair2[2 + y], V2[1, 5 + y, :, :128])
    x_b2 = exchange(X_B2, block_pieces(CX))
    x_v0 = exchange(X_V0, v0_pieces)

    def new_ice(r, j):
        both = jnp.concatenate([und[0, r, :, :128], und[1, r, :, :128]], axis=0)
        return [(outb, (r - HY,), both.astype(BF16))]

    loop(HY, HY + NY, new_ice, 4)
    copy = pltpu.make_async_copy(outb, ice_o, osem.at[4])
    copy.start()
    stores_out = [copy]
    all_bytes(GK, gr.at[0])
    k3r, k3b = global_level3(GK)
    row3 = lax.broadcasted_iota(jnp.int32, (64, 128), 0)
    lane3 = lax.broadcasted_iota(jnp.int32, (64, 128), 1)
    odd3 = (row3 + lane3) % 2 == 1
    edges3 = (row3 == 0, row3 == 63, lane3 == 0, lane3 == 127)

    def near3(o):
        return (roll(o, 1, 0), roll(o, -1, 0), roll(o, 1, 1), roll(o, -1, 1), o)

    def faces3(c, k, o):
        s = 0.25**3
        near = [jnp.where(e, 0.0, v) for e, v in zip(edges3, near3(o))] + [o]
        f = [0.5 * (k + value) for value in near] + [0.5 * k]
        d = ((f[0] + f[1]) + (f[2] + f[3])) + (f[4] + f[5])
        inv = 1.0 / d
        for n in range(5):
            g = f[n] * inv
            G3[c, n] = jnp.where(edges3[n], 0.0, g) if n < 4 else g
        I3[c] = inv * (1.0 / s)
        if c == 0:
            D3[...] = s * d

    faces3(0, k3r, k3b)
    faces3(1, k3b, k3r)

    lane4 = lax.broadcasted_iota(jnp.int32, (16, 128), 1)
    row4 = lax.broadcasted_iota(jnp.int32, (16, 128), 0)
    p4 = (lane4 // 2) % 2 == 1

    def level4_of(total):
        t = total + swap_subs(total, 1)
        buf4[...] = 0.125 * (t + swap_lanes(t, 1))
        low, high = buf4[pl.ds(0, 16, stride=4), :], buf4[pl.ds(2, 16, stride=4), :]
        return split(p4, low, high)

    k4 = level4_of(k3r + k3b)

    def near4(c, o):
        low, high = roll(o, 1, 0), roll(o, -1, 0)
        outer = jnp.where(p4, high, low) if c == 0 else jnp.where(p4, low, high)
        return (o, outer, roll(o, -2, 1), roll(o, 2, 1))

    def faces4(c):
        s = 0.25**4
        k = k4[c]
        take = p4 if c == 0 else jnp.logical_not(p4)
        edges = (None, jnp.where(take, row4, 15 - row4) == 15, lane4 >= 126, lane4 < 2)
        near = near4(c, k4[1 - c])
        near = [v if e is None else jnp.where(e, 0.0, v) for e, v in zip(edges, near)]
        f = [0.5 * (k + value) for value in near]
        d = ((f[0] + f[1]) + (f[2] + f[3])) + k
        inv = 1.0 / d
        g = [v * inv if e is None else jnp.where(e, 0.0, v * inv) for e, v in zip(edges, f)]
        return g, inv * (1.0 / s)

    g4r, i4r = faces4(0)
    g4b, i4b = faces4(1)

    def shifts4(o):
        return near4(1, o)

    back4 = [shifts4(g) for g in g4r]
    m4 = (
        (g4b[0] * back4[0][0] + g4b[1] * back4[1][1]) + (g4b[2] * back4[3][2] + g4b[3] * back4[2][3]),
        g4b[0] * back4[1][0],
        g4b[1] * back4[0][1],
        g4b[0] * back4[2][0] + g4b[2] * back4[0][2],
        g4b[0] * back4[3][0] + g4b[3] * back4[0][3],
        g4b[1] * back4[2][1] + g4b[2] * back4[1][2],
        g4b[1] * back4[3][1] + g4b[3] * back4[1][3],
        g4b[2] * back4[2][2],
        g4b[3] * back4[3][3],
    )

    received(x_b2)
    for yb in range(3):
        row_ok = (up_in, True, down_in)[yb]
        for r in range(4):
            x = joined(CX, yb, r)
            row = 1 + 4 * yb + r

            def fill(x):
                a, b = x[:, :128], x[:, 128:]
                first = cat(jnp.where(odd, roll(a, 1, 1), a), jnp.where(odd, roll(b, 1, 1), b))
                second = cat(jnp.where(odd, a, roll(a, -1, 1)), jnp.where(odd, b, roll(b, -1, 1)))
                return first, second

            first, second = fill(x)
            head = lane2 % 4 < 2

            def pair_up(y):
                return cat(roll(y[:, :128], 2, 1), roll(y[:, 128:], 2, 1))

            def pair_down(y):
                return cat(roll(y[:, :128], -2, 1), roll(y[:, 128:], -2, 1))

            BD2[0, row] = jnp.where(head, first, pair_up(first)) * I2[0, row]
            BD2[1, row] = jnp.where(head, second, pair_up(second)) * I2[1, row]
            V2[1, row] = jnp.where(ring_in & row_ok, jnp.where(head, pair_down(x), x), 0.0)

    received(x_v0)
    for copy in x_v0:
        copy.wait_send()

    def v0_sides(r, j):
        ok = ((r >= HY) | up_in) & ((r < HY + NY) | down_in)
        side = jnp.where(
            ok & (((lane < 5) & right_in) | ((lane >= 123) & left_in)), jnp.where(lane < 64, zv[1, r], zv[0, r]), 0.0
        )
        return [(V0, (1, r), cat(jnp.where(ok, V0[1, r, :, :128], 0.0), side))]

    loop(HY - 5, HY + NY + 5, v0_sides, 3)
    zrow = lax.broadcasted_iota(jnp.int32, (128, 256), 0)
    zcol = lax.broadcasted_iota(jnp.int32, (128, 256), 1)
    expand = (zrow == gz * 16 + zcol // 8 - jnp.where(zcol >= 192, 32, 0)).astype(F32)

    all_bytes(GB, gr.at[1])
    b3r, b3b = global_level3(GB)
    bd3 = (b3r * I3[0], b3b * I3[1])

    def update3(c, o):
        near = near3(o)
        t = [G3[c, n] * near[n] for n in range(5)]
        return bd3[c] + (((t[0] + t[1]) + (t[2] + t[3])) + t[4])

    v_r = bd3[0]
    v_b = update3(1, v_r)
    v_r = update3(0, v_b)
    v_b = update3(1, v_r)
    r3 = D3[...] * (update3(0, v_b) - v_r)
    b4 = level4_of(r3)
    bd4r, bd4b = b4[0] * i4r, b4[1] * i4b

    def update4(c, g, bd, o):
        near = near4(c, o)
        return bd + ((g[0] * near[0] + g[1] * near[1]) + (g[2] * near[2] + g[3] * near[3]))

    c4 = update4(1, g4b, bd4b, bd4r)

    def sweep4(i, black):
        low, high = roll(black, 1, 0), roll(black, -1, 0)
        outer, inner = jnp.where(p4, high, low), jnp.where(p4, low, high)
        t = [
            m * v
            for m, v in zip(
                m4,
                (
                    black, outer, inner, roll(black, -2, 1), roll(black, 2, 1),
                    roll(outer, -2, 1), roll(outer, 2, 1), roll(black, -4, 1), roll(black, 4, 1),
                ),
            )
        ]
        near = ((c4 + t[0]) + (t[1] + t[2])) + ((t[3] + t[4]) + (t[7] + t[8]))
        return near + (t[5] + t[6])

    black4 = lax.fori_loop(0, COARSE_SWEEPS - 2, sweep4, c4)
    e_r = update4(0, g4r, bd4r, black4)
    e_b = update4(1, g4b, bd4b, e_r)
    low, high = split(p4, e_r, e_b)
    buf4[pl.ds(0, 16, stride=4), :] = low
    buf4[pl.ds(1, 16, stride=4), :] = low
    buf4[pl.ds(2, 16, stride=4), :] = high
    buf4[pl.ds(3, 16, stride=4), :] = high
    v_b = v_b + buf4[...]
    v_r = update3(0, v_b)
    v_b = update3(1, v_r)
    v_r = update3(0, v_b)
    v_b = update3(1, v_r)

    x_low, x_high = split(odd3, v_r, v_b)
    e3x[0, pl.ds(8, 64), :] = x_low
    e3x[1, pl.ds(8, 64), :] = x_high
    parts = []
    for n in range(2):
        for i in range(12):
            parts.append(e3x[n, pl.ds(gy * 4 + (4 + i), 1), :])
    wide = dot(jnp.concatenate(parts, axis=0), expand)
    for i in range(12):
        e = jnp.where(sub2 < 4, wide[i : i + 1], wide[12 + i : 13 + i])
        row_ok = up_in if i < 4 else (down_in if i >= 8 else True)
        V2[1, 1 + i] = V2[1, 1 + i] + jnp.where(ring_in & row_ok, e, 0.0)
    sweep_y(2, V2, G2, BD2, 0, 1, 13)
    sweep_y(2, V2, G2, BD2, 1, 1, 13)
    sweep_y(2, V2, G2, BD2, 0, 1, 13)
    sweep_y(2, V2, G2, BD2, 1, 3, 11)

    p1w = parity_y(1, lane2, sub2)

    def correct1(i, j):
        low, high = split(p2w, V2[0, 3 + i], V2[1, 3 + i])
        return [(V1, (1, 4 + 2 * i + n), V1[1, 4 + 2 * i + n] + e) for n, e in ((0, low), (1, high))]

    loop(0, 8, correct1, 4)
    sweep_y(1, V1, G1, BD1, 0, 4, 20)
    sweep_y(1, V1, G1, BD1, 1, 4, 20)
    sweep_y(1, V1, G1, BD1, 0, 4, 20)
    sweep_y(1, V1, G1, BD1, 1, 6, 18)

    def correct0(i, j):
        low, high = split(p1w, V1[0, 6 + i], V1[1, 6 + i])
        return [
            (V0, (1, 4 * i + n), V0[1, 4 * i + n] + e) for n, e in ((0, low), (1, low), (2, high), (3, high))
        ]

    loop(0, 12, correct0, 2)
    sweep0(0, 4, R0 - 4)
    sweep0(1, 4, R0 - 4)
    sweep0(0, 6, R0 - 6)
    sweep0(1, 6, R0 - 6)

    def results(r, j):
        stores = []
        for c in range(2):
            v = V0[c, r]
            res = D0[c, r] * (update0(c, r, j % 2) - v)
            stores.append((outf, (0, r - HY, c), v[:, :128]))
            stores.append((outf, (1, r - HY, c), res[:, :128]))
        return stores

    for k in range(4):
        lo = 8 * k
        loop(HY + lo, HY + lo + 8, results, 8)
        copy = pltpu.make_async_copy(outf.at[:, pl.ds(lo, 8)], fin_o.at[:, pl.ds(lo, 8)], osem.at[k])
        copy.start()
        stores_out.append(copy)

    for copies in (x_in, x_f, x_k, x_b1, x_b2):
        for copy in copies:
            copy.wait_send()
    all_bytes(GK, gs.at[0])
    all_bytes(GB, gs.at[1])
    for copy in stores_out:
        copy.wait()


def unpair(ice_h, fin_h, phase_o, pres_o, res_o, ice, fin, tmp, narrow, isem, osem):
    loads = [
        pltpu.make_async_copy(src, dst, isem.at[n])
        for n, (src, dst) in enumerate(((ice_h, ice), (fin_h.at[0], fin.at[0]), (fin_h.at[1], fin.at[1])))
    ]
    for copy in loads:
        copy.start()
    odd = lax.broadcasted_iota(jnp.int32, (8, 128), 1) % 2 == 1
    stores = []
    for n, out in enumerate((phase_o, pres_o, res_o)):
        loads[n].wait()

        def row(y, j, n=n):
            par = odd if j % 2 == 0 else jnp.logical_not(odd)
            if n == 0:
                both = ice[y].astype(F32)
                red, black = both[:8], both[8:]
            else:
                red, black = fin[n - 1, y, 0], fin[n - 1, y, 1]
            return [
                (tmp, (n, pl.ds(y, 8, stride=2 * NY), slice(None)), jnp.where(par, black, red)),
                (tmp, (n, pl.ds(NY + y, 8, stride=2 * NY), slice(None)), jnp.where(par, red, black)),
            ]

        loop(0, NY, row, 16)
        if n == 0:
            narrow[...] = tmp[0].astype(BF16)
        copy = pltpu.make_async_copy(narrow if n == 0 else tmp.at[n], out, osem.at[n])
        copy.start()
        stores.append(copy)
    for copy in stores:
        copy.wait()


def per_device(GY, GZ, phase, undercool, perm_base, source, pressure):
    def vm(*shape):
        return pltpu.VMEM(shape, F32)

    scratch = [
        pltpu.VMEM((3, NX * NY, NZ), BF16),
        vm(5, NX * NY, NZ),
        pltpu.VMEM((NY, 16, 128), BF16),
        vm(2, NY, 2, 8, 128),
        pltpu.VMEM((R0, 48, 128), BF16),
        vm(R0, 24, 128),
        pltpu.VMEM((4, 48, 128), BF16),
        vm(4, 24, 128),
        pltpu.VMEM((2, 6, 48, 128), BF16),
        vm(2, 6, 24, 128),
        vm(2, R0, 8, 256),
        vm(2, R0, 8, 256),
        vm(2, R0, 8, 256),
        vm(2, R0, 8, 256),
        vm(2, R0, 8, 256),
        vm(2, R0, 8, 256),
        vm(2, R0, 6, 8, 256),
        vm(2, R0, 8, 256),
        vm(2, R0, 8, 256),
        vm(2, R0, 8, 128),
        vm(3, 3, 12, 8, 128),
        vm(3, 3, 4, 8, 128),
        vm(2, R1, 8, 256),
        vm(2, R1, 8, 256),
        vm(2, R1, 6, 8, 256),
        vm(2, R1, 8, 256),
        vm(2, R1, 8, 256),
        vm(R1, 8, 256),
        vm(2, R2, 8, 256),
        vm(2, R2, 8, 256),
        vm(2, R2, 6, 8, 256),
        vm(2, R2, 8, 256),
        vm(2, R2, 8, 256),
        vm(R2, 8, 256),
        vm(R1, 8, 128),
        vm(4, 8, 128),
        vm(2, 12, 8, 128),
        vm(1, 1, 128),
        vm(1, 1, 128),
        vm(GY * GZ, 1, 128),
        vm(GY * GZ, 1, 128),
        vm(2, 64, 128),
        vm(2, 5, 64, 128),
        vm(2, 64, 128),
        vm(64, 128),
        vm(64, 128),
        vm(2, 80, 128),
        vm(8, 8, 128),
        pltpu.SemaphoreType.DMA((N_X, 8)),
        pltpu.SemaphoreType.DMA((N_X, 8)),
        pltpu.SemaphoreType.DMA((2,)),
        pltpu.SemaphoreType.DMA((2,)),
        pltpu.SemaphoreType.DMA((5,)),
        pltpu.SemaphoreType.DMA((5,)),
        pltpu.SemaphoreType.REGULAR((3,)),
    ]
    hbm = pl.BlockSpec(memory_space=pltpu.HBM)
    flat = (NX * NY, NZ)
    packed_ice, packed = pl.pallas_call(
        functools.partial(kernel, GY, GZ),
        out_shape=(jax.ShapeDtypeStruct((NY, 16, NZ), BF16), jax.ShapeDtypeStruct((2, NY, 2, 8, NZ), F32)),
        in_specs=[hbm] * 5,
        out_specs=(hbm, hbm),
        scratch_shapes=scratch,
        compiler_params=pltpu.CompilerParams(
            collective_id=0, has_side_effects=True, vmem_limit_bytes=63 * 2**20
        ),
    )(*[a.reshape(flat) for a in (phase, undercool, perm_base, source, pressure)])
    outs = pl.pallas_call(
        unpair,
        out_shape=(
            jax.ShapeDtypeStruct(flat, BF16),
            jax.ShapeDtypeStruct(flat, F32),
            jax.ShapeDtypeStruct(flat, F32),
        ),
        in_specs=[hbm] * 2,
        out_specs=(hbm, hbm, hbm),
        scratch_shapes=[
            pltpu.VMEM((NY, 16, NZ), BF16),
            vm(2, NY, 2, 8, NZ),
            vm(3, NX * NY, NZ),
            pltpu.VMEM(flat, BF16),
            pltpu.SemaphoreType.DMA((3,)),
            pltpu.SemaphoreType.DMA((3,)),
        ],
        compiler_params=pltpu.CompilerParams(vmem_limit_bytes=63 * 2**20),
    )(packed_ice, packed)
    return tuple(a.reshape(NX, NY, NZ) for a in outs)


def solution(mesh):
    spec = P(None, "gy", "gz")
    return jax.shard_map(
        functools.partial(per_device, mesh.shape["gy"], mesh.shape["gz"]),
        mesh=mesh,
        in_specs=(spec,) * 5,
        out_specs=(spec,) * 3,
        check_vma=False,
    )
```
